32 devices in a mesh: clip: 2 (over x), frame: 8 (over z, y), head: 2 (over core).
Axes of the slice: x: 2, y: 2, z: 4, core: 2. Of those that a mesh axis runs over, the one named last changes fastest.
Arguments:
- queries: bfloat16 [8192, 1536], P(('clip', 'frame', 'head')), parts along dimension 0, may hold values from -12 to 12
- key_tokens: bfloat16 [8192, 1536], P(('clip', 'frame', 'head')), parts along dimension 0, may hold values from -6 to 6
- value_tokens: bfloat16 [8192, 1536], P(('clip', 'frame', 'head')), parts along dimension 0, may hold values from -6 to 6
- radial_table: int32 [8, 8], replicated, may hold values from 0 to 4, as said below
- out_weight: bfloat16 [1536, 3072], P('head'), may hold values from -1.5 to 1.5
Outputs:
- projected: bfloat16 [8192, 3072], P(('clip', 'frame', 'head')), parts along dimension 0
The draws below stay inside these ranges and needn't reach their ends.
There are 2 independent parts, one for each index of `clip`. The reference program is written for one: setup_inputs(seed, part) draws one part's arguments, and reference() takes and returns one part's arrays. A program takes and returns all parts, laid end to end along the dimension named above; an argument that names none is the same for every part. Nothing has to cross between parts.
Inputs may be any that keep to these rules, and one draw needn't show every extreme that they name: radial_table[f, f] = 4; for 1 <= |f - g| <= 3 the entry lies from c - c // 2 to c, where c = 2 at distance 1 and 1 at distances 2 and 3; beyond distance 3 it is 0.
All inputs are finite; a program needn't handle non-finite values.
Results may differ from the reference program's by a relative error of at most 0.0055.
Values may be sent and summed in bfloat16 or wider, within the bound.
No kernel may reach another device: no remote copies, remote signals or barrier semaphores. Data moves between devices by JAX's collectives and lax.ppermute only.
A program may use at most 128 MiB of HBM per device.

```python
import math
import jax
import jax.numpy as jnp
from jax import lax

D = 3072
DH = 128
HEADS = 12
BS = 128
NB = 4
REACH = 3
FRAMES = 8
TOKENS = 4096
HD = 1536


def draw_queries(key, part):
    key = jax.random.fold_in(key, 11)
    sample = 1.5 * jax.random.truncated_normal(key, -4.0, 4.0, (TOKENS, HEADS * DH), jnp.float32)
    return sample.astype(jnp.bfloat16)


def draw_key_tokens(key, part):
    key = jax.random.fold_in(key, 22)
    sample = jax.random.truncated_normal(key, -5.0, 5.0, (TOKENS, HEADS * DH), jnp.float32)
    return sample.astype(jnp.bfloat16)


def draw_radial_table(key, part):
    key = jax.random.fold_in(key, 33)
    frame_index = jnp.arange(FRAMES)
    frame_gap = jnp.abs(frame_index[:, None] - frame_index[None, :])
    band_size = jnp.where(frame_gap == 1, NB // 2, jnp.where(frame_gap <= REACH, NB // 4, 0))
    cut_down = jax.random.randint(key, (FRAMES, FRAMES), 0, 1000) % (band_size // 2 + 1)
    return jnp.where(frame_gap == 0, NB, band_size - cut_down).astype(jnp.int32)


def block_scale(key, extent, shards, least, largest):
    gain, own = 1.0, jax.random.fold_in(key, 6)
    for dim, parts in shards:
        steps = jnp.exp(jax.random.uniform(jax.random.fold_in(own, dim), (parts,), jnp.float32, least / len(shards), largest / len(shards)))
        gain = gain * jnp.repeat(steps, extent[dim] // parts).reshape([-1 if axis == dim else 1 for axis in range(len(extent))])
    return gain


def noise(key, shape, deviation, reach, pieces=(), kind=jnp.bfloat16):
    gain = block_scale(key, shape, pieces, -0.22, 0.18) if pieces else 1.0
    drawn = jax.random.normal(key, shape, jnp.float32) * deviation * gain
    return jnp.minimum(jnp.maximum(drawn, -reach), reach).astype(kind)


def setup_inputs(seed: int = 0, part: int = 0) -> dict:
    key_list = jax.random.split(jax.random.key(seed), 6)
    own_keys = jax.random.split(jax.random.fold_in(key_list[5], part), 6)
    return {
        "queries": draw_queries(jax.random.fold_in(jax.random.fold_in(key_list[5], part), 71), part),
        "key_tokens": draw_key_tokens(jax.random.fold_in(jax.random.fold_in(key_list[5], part), 71), part),
        "value_tokens": noise(own_keys[2], (TOKENS, HD), 1.0, 6.0, ((0, 16),)),
        "radial_table": draw_radial_table(jax.random.fold_in(key_list[5], 71), part),
        "out_weight": noise(key_list[4], (HD, D), 0.25, 1.5, ((0, 2),)),
    }


def band_blocks(distance, blocks):
    if distance == 0:
        return blocks
    return blocks // 2 ** distance.bit_length()

def head_attend(query_head, near_keys, near_values, counts):
    query_blocks = query_head.reshape(NB, BS, DH).astype(jnp.float32)
    key_parts = []
    value_parts = []
    mask_parts = []
    for slot_index in range(2 * REACH + 1):
        band_size = band_blocks(abs(slot_index - REACH), NB)
        if band_size == 0:
            continue
        key_blocks = near_keys[slot_index].reshape(NB, BS, DH)
        value_blocks = near_values[slot_index].reshape(NB, BS, DH)
        for offset in range(band_size):
            key_parts.append(jnp.roll(key_blocks, -offset, axis=0))
            value_parts.append(jnp.roll(value_blocks, -offset, axis=0))
            mask_parts.append(jnp.full((BS,), offset, jnp.int32) < counts[slot_index])
    gathered_keys = jnp.concatenate(key_parts, axis=1).astype(jnp.float32)
    gathered_values = jnp.concatenate(value_parts, axis=1).astype(jnp.float32)
    key_mask = jnp.concatenate(mask_parts)
    scores = jnp.einsum('nqd,nkd->nqk', query_blocks, gathered_keys) / math.sqrt(DH)
    scores = jnp.where(key_mask[None, None, :], scores, -jnp.inf)
    row_max = lax.optimization_barrier(jnp.max(scores, axis=-1, keepdims=True))
    weights = jnp.exp(scores - row_max)
    weight_sum = lax.optimization_barrier(jnp.sum(weights, axis=-1, keepdims=True))
    weight_bf16 = lax.optimization_barrier(weights.astype(jnp.bfloat16)).astype(jnp.float32)
    blended = jnp.einsum('nqk,nkd->nqd', weight_bf16, gathered_values) / weight_sum
    return blended.reshape(NB * BS, DH)

def reference(queries, key_tokens, value_tokens, radial_table, out_weight):
    frame_len = NB * BS
    near_span = 2 * REACH + 1
    frame_shape = (FRAMES, frame_len, HEADS, DH)
    frame_padding = ((REACH, REACH), (0, 0), (0, 0), (0, 0))
    query_frames = queries.reshape(frame_shape)
    padded_keys = jnp.pad(key_tokens.reshape(frame_shape), frame_padding)
    padded_values = jnp.pad(value_tokens.reshape(frame_shape), frame_padding)
    padded_table = jnp.pad(radial_table, ((0, 0), (REACH, REACH)))

    def attend_frame(frame_index):
        query_frame = lax.dynamic_index_in_dim(query_frames, frame_index, 0, keepdims=False)
        near_keys = lax.dynamic_slice_in_dim(padded_keys, frame_index, near_span, 0)
        near_values = lax.dynamic_slice_in_dim(padded_values, frame_index, near_span, 0)
        table_row = lax.dynamic_index_in_dim(padded_table, frame_index, 0, keepdims=False)
        counts = lax.dynamic_slice_in_dim(table_row, frame_index, near_span, 0)

        def per_head(inputs):
            return head_attend(inputs[0], inputs[1], inputs[2], counts)
        head_inputs = (jnp.moveaxis(query_frame, 1, 0), jnp.moveaxis(near_keys, 2, 0), jnp.moveaxis(near_values, 2, 0))
        outputs = lax.map(per_head, head_inputs)
        return jnp.transpose(outputs, (1, 0, 2)).reshape(frame_len, HEADS * DH).astype(jnp.bfloat16)
    attended = lax.map(attend_frame, jnp.arange(FRAMES).astype(jnp.int32))
    attended = attended.reshape(TOKENS, HEADS * DH)
    return jnp.dot(attended, out_weight, preferred_element_type=jnp.float32).astype(jnp.bfloat16)
```

```python
import functools
import math

import jax
import jax.numpy as jnp
from jax import lax
from jax.experimental import pallas as pl
from jax.experimental.pallas import tpu as pltpu
from jax.sharding import PartitionSpec as P

DH = 128
BS = 128
GROUPS = (4, 4, 4)
STAT_ROWS = 16
NEG = -1e30
LOG2_SCALE = math.log2(math.e) / math.sqrt(DH)


def frame_ids(frames):
    frame = lax.axis_index("frame")
    odd = lax.rem(frame, 2)
    partner = frame + 1 - 2 * odd
    near = frame + 2 - 4 * odd
    away = frame - 2 + 4 * odd
    return frame, partner, near, away


def entry(table_ref, frames, query_frame, key_frame):
    inside = (key_frame >= 0) & (key_frame < frames)
    count = table_ref[query_frame, jnp.clip(key_frame, 0, frames - 1)]
    return jnp.where(inside, count, 0)


def attend(query, parts):
    scores = []
    for keys, _, valid in parts:
        raw = lax.dot_general(
            query, keys, (((1,), (1,)), ((), ())), preferred_element_type=jnp.float32
        )
        scores.append(raw if valid is None else jnp.where(valid, raw, NEG))
    row_max = scores[0].max(axis=1, keepdims=True)
    for raw in scores[1:]:
        row_max = jnp.maximum(row_max, raw.max(axis=1, keepdims=True))
    total, blended = 0.0, 0.0
    for raw, (_, values, _) in zip(scores, parts):
        weights = jnp.exp2((raw - row_max) * LOG2_SCALE)
        total = total + weights.sum(axis=1, keepdims=True)
        blended = blended + jnp.dot(
            weights.astype(jnp.bfloat16), values, preferred_element_type=jnp.float32
        )
    return blended / total, row_max * LOG2_SCALE + jnp.log2(total)


def split_three(x):
    high = x.astype(jnp.bfloat16).astype(jnp.float32)
    rest = x - high
    middle = rest.astype(jnp.bfloat16).astype(jnp.float32)
    return high, middle, rest - middle


def put_stats(stats, lanes, head, logsum):
    for part, value in enumerate(split_three(logsum)):
        stats = jnp.where(lanes == 3 * head + part, value, stats)
    return stats


def write_stats(out_ref, stats, rows):
    out_ref[rows : rows + STAT_ROWS, :] = jnp.zeros(
        (STAT_ROWS, out_ref.shape[1]), out_ref.dtype
    )
    out_ref[rows : rows + STAT_ROWS, :rows] = stats.T[:STAT_ROWS].astype(out_ref.dtype)


def read_stats(ref, rows):
    stats = ref[rows : rows + STAT_ROWS, :rows].astype(jnp.float32)
    padding = jnp.zeros((DH - STAT_ROWS, rows), jnp.float32)
    return jnp.concatenate([stats, padding], axis=0).T


def lane_of(stats, lanes, lane):
    return jnp.sum(jnp.where(lanes == lane, stats, 0.0), axis=1, keepdims=True)


def partner_kernel(
    frames, heads, table_ref, partner_query, far_query, keys, values, near, near_first, away, out, far_out
):
    rows = partner_query.shape[0]
    frame, partner_frame, near_frame, away_frame = frame_ids(frames)
    core = lax.axis_index("head")
    own_count = entry(table_ref, frames, partner_frame, frame)
    near_count = entry(table_ref, frames, partner_frame, near_frame)
    away_count = entry(table_ref, frames, partner_frame, away_frame)
    lanes = lax.broadcasted_iota(jnp.int32, (rows, DH), 1)
    stats = jnp.zeros((rows, DH), jnp.float32)
    far_stats = jnp.zeros((rows, DH), jnp.float32)
    blocks = rows // BS
    all_blocks = keys.shape[0] // BS
    for head in range(heads):
        cols = slice(head * DH, (head + 1) * DH)
        sums, far_sums = [], []
        for block in range(blocks):
            mine = slice(block * BS, (block + 1) * BS)
            mine_values = slice(rows + block * BS, rows + (block + 1) * BS)
            parts = []
            for offset in range(2):
                place = lax.rem(core * blocks + block + offset, all_blocks)
                here = pl.ds(pl.multiple_of(place * BS, BS), BS)
                valid = None if offset == 0 else own_count > offset
                parts.append((keys[here, cols], values[here, cols], valid))
                if block + offset < blocks:
                    at = (block + offset) * BS
                    near_keys = near[at : at + BS, cols]
                    near_values = near[rows + at : rows + at + BS, cols]
                else:
                    near_keys = near_first[:BS, cols]
                    near_values = near_first[BS : 2 * BS, cols]
                parts.append((near_keys, near_values, near_count > offset))
            parts.append((away[mine, cols], away[mine_values, cols], away_count > 0))
            blended, logsum = attend(partner_query[mine, cols], parts)
            out[mine, cols] = blended.astype(out.dtype)
            sums.append(logsum)
            far_blended, far_logsum = attend(
                far_query[mine, cols], [(near[mine, cols], near[mine_values, cols], None)]
            )
            far_out[mine, cols] = far_blended.astype(out.dtype)
            far_sums.append(far_logsum)
        stats = put_stats(stats, lanes, head, jnp.concatenate(sums, axis=0))
        far_stats = put_stats(far_stats, lanes, head, jnp.concatenate(far_sums, axis=0))
    write_stats(out, stats, rows)
    write_stats(far_out, far_stats, rows)


def own_kernel(frames, heads, table_ref, query, keys, values, near, away, out, out_stats):
    rows = query.shape[0]
    frame, _, near_frame, away_frame = frame_ids(frames)
    near_valid = entry(table_ref, frames, frame, near_frame) > 0
    away_valid = entry(table_ref, frames, frame, away_frame) > 0
    lanes = lax.broadcasted_iota(jnp.int32, (rows, DH), 1)
    stats = jnp.zeros((rows, DH), jnp.float32)
    for head in range(heads):
        cols = slice(head * DH, (head + 1) * DH)
        sums = []
        for block in range(rows // BS):
            mine = slice(block * BS, (block + 1) * BS)
            mine_values = slice(rows + block * BS, rows + (block + 1) * BS)
            blended, logsum = attend(
                query[mine, cols],
                [
                    (keys[:, cols], values[:, cols], None),
                    (near[mine, cols], near[mine_values, cols], near_valid),
                    (away[mine, cols], away[mine_values, cols], away_valid),
                ],
            )
            out[mine, cols] = blended
            sums.append(logsum)
        stats = jnp.where(lanes == head, jnp.concatenate(sums, axis=0), stats)
    out_stats[...] = stats


def merge_kernel(frames, heads, table_ref, own, own_stats, partner, far, out):
    rows = own.shape[0]
    frame, _, _, _ = frame_ids(frames)
    odd = lax.rem(frame, 2)
    far_valid = entry(table_ref, frames, frame, frame - 3 + 6 * odd) > 0
    lanes = lax.broadcasted_iota(jnp.int32, (rows, DH), 1)
    own_all = own_stats[...]
    partner_all = read_stats(partner, rows)
    far_all = read_stats(far, rows)
    for head in range(heads):
        cols = slice(head * DH, (head + 1) * DH)
        mine = (lanes >= 3 * head) & (lanes < 3 * head + 3)
        own_sum = lane_of(own_all, lanes, head)
        partner_sum = jnp.sum(jnp.where(mine, partner_all, 0.0), axis=1, keepdims=True)
        far_sum = jnp.sum(jnp.where(mine, far_all, 0.0), axis=1, keepdims=True)
        far_sum = jnp.where(far_valid, far_sum, NEG)
        top = jnp.maximum(jnp.maximum(own_sum, partner_sum), far_sum)
        own_weight = jnp.exp2(own_sum - top)
        partner_weight = jnp.exp2(partner_sum - top)
        far_weight = jnp.exp2(far_sum - top)
        mixed = (
            own_weight * own[:, cols]
            + partner_weight * partner[:rows, cols].astype(jnp.float32)
            + far_weight * far[:rows, cols].astype(jnp.float32)
        )
        out[:, cols] = (mixed / (own_weight + partner_weight + far_weight)).astype(out.dtype)


def whole(shape):
    return pl.BlockSpec(shape, lambda i: (0,) * len(shape))


def column(rows, width, index):
    return pl.BlockSpec((rows, width), lambda i: (0, index))


def run(body, name, table, operands, specs, out_shapes, flops):
    one = not isinstance(out_shapes, (list, tuple))
    shapes = [out_shapes] if one else list(out_shapes)
    out = pl.pallas_call(
        body,
        grid=(1,),
        in_specs=[pl.BlockSpec(memory_space=pltpu.SMEM)] + specs,
        out_specs=[whole(s.shape) for s in shapes],
        out_shape=shapes,
        compiler_params=pltpu.CompilerParams(vmem_limit_bytes=40 * 1024 * 1024),
        cost_estimate=pl.CostEstimate(
            flops=flops, bytes_accessed=4 * 1024 * 1024, transcendentals=flops // 512
        ),
        name=name,
    )(table, *operands)
    return out[0] if one else out


def per_device(queries, key_tokens, value_tokens, radial_table, out_weight):
    frames = lax.axis_size("frame")
    rows = queries.shape[0]
    cores = lax.axis_size("head")
    every = range(frames)

    def moves(target):
        return [(f, target(f)) for f in every if 0 <= target(f) < frames]

    partner_moves = moves(lambda f: f ^ 1)
    near_moves = moves(lambda f: f - 2 if f % 2 == 0 else f + 2)
    away_moves = moves(lambda f: f + 2 if f % 2 == 0 else f - 2)
    far_moves = moves(lambda f: f - 1 if f % 2 == 0 else f + 1)
    core_moves = [(c, cores - 1 - c) for c in range(cores)]

    all_keys = lax.all_gather(key_tokens, "head", axis=0, tiled=True)
    all_values = lax.all_gather(value_tokens, "head", axis=0, tiled=True)
    all_weight = lax.all_gather(out_weight, "head", axis=0, tiled=True)

    attended = []
    first = 0
    for heads in GROUPS:
        width = heads * DH
        index = first // heads
        at = first * DH
        first += heads
        query = queries[:, at : at + width]
        key_value = jnp.concatenate(
            [key_tokens[:, at : at + width], value_tokens[:, at : at + width]], axis=0
        )
        partner_query = lax.ppermute(query, "frame", partner_moves)
        near = lax.ppermute(key_value, "frame", near_moves)
        away = lax.ppermute(key_value, "frame", away_moves)
        far_query = lax.ppermute(partner_query, "frame", away_moves)
        near_first = lax.ppermute(
            jnp.concatenate([near[:BS], near[rows : rows + BS]], axis=0), "head", core_moves
        )
        packed = jax.ShapeDtypeStruct((rows + STAT_ROWS, width), jnp.bfloat16)
        full = column(cores * rows, width, index)
        part, far_part = run(
            functools.partial(partner_kernel, frames, heads),
            "partner_part",
            radial_table,
            (partner_query, far_query, all_keys, all_values, near, near_first, away),
            [whole((rows, width))] * 2
            + [full, full, whole((2 * rows, width)), whole((2 * BS, width)), whole((2 * rows, width))],
            [packed, packed],
            heads * rows * 768 * DH * 4,
        )
        part = lax.ppermute(part, "frame", partner_moves)
        far_part = lax.ppermute(far_part, "frame", far_moves)
        own, own_stats = run(
            functools.partial(own_kernel, frames, heads),
            "own_part",
            radial_table,
            (queries, all_keys, all_values, near, away),
            [column(rows, width, index), full, full] + [whole((2 * rows, width))] * 2,
            [
                jax.ShapeDtypeStruct((rows, width), jnp.float32),
                jax.ShapeDtypeStruct((rows, DH), jnp.float32),
            ],
            heads * rows * 768 * DH * 4,
        )
        attended.append(
            run(
                functools.partial(merge_kernel, frames, heads),
                "merge_parts",
                radial_table,
                (own, own_stats, part, far_part),
                [whole((rows, width)), whole((rows, DH))] + [whole((rows + STAT_ROWS, width))] * 2,
                jax.ShapeDtypeStruct((rows, width), jnp.bfloat16),
                heads * rows * DH * 8,
            )
        )
    projected = jnp.dot(
        jnp.concatenate(attended, axis=1), all_weight, preferred_element_type=jnp.float32
    )
    return projected.astype(jnp.bfloat16)


def solution(mesh):
    in_specs = (
        P(("clip", "frame", "head"), None),
        P(("clip", "frame", "head"), None),
        P(("clip", "frame", "head"), None),
        P(),
        P("head", None),
    )
    out_specs = P(("clip", "frame", "head"), None)
    return jax.shard_map(
        per_device, mesh=mesh, in_specs=in_specs, out_specs=out_specs, check_vma=False
    )
```

```python
import functools
import math

import jax
import jax.numpy as jnp
from jax import lax
from jax.experimental import pallas as pl
from jax.experimental.pallas import tpu as pltpu
from jax.sharding import PartitionSpec as P

DH = 128
BS = 128
CROSS = 3
STAT_ROWS = 16
BATCH = 4
TILE = 768
NEG = -1e30
LOG2_SCALE = math.log2(math.e) / math.sqrt(DH)
MIB = 1024 * 1024


def frame_ids():
    frame = lax.axis_index("frame")
    odd = lax.rem(frame, 2)
    sign = 1 - 2 * odd
    return frame, sign


def entry(table_ref, query_frame, key_frame):
    frames = table_ref.shape[0]
    inside = (key_frame >= 0) & (key_frame < frames)
    count = table_ref[query_frame, jnp.clip(key_frame, 0, frames - 1)]
    return jnp.where(inside, count, 0)


def attend(problems):
    scores = []
    for query, parts in problems:
        row = []
        for keys, _, valid in parts:
            raw = lax.dot_general(
                query, keys, (((1,), (1,)), ((), ())), preferred_element_type=jnp.float32
            )
            row.append(raw if valid is None else jnp.where(valid, raw, NEG))
        scores.append(row)
    tops = []
    for row in scores:
        best = None
        for raw in row:
            for at in range(0, raw.shape[1], BS):
                piece = raw[:, at : at + BS]
                best = piece if best is None else jnp.maximum(best, piece)
        tops.append(best.max(axis=1, keepdims=True))
    weights = [
        [jnp.exp2((raw - top) * LOG2_SCALE) for raw in row] for row, top in zip(scores, tops)
    ]
    totals = []
    for row in weights:
        total = None
        for weight in row:
            for at in range(0, weight.shape[1], BS):
                piece = weight[:, at : at + BS]
                total = piece if total is None else total + piece
        totals.append(total.sum(axis=1, keepdims=True))
    results = []
    for (_, parts), row, top, total in zip(problems, weights, tops, totals):
        blended = 0.0
        for (_, values, _), weight in zip(parts, row):
            blended = blended + jnp.dot(
                weight.astype(jnp.bfloat16), values, preferred_element_type=jnp.float32
            )
        results.append((blended / total, top * LOG2_SCALE + jnp.log2(total)))
    return results


def attend_heads(heads, blocks, problem, out, dtype):
    rows = blocks * BS
    lanes = lax.broadcasted_iota(jnp.int32, (rows, DH), 1)
    stats = jnp.zeros((rows, DH), jnp.float32)
    items = [(place, head, block) for place, head in enumerate(heads) for block in range(blocks)]
    sums = {}
    for at in range(0, len(items), BATCH):
        chunk = items[at : at + BATCH]
        results = attend([problem(head, block) for _, head, block in chunk])
        for (place, head, block), (blended, logsum) in zip(chunk, results):
            out[block * BS : (block + 1) * BS, place * DH : (place + 1) * DH] = blended.astype(dtype)
            sums[head, block] = logsum
    for head in heads:
        column = jnp.concatenate([sums[head, block] for block in range(blocks)], axis=0)
        stats = jnp.where(lanes == head, column, stats)
    return stats


def head_cols(head):
    return slice(head * DH, (head + 1) * DH)


def pair(ref, col, block):
    rows = ref.shape[0] // 2
    cols = head_cols(col)
    return (
        ref[block * BS : (block + 1) * BS, cols],
        ref[rows + block * BS : rows + (block + 1) * BS, cols],
    )


def following(ref, first, col, first_col, block):
    if (block + 1) * BS < ref.shape[0] // 2:
        return pair(ref, col, block + 1)
    return pair(first, first_col, 0)


class Near:
    def __init__(self, refs):
        self.refs = refs

    def away(self, head):
        if head < 6:
            return self.refs["major1"], head
        if head < 9:
            return self.refs["major2"], head - 6
        return self.refs["major3"], head - 9

    def near(self, head):
        if head < 9:
            return self.refs["minor1"], head - 3
        return self.refs["minor2"], head - 9

    def near_first(self, head):
        if head < 9:
            return self.refs["first1"], head - 3
        return self.refs["first2"], head - 9

    def relay(self, head):
        if head < 6:
            return self.refs["minor2"], head
        return self.refs["minor3"], head - 6


def partner_kernel(heads, names, table_ref, query, keys, values, sib_keys, sib_values, *rest):
    refs = dict(zip(names, rest))
    out = rest[len(names)]
    buffers = Near(refs)
    rows = query.shape[0]
    blocks = rows // BS
    frame, sign = frame_ids()
    partner = frame + sign
    own_count = entry(table_ref, partner, frame)
    near_count = entry(table_ref, partner, frame + 2 * sign)
    away_valid = entry(table_ref, partner, frame - 2 * sign) > 0
    relay_valid = entry(table_ref, partner, frame + 4 * sign) > 0
    cross_valid = entry(table_ref, partner, frame - sign) > 0

    def problem(head, block):
        mine = slice(block * BS, (block + 1) * BS)
        cols = head_cols(head)
        parts = [(keys[mine, cols], values[mine, cols], None)]
        if block + 1 < blocks:
            after = slice((block + 1) * BS, (block + 2) * BS)
            parts.append((keys[after, cols], values[after, cols], own_count > 1))
        else:
            parts.append((sib_keys[:BS, cols], sib_values[:BS, cols], own_count > 1))
        away, col = buffers.away(head)
        parts.append((*pair(away, col, block), away_valid))
        if head < CROSS:
            parts.append((*pair(refs["major2"], CROSS + head, block), cross_valid))
        else:
            near, col = buffers.near(head)
            first, first_col = buffers.near_first(head)
            parts.append((*pair(near, col, block), near_count > 0))
            parts.append((*following(near, first, col, first_col, block), near_count > 1))
            relay, col = buffers.relay(head)
            parts.append((*pair(relay, col, block), relay_valid))
        return query[mine, cols], parts

    stats = attend_heads(heads, blocks, problem, out, out.dtype)
    out[rows:, :] = jnp.zeros((STAT_ROWS, out.shape[1]), out.dtype)
    rest_sum = stats.T[:STAT_ROWS]
    for part in range(3):
        piece = rest_sum.astype(jnp.bfloat16)
        out[rows:, part * rows : (part + 1) * rows] = piece
        rest_sum = rest_sum - piece.astype(jnp.float32)


def own_kernel(heads, names, table_ref, query, keys, values, sib_keys, sib_values, *rest):
    refs = dict(zip(names, rest))
    out, out_stats = rest[len(names) :]
    buffers = Near(refs)
    rows = query.shape[0]
    blocks = rows // BS
    frame, sign = frame_ids()
    near_valid = entry(table_ref, frame, frame + 2 * sign) > 0
    away_valid = entry(table_ref, frame, frame - 2 * sign) > 0
    cross_count = entry(table_ref, frame, frame - sign)
    far_valid = entry(table_ref, frame, frame - 3 * sign) > 0

    def problem(head, block):
        mine = slice(block * BS, (block + 1) * BS)
        cols = head_cols(head)
        parts = [
            (keys[:, cols], values[:, cols], None),
            (sib_keys[:, cols], sib_values[:, cols], None),
        ]
        away, col = buffers.away(head)
        parts.append((*pair(away, col, block), away_valid))
        if head < CROSS:
            cross = refs["major2"]
            parts.append((*pair(cross, CROSS + head, block), cross_count > 0))
            parts.append(
                (
                    *following(cross, refs["first2"], CROSS + head, CROSS + head, block),
                    cross_count > 1,
                )
            )
            parts.append((*pair(refs["major3"], CROSS + head, block), far_valid))
        else:
            near, col = buffers.near(head)
            parts.append((*pair(near, col, block), near_valid))
        return query[mine, cols], parts

    out_stats[...] = attend_heads(heads, blocks, problem, out, out.dtype)


def read_stats(ref):
    rows = ref.shape[0] - STAT_ROWS
    total = 0.0
    for part in range(3):
        total = total + ref[rows:, part * rows : (part + 1) * rows].astype(jnp.float32)
    padding = jnp.zeros((DH - STAT_ROWS, rows), jnp.float32)
    return jnp.concatenate([total, padding], axis=0).T


def final_kernel(own_heads, part_heads, *refs):
    count = len(own_heads)
    owns, stats = refs[0 : 2 * count : 2], refs[1 : 2 * count : 2]
    parts = refs[2 * count : 2 * count + len(part_heads)]
    weight, out, attended = refs[2 * count + len(part_heads) :]

    @pl.when(pl.program_id(0) == 0)
    def _():
        rows = out.shape[0]
        lanes = lax.broadcasted_iota(jnp.int32, (rows, DH), 1)
        own_sum = jnp.zeros((rows, DH), jnp.float32)
        own_at, part_at = {}, {}
        for ref, stat, heads in zip(owns, stats, own_heads):
            for place, head in enumerate(heads):
                own_at[head] = ref, place
                own_sum = jnp.where(lanes == head, stat[...], own_sum)
        part_sum = jnp.zeros((rows, DH), jnp.float32)
        for ref, heads in zip(parts, part_heads):
            received = read_stats(ref)
            for place, head in enumerate(heads):
                part_at[head] = ref, place
                part_sum = jnp.where(lanes == head, received, part_sum)
        top = jnp.maximum(own_sum, part_sum)
        own_weight = jnp.exp2(own_sum - top)
        part_weight = jnp.exp2(part_sum - top)
        total = own_weight + part_weight
        own_weight = own_weight / total
        part_weight = part_weight / total
        for head in sorted(own_at):
            own, own_place = own_at[head]
            part, part_place = part_at[head]
            mixed = (
                own_weight[:, head : head + 1] * own[:, head_cols(own_place)]
                + part_weight[:, head : head + 1]
                * part[:rows, head_cols(part_place)].astype(jnp.float32)
            )
            attended[:, head_cols(head)] = mixed.astype(attended.dtype)

    out[...] = jnp.dot(
        attended[...], weight[...], preferred_element_type=jnp.float32
    ).astype(out.dtype)


def whole(shape):
    return pl.BlockSpec(shape, lambda i: (0,) * len(shape))


def run(body, name, table, operands, out_shapes, flops):
    return pl.pallas_call(
        body,
        grid=(1,),
        in_specs=[pl.BlockSpec(memory_space=pltpu.SMEM)] + [whole(x.shape) for x in operands],
        out_specs=[whole(s.shape) for s in out_shapes],
        out_shape=out_shapes,
        compiler_params=pltpu.CompilerParams(vmem_limit_bytes=40 * MIB),
        cost_estimate=pl.CostEstimate(
            flops=flops, bytes_accessed=4 * MIB, transcendentals=flops // 512
        ),
        name=name,
    )(table, *operands)


def per_device(queries, key_tokens, value_tokens, radial_table, out_weight):
    frames = lax.axis_size("frame")
    cores = lax.axis_size("head")
    rows, features = queries.shape
    heads_all = features // DH

    def moves(target):
        return [(f, target(f)) for f in range(frames) if 0 <= target(f) < frames]

    partner_moves = moves(lambda f: f ^ 1)
    near_moves = moves(lambda f: f - 2 if f % 2 == 0 else f + 2)
    away_moves = moves(lambda f: f + 2 if f % 2 == 0 else f - 2)
    core_moves = [(c, cores - 1 - c) for c in range(cores)]

    def pack(first, last):
        cols = slice(first * DH, last * DH)
        return jnp.concatenate([key_tokens[:, cols], value_tokens[:, cols]], axis=0)

    def firsts(packed):
        return jnp.concatenate([packed[:BS], packed[rows : rows + BS]], axis=0)

    def beside(*packed):
        return jnp.concatenate(packed, axis=1)

    half = CROSS * DH
    major1 = lax.ppermute(pack(0, 6), "frame", away_moves)
    minor1 = lax.ppermute(pack(3, 9), "frame", near_moves)
    cross = lax.ppermute(pack(0, 3), "frame", partner_moves)
    partner_query = lax.ppermute(queries, "frame", partner_moves)
    sib_keys = lax.ppermute(key_tokens, "head", core_moves)
    sib_values = lax.ppermute(value_tokens, "head", core_moves)
    all_weight = lax.all_gather(out_weight, "head", axis=0, tiled=True)
    major2 = lax.ppermute(beside(pack(6, 9), cross), "frame", away_moves)
    minor2 = lax.ppermute(beside(pack(9, 12), minor1[:, :half]), "frame", near_moves)
    first1 = lax.ppermute(firsts(minor1), "head", core_moves)
    major3 = lax.ppermute(beside(pack(9, 12), major2[:, half:]), "frame", away_moves)
    minor3 = lax.ppermute(beside(minor1[:, half:], minor2[:, :half]), "frame", near_moves)
    first2 = lax.ppermute(
        firsts(beside(minor2[:, :half], major2[:, half:])), "head", core_moves
    )
    refs = {
        "major1": major1,
        "major2": major2,
        "major3": major3,
        "minor1": minor1,
        "minor2": minor2,
        "minor3": minor3,
        "first1": first1,
        "first2": first2,
    }
    local = (key_tokens, value_tokens, sib_keys, sib_values)

    def partner_part(heads, names):
        shape = jax.ShapeDtypeStruct((rows + STAT_ROWS, len(heads) * DH), jnp.bfloat16)
        (part,) = run(
            functools.partial(partner_kernel, heads, names),
            "partner_part",
            radial_table,
            (partner_query, *local, *(refs[n] for n in names)),
            [shape],
            len(heads) * rows * 6 * BS * DH * 4,
        )
        return lax.ppermute(part, "frame", partner_moves)

    def own_part(heads, names):
        return run(
            functools.partial(own_kernel, heads, names),
            "own_part",
            radial_table,
            (queries, *local, *(refs[n] for n in names)),
            [
                jax.ShapeDtypeStruct((rows, len(heads) * DH), jnp.float32),
                jax.ShapeDtypeStruct((rows, DH), jnp.float32),
            ],
            len(heads) * rows * 6 * BS * DH * 4,
        )

    part_heads = (tuple(range(0, 6)), tuple(range(6, 12)))
    own_heads = (tuple(range(3, 9)), (0, 1, 2, 9, 10, 11))
    part0 = partner_part(part_heads[0], ("major1", "major2", "minor1", "minor2", "first1"))
    own0 = own_part(own_heads[0], ("major1", "major2", "minor1"))
    part1 = partner_part(
        part_heads[1], ("major2", "major3", "minor1", "minor2", "minor3", "first1", "first2")
    )
    own1 = own_part(own_heads[1], ("major1", "major2", "major3", "minor2", "first2"))

    operands = (*own0, *own1, part0, part1)
    columns = out_weight.shape[1]
    projected = pl.pallas_call(
        functools.partial(final_kernel, own_heads, part_heads),
        grid=(columns // TILE,),
        in_specs=[whole(x.shape) for x in operands]
        + [pl.BlockSpec((features, TILE), lambda i: (0, i))],
        out_specs=pl.BlockSpec((rows, TILE), lambda i: (0, i)),
        out_shape=jax.ShapeDtypeStruct((rows, columns), jnp.bfloat16),
        scratch_shapes=[pltpu.VMEM((rows, features), jnp.bfloat16)],
        compiler_params=pltpu.CompilerParams(vmem_limit_bytes=40 * MIB),
        cost_estimate=pl.CostEstimate(
            flops=2 * rows * features * columns, bytes_accessed=12 * MIB, transcendentals=0
        ),
        name="merge_and_project",
    )(*operands, all_weight)
    return projected


def solution(mesh):
    in_specs = (
        P(("clip", "frame", "head"), None),
        P(("clip", "frame", "head"), None),
        P(("clip", "frame", "head"), None),
        P(),
        P("head", None),
    )
    out_specs = P(("clip", "frame", "head"), None)
    return jax.shard_map(
        per_device, mesh=mesh, in_specs=in_specs, out_specs=out_specs, check_vma=False
    )
```

```python
import functools
import math

import jax
import jax.numpy as jnp
from jax import lax
from jax.experimental import pallas as pl
from jax.experimental.pallas import tpu as pltpu
from jax.sharding import PartitionSpec as P

DH = 128
BS = 128
GROUPS = ((0, 3), (3, 9), (9, 12))
CROSS = 3
BATCH = 4
TILE = 768
NEG = -1e30
LOG2_SCALE = math.log2(math.e) / math.sqrt(DH)
MIB = 1024 * 1024


def frame_ids():
    frame = lax.axis_index("frame")
    sign = 1 - 2 * lax.rem(frame, 2)
    pair_is_away = lax.rem(lax.div(frame, 2) + lax.rem(frame, 2), 2) == 1
    return frame, sign, pair_is_away


def entry(table_ref, query_frame, key_frame):
    frames = table_ref.shape[0]
    inside = (key_frame >= 0) & (key_frame < frames)
    count = table_ref[query_frame, jnp.clip(key_frame, 0, frames - 1)]
    return jnp.where(inside, count, 0)


def attend(problems):
    scores = []
    for query, parts in problems:
        row = []
        for keys, _, valid in parts:
            raw = lax.dot_general(
                query, keys, (((1,), (1,)), ((), ())), preferred_element_type=jnp.float32
            )
            row.append(raw if valid is None else jnp.where(valid, raw, NEG))
        scores.append(row)
    tops = []
    for row in scores:
        best = None
        for raw in row:
            for at in range(0, raw.shape[1], BS):
                piece = raw[:, at : at + BS]
                best = piece if best is None else jnp.maximum(best, piece)
        tops.append(best.max(axis=1, keepdims=True))
    weights = [
        [jnp.exp2((raw - top) * LOG2_SCALE) for raw in row] for row, top in zip(scores, tops)
    ]
    totals = []
    for row in weights:
        total = None
        for weight in row:
            for at in range(0, weight.shape[1], BS):
                piece = weight[:, at : at + BS]
                total = piece if total is None else total + piece
        totals.append(total.sum(axis=1, keepdims=True))
    results = []
    for (_, parts), row, top, total in zip(problems, weights, tops, totals):
        blended = 0.0
        for (_, values, _), weight in zip(parts, row):
            blended = blended + jnp.dot(
                weight.astype(jnp.bfloat16), values, preferred_element_type=jnp.float32
            )
        results.append((blended / total, top * LOG2_SCALE + jnp.log2(total)))
    return results


def attend_heads(group, blocks, problem, out):
    rows = blocks * BS
    heads = range(*group)
    lanes = lax.broadcasted_iota(jnp.int32, (rows, DH), 1)
    stats = jnp.zeros((rows, DH), jnp.float32)
    items = [(place, head, block) for place, head in enumerate(heads) for block in range(blocks)]
    sums = {}
    for at in range(0, len(items), BATCH):
        chunk = items[at : at + BATCH]
        results = attend([problem(head, block) for _, head, block in chunk])
        for (place, head, block), (blended, logsum) in zip(chunk, results):
            out[block * BS : (block + 1) * BS, head_cols(place)] = blended.astype(out.dtype)
            sums[place, block] = logsum
    for place in range(len(heads)):
        column = jnp.concatenate([sums[place, block] for block in range(blocks)], axis=0)
        stats = jnp.where(lanes == place, column, stats)
    return stats


def head_cols(head):
    return slice(head * DH, (head + 1) * DH)


def stat_rows(heads):
    return (4, 16) if heads <= 4 else (8, 32)


def write_stats(out, stats, heads):
    pad, count = stat_rows(heads)
    rows = stats.shape[0]
    packed, rest = 0.0, stats
    for part in range(3):
        piece = rest.astype(jnp.bfloat16).astype(jnp.float32)
        rest = rest - piece
        packed = packed + (pltpu.roll(piece, part * pad, 1) if part else piece)
    out[rows:, :] = jnp.zeros((count, out.shape[1]), out.dtype)
    out[rows:, :rows] = packed.T[:count].astype(out.dtype)


def read_stats(ref, heads):
    pad, count = stat_rows(heads)
    rows = ref.shape[0] - count
    packed = ref[rows:, :rows].astype(jnp.float32)
    padding = jnp.zeros((DH - count, rows), jnp.float32)
    packed = jnp.concatenate([packed, padding], axis=0).T
    return packed + pltpu.roll(packed, DH - pad, 1) + pltpu.roll(packed, DH - 2 * pad, 1)


def pair(ref, col, block):
    rows = ref.shape[0] // 2
    cols = head_cols(col)
    return (
        ref[block * BS : (block + 1) * BS, cols],
        ref[rows + block * BS : rows + (block + 1) * BS, cols],
    )


class Buffers:
    def __init__(self, refs, pair_is_away):
        self.refs = refs
        self.pair_is_away = pair_is_away

    def choose(self, first, second):
        return tuple(jnp.where(self.pair_is_away, a, b) for a, b in zip(first, second))

    def major(self, step, col, block):
        a, b = self.refs["a%d" % step], self.refs["b%d" % step]
        return self.choose(pair(a, col, block), pair(b, col, block))

    def minor(self, step, col, block):
        a, b = self.refs["a%d" % step], self.refs["b%d" % step]
        return self.choose(pair(b, col, block), pair(a, col, block))

    def away(self, head, block):
        return self.major(1, head, block) if head < 6 else self.major(3, head - 6, block)

    def near(self, head, block):
        return self.minor(1, head - 3, block) if head < 9 else self.minor(2, head - 9, block)

    def near_first(self, head):
        if head < 9:
            return pair(self.refs["first1"], head - 3, 0)
        first = self.refs["first2"]
        return self.choose(pair(first, CROSS + head - 9, 0), pair(first, head - 9, 0))

    def cross_first(self, head):
        first = self.refs["first2"]
        return self.choose(pair(first, head, 0), pair(first, CROSS + head, 0))

    def relay(self, head, block):
        return self.minor(3, head - 3, block) if head < 9 else self.minor(4, head - 9, block)


def partner_kernel(group, names, table_ref, query, keys, values, sib_keys, sib_values, *rest):
    frame, sign, pair_is_away = frame_ids()
    buffers = Buffers(dict(zip(names, rest)), pair_is_away)
    out = rest[len(names)]
    rows = query.shape[0]
    blocks = rows // BS
    partner = frame + sign
    own_count = entry(table_ref, partner, frame)
    near_count = entry(table_ref, partner, frame + 2 * sign)
    away_valid = entry(table_ref, partner, frame - 2 * sign) > 0
    relay_valid = entry(table_ref, partner, frame + 4 * sign) > 0
    cross_valid = entry(table_ref, partner, frame - sign) > 0

    def problem(head, block):
        mine = slice(block * BS, (block + 1) * BS)
        cols = head_cols(head)
        last = block + 1 == blocks
        parts = [(keys[mine, cols], values[mine, cols], None)]
        if last:
            parts.append((sib_keys[:BS, cols], sib_values[:BS, cols], own_count > 1))
        else:
            after = slice((block + 1) * BS, (block + 2) * BS)
            parts.append((keys[after, cols], values[after, cols], own_count > 1))
        parts.append((*buffers.away(head, block), away_valid))
        if head < CROSS:
            parts.append((*buffers.major(2, head, block), cross_valid))
        else:
            parts.append((*buffers.near(head, block), near_count > 0))
            after = buffers.near_first(head) if last else buffers.near(head, block + 1)
            parts.append((*after, near_count > 1))
            parts.append((*buffers.relay(head, block), relay_valid))
        return query[mine, cols], parts

    stats = attend_heads(group, blocks, problem, out)
    write_stats(out, stats, group[1] - group[0])


def own_kernel(group, names, table_ref, query, keys, values, sib_keys, sib_values, *rest):
    frame, sign, pair_is_away = frame_ids()
    buffers = Buffers(dict(zip(names, rest)), pair_is_away)
    out, out_stats = rest[len(names) :]
    rows = query.shape[0]
    blocks = rows // BS
    near_valid = entry(table_ref, frame, frame + 2 * sign) > 0
    away_valid = entry(table_ref, frame, frame - 2 * sign) > 0
    cross_count = entry(table_ref, frame, frame - sign)
    far_valid = entry(table_ref, frame, frame - 3 * sign) > 0

    def problem(head, block):
        mine = slice(block * BS, (block + 1) * BS)
        cols = head_cols(head)
        parts = [
            (keys[:, cols], values[:, cols], None),
            (sib_keys[:, cols], sib_values[:, cols], None),
            (*buffers.away(head, block), away_valid),
        ]
        if head < CROSS:
            last = block + 1 == blocks
            parts.append((*buffers.major(2, head, block), cross_count > 0))
            after = buffers.cross_first(head) if last else buffers.major(2, head, block + 1)
            parts.append((*after, cross_count > 1))
            parts.append((*buffers.major(4, head, block), far_valid))
        else:
            parts.append((*buffers.near(head, block), near_valid))
        return query[mine, cols], parts

    out_stats[...] = attend_heads(group, blocks, problem, out)


def weight_copies(groups, weight, buffer, sems):
    columns = buffer.shape[1]
    copies = []
    for tile in range(columns // TILE):
        cols = slice(tile * TILE, (tile + 1) * TILE)
        at, row = 0, []
        for index, (first, last) in enumerate(groups):
            size = (last - first) * DH
            row.append(
                pltpu.make_async_copy(
                    weight.at[first * DH : last * DH, cols],
                    buffer.at[at : at + size, cols],
                    sems.at[tile, index],
                )
            )
            at += size
        copies.append(row)
    return copies


def project_kernel(groups, has_base, weight, *refs):
    count = len(groups)
    operands, refs = refs[: 3 * count], refs[3 * count :]
    base = refs[0] if has_base else None
    out, attended, buffer, sems = refs[1:] if has_base else refs
    copies = weight_copies(groups, weight, buffer, sems)
    for row in copies:
        for copy in row:
            copy.start()
    rows = out.shape[0]
    at = 0
    for index, (first, last) in enumerate(groups):
        own, own_stats, part = operands[3 * index : 3 * index + 3]
        own_sum = own_stats[...]
        part_sum = read_stats(part, last - first)
        top = jnp.maximum(own_sum, part_sum)
        own_weight = jnp.exp2(own_sum - top)
        part_weight = jnp.exp2(part_sum - top)
        total = own_weight + part_weight
        own_weight = own_weight / total
        part_weight = part_weight / total
        for place in range(last - first):
            cols = head_cols(place)
            mixed = own_weight[:, place : place + 1] * own[:, cols] + part_weight[
                :, place : place + 1
            ] * part[:rows, cols].astype(jnp.float32)
            attended[:, head_cols(at + place)] = mixed.astype(attended.dtype)
        at += last - first
    for tile, row in enumerate(copies):
        cols = slice(tile * TILE, (tile + 1) * TILE)
        for copy in row:
            copy.wait()
        product = jnp.dot(attended[...], buffer[:, cols], preferred_element_type=jnp.float32)
        if has_base:
            product = product + base[:, cols]
        out[:, cols] = product.astype(out.dtype)


def whole(shape):
    return pl.BlockSpec(shape, lambda i: (0,) * len(shape))


def run(body, name, table, operands, out_shapes, flops):
    return pl.pallas_call(
        body,
        grid=(1,),
        in_specs=[pl.BlockSpec(memory_space=pltpu.SMEM)] + [whole(x.shape) for x in operands],
        out_specs=[whole(s.shape) for s in out_shapes],
        out_shape=out_shapes,
        compiler_params=pltpu.CompilerParams(vmem_limit_bytes=40 * MIB),
        cost_estimate=pl.CostEstimate(
            flops=flops, bytes_accessed=4 * MIB, transcendentals=flops // 512
        ),
        name=name,
    )(table, *operands)


def project(groups, weight, operands, base, dtype):
    rows = operands[0].shape[0]
    depth = sum(last - first for first, last in groups) * DH
    columns = weight.shape[1]
    extra = () if base is None else (base,)
    inputs = (*operands, *extra)
    return pl.pallas_call(
        functools.partial(project_kernel, groups, base is not None),
        grid=(1,),
        in_specs=[pl.BlockSpec(memory_space=pl.ANY)] + [whole(x.shape) for x in inputs],
        out_specs=whole((rows, columns)),
        out_shape=jax.ShapeDtypeStruct((rows, columns), dtype),
        scratch_shapes=[
            pltpu.VMEM((rows, depth), jnp.bfloat16),
            pltpu.VMEM((depth, columns), jnp.bfloat16),
            pltpu.SemaphoreType.DMA((columns // TILE, len(groups))),
        ],
        compiler_params=pltpu.CompilerParams(vmem_limit_bytes=40 * MIB),
        cost_estimate=pl.CostEstimate(
            flops=2 * rows * depth * columns, bytes_accessed=8 * MIB, transcendentals=0
        ),
        name="merge_and_project",
    )(weight, *inputs)


def per_device(queries, key_tokens, value_tokens, radial_table, out_weight):
    frames = lax.axis_size("frame")
    cores = lax.axis_size("head")
    rows = queries.shape[0]
    _, _, pair_is_away = frame_ids()

    def moves(target):
        return [(f, target(f)) for f in range(frames) if 0 <= target(f) < frames]

    partner_moves = moves(lambda f: f ^ 1)
    a_moves = moves(lambda f: f ^ 2)
    b_moves = moves(lambda f: f + 2 if f & 2 else f - 2)
    core_moves = [(c, cores - 1 - c) for c in range(cores)]

    def pack(first, last):
        cols = slice(first * DH, last * DH)
        return jnp.concatenate([key_tokens[:, cols], value_tokens[:, cols]], axis=0)

    def firsts(packed):
        return jnp.concatenate([packed[:BS], packed[rows : rows + BS]], axis=0)

    def choose(first, second):
        return jnp.where(pair_is_away, first, second)

    cross = lax.ppermute(pack(0, 3), "frame", partner_moves)
    a1 = lax.ppermute(choose(pack(3, 9), pack(0, 6)), "frame", a_moves)
    b1 = lax.ppermute(choose(pack(0, 6), pack(3, 9)), "frame", b_moves)
    partner_query = lax.ppermute(queries, "frame", partner_moves)
    sib_keys = lax.ppermute(key_tokens, "head", core_moves)
    sib_values = lax.ppermute(value_tokens, "head", core_moves)
    all_weight = lax.all_gather(out_weight, "head", axis=0, tiled=True)
    a2 = lax.ppermute(choose(pack(9, 12), cross), "frame", a_moves)
    b2 = lax.ppermute(choose(cross, pack(9, 12)), "frame", b_moves)
    a3 = lax.ppermute(choose(b1, pack(6, 12)), "frame", a_moves)
    b3 = lax.ppermute(choose(pack(6, 12), a1), "frame", b_moves)
    a4 = lax.ppermute(b2, "frame", a_moves)
    b4 = lax.ppermute(a2, "frame", b_moves)
    first1 = lax.ppermute(firsts(choose(b1, a1)), "head", core_moves)
    first2 = lax.ppermute(firsts(jnp.concatenate([a2, b2], axis=1)), "head", core_moves)
    refs = {
        "a1": a1,
        "a2": a2,
        "a3": a3,
        "a4": a4,
        "b1": b1,
        "b2": b2,
        "b3": b3,
        "b4": b4,
        "first1": first1,
        "first2": first2,
    }
    local = (key_tokens, value_tokens, sib_keys, sib_values)

    def partner_part(group, names):
        heads = group[1] - group[0]
        shape = jax.ShapeDtypeStruct((rows + stat_rows(heads)[1], heads * DH), jnp.bfloat16)
        (part,) = run(
            functools.partial(partner_kernel, group, names),
            "partner_part",
            radial_table,
            (partner_query, *local, *(refs[n] for n in names)),
            [shape],
            heads * rows * 6 * BS * DH * 4,
        )
        return lax.ppermute(part, "frame", partner_moves)

    def own_part(group, names):
        heads = group[1] - group[0]
        return run(
            functools.partial(own_kernel, group, names),
            "own_part",
            radial_table,
            (queries, *local, *(refs[n] for n in names)),
            [
                jax.ShapeDtypeStruct((rows, heads * DH), jnp.float32),
                jax.ShapeDtypeStruct((rows, DH), jnp.float32),
            ],
            heads * rows * 6 * BS * DH * 4,
        )

    low, middle, high = GROUPS
    part_low = partner_part(low, ("a1", "b1", "a2", "b2"))
    part_middle = partner_part(middle, ("a1", "b1", "a3", "b3", "first1"))
    own_middle = own_part(middle, ("a1", "b1", "a3", "b3"))
    own_high = own_part(high, ("a2", "b2", "a3", "b3"))
    part_high = partner_part(high, ("a2", "b2", "a3", "b3", "a4", "b4", "first2"))
    own_low = own_part(low, ("a1", "b1", "a2", "b2", "a4", "b4", "first2"))
    base = project((middle,), all_weight, (*own_middle, part_middle), None, jnp.float32)
    return project(
        (low, high), all_weight, (*own_low, part_low, *own_high, part_high), base, jnp.bfloat16
    )


def solution(mesh):
    in_specs = (
        P(("clip", "frame", "head"), None),
        P(("clip", "frame", "head"), None),
        P(("clip", "frame", "head"), None),
        P(),
        P("head", None),
    )
    out_specs = P(("clip", "frame", "head"), None)
    return jax.shard_map(
        per_device, mesh=mesh, in_specs=in_specs, out_specs=out_specs, check_vma=False
    )
```

```python
import functools
import math

import jax
import jax.numpy as jnp
from jax import lax
from jax.experimental import pallas as pl
from jax.experimental.pallas import tpu as pltpu
from jax.sharding import PartitionSpec as P

DH = 128
BS = 128
GROUP = 3
CROSS = 3
BATCH = 4
TILE = 768
NEG = -1e30
LOG2_SCALE = math.log2(math.e) / math.sqrt(DH)
MIB = 1024 * 1024


def frame_ids():
    frame = lax.axis_index("frame")
    sign = 1 - 2 * lax.rem(frame, 2)
    pair_is_away = lax.rem(lax.div(frame, 2) + lax.rem(frame, 2), 2) == 1
    return frame, sign, pair_is_away


def entry(table_ref, query_frame, key_frame):
    frames = table_ref.shape[0]
    inside = (key_frame >= 0) & (key_frame < frames)
    count = table_ref[query_frame, jnp.clip(key_frame, 0, frames - 1)]
    return jnp.where(inside, count, 0)


def attend(problems):
    scores = []
    for query, parts, _ in problems:
        row = []
        for keys, _, valid in parts:
            raw = lax.dot_general(
                query, keys, (((1,), (1,)), ((), ())), preferred_element_type=jnp.float32
            )
            row.append(raw if valid is None else jnp.where(valid, raw, NEG))
        scores.append(row)
    tops = []
    for (_, _, prior), row in zip(problems, scores):
        best = None
        for raw in row:
            for at in range(0, raw.shape[1], BS):
                piece = raw[:, at : at + BS]
                best = piece if best is None else jnp.maximum(best, piece)
        top = best.max(axis=1, keepdims=True) * LOG2_SCALE
        tops.append(top if prior is None else jnp.maximum(top, prior[1]))
    weights = [
        [jnp.exp2(raw * LOG2_SCALE - top) for raw in row] for row, top in zip(scores, tops)
    ]
    totals = []
    for row in weights:
        total = None
        for weight in row:
            for at in range(0, weight.shape[1], BS):
                piece = weight[:, at : at + BS]
                total = piece if total is None else total + piece
        totals.append(total.sum(axis=1, keepdims=True))
    results = []
    for (_, parts, prior), row, top, total in zip(problems, weights, tops, totals):
        blended = 0.0
        for (_, values, _), weight in zip(parts, row):
            blended = blended + jnp.dot(
                weight.astype(jnp.bfloat16), values, preferred_element_type=jnp.float32
            )
        if prior is not None:
            carry = jnp.exp2(prior[1] - top)
            total = total + carry
            blended = blended + carry * prior[0]
        results.append((blended / total, top + jnp.log2(total)))
    return results


def head_cols(head):
    return slice(head * DH, (head + 1) * DH)


def stat_rows(heads):
    return (4, 16) if heads <= 4 else (8, 32)


def write_stats(out, stats, heads):
    pad, count = stat_rows(heads)
    rows = stats.shape[0]
    packed, rest = 0.0, stats
    for part in range(3):
        piece = rest.astype(jnp.bfloat16).astype(jnp.float32)
        rest = rest - piece
        packed = packed + (pltpu.roll(piece, part * pad, 1) if part else piece)
    out[rows:, :] = jnp.zeros((count, out.shape[1]), out.dtype)
    out[rows:, :rows] = packed.T[:count].astype(out.dtype)


def read_stats(ref, heads):
    pad, count = stat_rows(heads)
    rows = ref.shape[0] - count
    packed = ref[rows:, :rows].astype(jnp.float32)
    padding = jnp.zeros((DH - count, rows), jnp.float32)
    packed = jnp.concatenate([packed, padding], axis=0).T
    return packed + pltpu.roll(packed, DH - pad, 1) + pltpu.roll(packed, DH - 2 * pad, 1)


def pair(ref, col, block):
    rows = ref.shape[0] // 2
    cols = head_cols(col)
    return (
        ref[block * BS : (block + 1) * BS, cols],
        ref[rows + block * BS : rows + (block + 1) * BS, cols],
    )


class Buffers:
    def __init__(self, refs, pair_is_away):
        self.refs = refs
        self.pair_is_away = pair_is_away

    def choose(self, first, second):
        return tuple(jnp.where(self.pair_is_away, a, b) for a, b in zip(first, second))

    def major(self, step, col, block):
        a, b = self.refs["a%d" % step], self.refs["b%d" % step]
        return self.choose(pair(a, col, block), pair(b, col, block))

    def minor(self, step, col, block):
        a, b = self.refs["a%d" % step], self.refs["b%d" % step]
        return self.choose(pair(b, col, block), pair(a, col, block))

    def away(self, head, block):
        return self.major(1, head, block) if head < 6 else self.major(3, head - 6, block)

    def near(self, head, block):
        return self.minor(1, head - 3, block) if head < 9 else self.minor(2, head - 9, block)

    def near_first(self, head):
        if head < 9:
            return pair(self.refs["first1"], head - 3, 0)
        first = self.refs["first2"]
        return self.choose(pair(first, CROSS + head - 9, 0), pair(first, head - 9, 0))

    def cross_first(self, head):
        first = self.refs["first2"]
        return self.choose(pair(first, head, 0), pair(first, CROSS + head, 0))

    def relay(self, head, block):
        return self.minor(3, head - 3, block) if head < 9 else self.minor(4, head - 9, block)


class Stage:
    def __init__(self, refs):
        frame, sign, pair_is_away = frame_ids()
        self.refs = refs
        self.buffers = Buffers(refs, pair_is_away)
        self.frame, self.sign = frame, sign
        self.partner = frame + sign
        self.counts = {}

    def count(self, kind, distance):
        key = (kind, distance)
        if key not in self.counts:
            source = self.frame if kind == "own" else self.partner
            target = self.frame + distance * self.sign
            self.counts[key] = entry(self.refs["table"], source, target)
        return self.counts[key]

    def parts(self, kind, name, head, block, blocks):
        buffers, refs = self.buffers, self.refs
        cols = head_cols(head)
        mine = slice(block * BS, (block + 1) * BS)
        after = slice((block + 1) * BS, (block + 2) * BS)
        last = block + 1 == blocks
        if name == "local" and kind == "own":
            yield refs["keys"][:, cols], refs["values"][:, cols], None
            yield refs["sib_keys"][:, cols], refs["sib_values"][:, cols], None
        elif name == "local":
            yield refs["keys"][mine, cols], refs["values"][mine, cols], None
            valid = self.count(kind, 0) > 1
            if last:
                yield refs["sib_keys"][:BS, cols], refs["sib_values"][:BS, cols], valid
            else:
                yield refs["keys"][after, cols], refs["values"][after, cols], valid
        elif name == "away":
            yield *buffers.away(head, block), self.count(kind, -2) > 0
        elif name == "near":
            count = self.count(kind, 2)
            yield *buffers.near(head, block), count > 0
            if kind == "partner":
                follow = buffers.near_first(head) if last else buffers.near(head, block + 1)
                yield *follow, count > 1
        elif name == "cross":
            count = self.count(kind, -1)
            yield *buffers.major(2, head, block), count > 0
            if kind == "own":
                follow = buffers.cross_first(head) if last else buffers.major(2, head, block + 1)
                yield *follow, count > 1
        elif name == "relay":
            yield *buffers.relay(head, block), self.count(kind, 4) > 0
        elif name == "far":
            yield *buffers.major(4, head, block), self.count(kind, -3) > 0


def state_names(kind, group):
    return "%s%d" % (kind, group), "%s%d_sum" % (kind, group)


def stage_kernel(tasks, names, *refs):
    refs = dict(zip(names, refs))
    stage = Stage(refs)
    items, outs, sums = [], {}, {}
    for kind, group, names, has_prior, packet in tasks:
        state, state_sum = state_names(kind, group)
        query = refs["query" if kind == "own" else "partner_query"]
        rows = query.shape[0]
        blocks = rows // BS
        for place in range(GROUP):
            for block in range(blocks):
                items.append((kind, group, names, has_prior, packet, place, block))
    for at in range(0, len(items), BATCH):
        problems = []
        for kind, group, names, has_prior, packet, place, block in items[at : at + BATCH]:
            head = group * GROUP + place
            mine = slice(block * BS, (block + 1) * BS)
            state, state_sum = state_names(kind, group)
            prior = None
            if has_prior:
                prior = (
                    refs[state + "_in"][mine, head_cols(place)],
                    refs[state_sum + "_in"][mine, place : place + 1],
                )
            parts = [p for n in names for p in stage.parts(kind, n, head, block, blocks)]
            query = refs["query" if kind == "own" else "partner_query"]
            problems.append((query[mine, head_cols(head)], parts, prior))
        for item, (blended, logsum) in zip(items[at : at + BATCH], attend(problems)):
            kind, group, _, _, packet, place, block = item
            mine = slice(block * BS, (block + 1) * BS)
            if packet is None:
                out, lane = refs[state_names(kind, group)[0]], place
                key = state_names(kind, group)[1]
            else:
                key, offset = packet
                lane = offset + place
                out = refs[key]
            out[mine, head_cols(lane)] = blended.astype(out.dtype)
            sums.setdefault(key, {})[lane, block] = logsum
    lanes = lax.broadcasted_iota(jnp.int32, (rows, DH), 1)
    for key, columns in sums.items():
        stats = jnp.zeros((rows, DH), jnp.float32)
        heads = 1 + max(lane for lane, _ in columns)
        for lane in range(heads):
            column = jnp.concatenate([columns[lane, block] for block in range(blocks)], axis=0)
            stats = jnp.where(lanes == lane, column, stats)
        if key.endswith("_sum"):
            refs[key][...] = stats
        else:
            write_stats(refs[key], stats, heads)


def project_kernel(packets, has_base, *refs):
    refs = list(refs)
    packed = []
    for groups in packets:
        owns = [(refs.pop(0), refs.pop(0)) for _ in groups]
        packed.append((owns, refs.pop(0)))
    weights = [refs.pop(0) for groups in packets for _ in groups]
    base = refs.pop(0) if has_base else None
    out, attended = refs

    @pl.when(pl.program_id(0) == 0)
    def _():
        rows = out.shape[0]
        lanes = lax.broadcasted_iota(jnp.int32, (rows, DH), 1)
        at = 0
        for owns, part in packed:
            heads = GROUP * len(owns)
            own_sum = owns[0][1][...]
            for index in range(1, len(owns)):
                shifted = pltpu.roll(owns[index][1][...], index * GROUP, 1)
                own_sum = jnp.where(lanes < index * GROUP, own_sum, shifted)
            part_sum = read_stats(part, heads)
            top = jnp.maximum(own_sum, part_sum)
            own_weight = jnp.exp2(own_sum - top)
            part_weight = jnp.exp2(part_sum - top)
            total = own_weight + part_weight
            own_weight = own_weight / total
            part_weight = part_weight / total
            for place in range(heads):
                own = owns[place // GROUP][0][:, head_cols(place % GROUP)]
                other = part[:rows, head_cols(place)].astype(jnp.float32)
                mixed = (
                    own_weight[:, place : place + 1] * own
                    + part_weight[:, place : place + 1] * other
                )
                attended[:, head_cols(at + place)] = mixed.astype(attended.dtype)
            at += heads

    product = base[...] if has_base else 0.0
    depth = GROUP * DH
    for index, weight in enumerate(weights):
        product = product + jnp.dot(
            attended[:, index * depth : (index + 1) * depth],
            weight[...],
            preferred_element_type=jnp.float32,
        )
    out[...] = product.astype(out.dtype)


def whole(shape):
    return pl.BlockSpec(shape, lambda i: (0,) * len(shape))


def run_stage(name, tasks, values):
    needed = {"table"}
    outs = {}
    work = 0
    rows = values["query"].shape[0]
    for kind, group, parts, has_prior, packet in tasks:
        needed.add("query" if kind == "own" else "partner_query")
        state, state_sum = state_names(kind, group)
        if has_prior:
            needed |= {state + "_in", state_sum + "_in"}
        if packet is None:
            outs[state] = jax.ShapeDtypeStruct((rows, GROUP * DH), jnp.float32)
            outs[state_sum] = jax.ShapeDtypeStruct((rows, DH), jnp.float32)
        else:
            heads = packet[1] + GROUP
            outs[packet[0]] = jax.ShapeDtypeStruct(
                (rows + stat_rows(heads)[1], heads * DH), jnp.bfloat16
            )
        low, high = group * GROUP, (group + 1) * GROUP
        for part in parts:
            work += GROUP * rows * BS * DH * 4
            if part == "local":
                needed |= {"keys", "values", "sib_keys", "sib_values"}
            elif part == "away":
                needed |= {"a1", "b1"} if high <= 6 else {"a3", "b3"}
            elif part == "near":
                needed |= {"a1", "b1"} if high <= 9 else {"a2", "b2"}
                if kind == "partner":
                    needed.add("first1" if high <= 9 else "first2")
            elif part == "cross":
                needed |= {"a2", "b2"} | ({"first2"} if kind == "own" else set())
            elif part == "relay":
                needed |= {"a3", "b3"} if high <= 9 else {"a4", "b4"}
            elif part == "far":
                needed |= {"a4", "b4"}
    names = ["table"] + sorted(needed - {"table"})
    source = {n: values[n[:-3] if n.endswith("_in") else n] for n in names}
    results = pl.pallas_call(
        functools.partial(stage_kernel, tuple(tasks), (*names, *outs)),
        grid=(1,),
        in_specs=[
            pl.BlockSpec(memory_space=pltpu.SMEM) if n == "table" else whole(source[n].shape)
            for n in names
        ],
        out_specs=[whole(s.shape) for s in outs.values()],
        out_shape=list(outs.values()),
        compiler_params=pltpu.CompilerParams(vmem_limit_bytes=40 * MIB),
        cost_estimate=pl.CostEstimate(
            flops=4 * work, bytes_accessed=4 * MIB, transcendentals=work // 256
        ),
        name=name,
    )(*(source[n] for n in names))
    values.update(zip(outs, results))


def tie_kernel(*refs):
    del refs


def tie(before, *payloads):
    anywhere = pl.BlockSpec(memory_space=pl.ANY)
    return pl.pallas_call(
        tie_kernel,
        in_specs=[anywhere] * (len(before) + len(payloads)),
        out_specs=[anywhere] * len(payloads),
        out_shape=[jax.ShapeDtypeStruct(p.shape, p.dtype) for p in payloads],
        input_output_aliases={len(before) + i: i for i in range(len(payloads))},
        name="tie",
    )(*before, *payloads)


def project(packets, values, packet_names, weight, base, dtype):
    rows, columns = values["query"].shape[0], weight.shape[1]
    depth = GROUP * DH
    operands, specs, blocks = [], [], []
    for groups, packet in zip(packets, packet_names):
        for group in groups:
            operands += [values[n] for n in state_names("own", group)]
            blocks.append(
                pl.BlockSpec((depth, TILE), functools.partial(lambda g, i: (g, i), group))
            )
        operands.append(values[packet])
    specs = [whole(x.shape) for x in operands] + blocks
    operands += [weight] * len(blocks)
    if base is not None:
        operands.append(base)
        specs.append(pl.BlockSpec((rows, TILE), lambda i: (0, i)))
    return pl.pallas_call(
        functools.partial(project_kernel, packets, base is not None),
        grid=(columns // TILE,),
        in_specs=specs,
        out_specs=pl.BlockSpec((rows, TILE), lambda i: (0, i)),
        out_shape=jax.ShapeDtypeStruct((rows, columns), dtype),
        scratch_shapes=[pltpu.VMEM((rows, depth * len(blocks)), jnp.bfloat16)],
        compiler_params=pltpu.CompilerParams(vmem_limit_bytes=56 * MIB),
        cost_estimate=pl.CostEstimate(
            flops=2 * rows * depth * len(blocks) * columns,
            bytes_accessed=8 * MIB,
            transcendentals=0,
        ),
        name="merge_and_project",
    )(*operands)


def per_device(queries, key_tokens, value_tokens, radial_table, out_weight):
    frames = lax.axis_size("frame")
    cores = lax.axis_size("head")
    rows = queries.shape[0]
    _, _, pair_is_away = frame_ids()

    def moves(target):
        return [(f, target(f)) for f in range(frames) if 0 <= target(f) < frames]

    partner_moves = moves(lambda f: f ^ 1)
    a_moves = moves(lambda f: f ^ 2)
    b_moves = moves(lambda f: f + 2 if f & 2 else f - 2)
    core_moves = [(c, cores - 1 - c) for c in range(cores)]

    def pack(first, last):
        cols = slice(first * DH, last * DH)
        return jnp.concatenate([key_tokens[:, cols], value_tokens[:, cols]], axis=0)

    def firsts(packed):
        return jnp.concatenate([packed[:BS], packed[rows : rows + BS]], axis=0)

    def choose(first, second):
        return jnp.where(pair_is_away, first, second)

    values = {
        "table": radial_table,
        "query": queries,
        "keys": key_tokens,
        "values": value_tokens,
    }
    cross = lax.ppermute(pack(0, 3), "frame", partner_moves)
    values["a1"] = a1 = lax.ppermute(choose(pack(3, 9), pack(0, 6)), "frame", a_moves)
    values["b1"] = b1 = lax.ppermute(choose(pack(0, 6), pack(3, 9)), "frame", b_moves)
    values["partner_query"] = lax.ppermute(queries, "frame", partner_moves)
    values["sib_keys"] = lax.ppermute(key_tokens, "head", core_moves)
    values["sib_values"] = lax.ppermute(value_tokens, "head", core_moves)
    all_weight = lax.all_gather(out_weight, "head", axis=0, tiled=True)
    run_stage(
        "own_local", [("own", g, ("local",), False, None) for g in range(4)], values
    )
    values["a2"] = a2 = lax.ppermute(choose(pack(9, 12), cross), "frame", a_moves)
    values["b2"] = b2 = lax.ppermute(choose(cross, pack(9, 12)), "frame", b_moves)
    to_a3, to_b3 = tie(
        (values["partner_query"], values["own0_sum"]),
        choose(b1, pack(6, 12)),
        choose(pack(6, 12), a1),
    )
    values["a3"] = lax.ppermute(to_a3, "frame", a_moves)
    values["b3"] = lax.ppermute(to_b3, "frame", b_moves)
    values["first1"] = lax.ppermute(firsts(choose(b1, a1)), "head", core_moves)
    values["first2"] = lax.ppermute(
        firsts(jnp.concatenate([a2, b2], axis=1)), "head", core_moves
    )
    run_stage(
        "partner_local", [("partner", g, ("local",), False, None) for g in range(4)], values
    )
    run_stage(
        "after_step_two",
        [
            ("partner", 0, ("away", "cross"), True, ("low", 0)),
            ("partner", 1, ("near", "away"), True, None),
            ("partner", 2, ("near",), True, None),
            ("partner", 3, ("near",), True, None),
            ("own", 0, ("away", "cross"), True, None),
            ("own", 1, ("near", "away"), True, None),
            ("own", 2, ("near",), True, None),
            ("own", 3, ("near",), True, None),
        ],
        values,
    )
    values["low"] = lax.ppermute(values["low"], "frame", partner_moves)
    to_a4, to_b4 = tie((values["own3_sum"],), b2, a2)
    values["a4"] = lax.ppermute(to_a4, "frame", a_moves)
    values["b4"] = lax.ppermute(to_b4, "frame", b_moves)
    run_stage(
        "after_step_three",
        [
            ("partner", 1, ("relay",), True, ("middle", 0)),
            ("partner", 2, ("away", "relay"), True, ("middle", GROUP)),
        ],
        values,
    )
    values["middle"] = lax.ppermute(values["middle"], "frame", partner_moves)
    run_stage(
        "more_after_step_three",
        [
            ("partner", 3, ("away",), True, None),
            ("own", 2, ("away",), True, None),
            ("own", 3, ("away",), True, None),
        ],
        values,
    )
    run_stage("after_step_four", [("partner", 3, ("relay",), True, ("high", 0))], values)
    values["high"] = lax.ppermute(values["high"], "frame", partner_moves)
    run_stage("more_after_step_four", [("own", 0, ("far",), True, None)], values)
    base = project(((1, 2),), values, ("middle",), all_weight, None, jnp.float32)
    return project(((0,), (3,)), values, ("low", "high"), all_weight, base, jnp.bfloat16)


def solution(mesh):
    in_specs = (
        P(("clip", "frame", "head"), None),
        P(("clip", "frame", "head"), None),
        P(("clip", "frame", "head"), None),
        P(),
        P("head", None),
    )
    out_specs = P(("clip", "frame", "head"), None)
    return jax.shard_map(
        per_device, mesh=mesh, in_specs=in_specs, out_specs=out_specs, check_vma=False
    )
```

```python
import functools
import math

import jax
import jax.numpy as jnp
from jax import lax
from jax.experimental import pallas as pl
from jax.experimental.pallas import tpu as pltpu
from jax.sharding import PartitionSpec as P

DH = 128
BS = 128
GROUP = 3
BATCH = 6
TILE = 768
NEG = -1e30
LOG2_SCALE = math.log2(math.e) / math.sqrt(DH)
MIB = 1024 * 1024


def frame_ids():
    frame = lax.axis_index("frame")
    sign = 1 - 2 * lax.rem(frame, 2)
    pair_is_away = lax.rem(lax.div(frame, 2) + lax.rem(frame, 2), 2) == 1
    return frame, sign, pair_is_away


def entry(table_ref, query_frame, key_frame):
    frames = table_ref.shape[0]
    inside = (key_frame >= 0) & (key_frame < frames)
    count = table_ref[query_frame, jnp.clip(key_frame, 0, frames - 1)]
    return jnp.where(inside, count, 0)


def attend(problems):
    scores = []
    for query, parts in problems:
        keys = jnp.concatenate([k for k, _, _ in parts], axis=0)
        raw = lax.dot_general(
            query, keys, (((1,), (1,)), ((), ())), preferred_element_type=jnp.float32
        )
        pieces, at = [], 0
        for k, _, valid in parts:
            for _ in range(k.shape[0] // BS):
                piece = raw[:, at : at + BS]
                pieces.append(piece if valid is None else jnp.where(valid, piece, NEG))
                at += BS
        scores.append(pieces)
    tops = []
    for pieces in scores:
        best = pieces[0]
        for piece in pieces[1:]:
            best = jnp.maximum(best, piece)
        tops.append(best.max(axis=1, keepdims=True))
    weights, totals = [], []
    for pieces, top in zip(scores, tops):
        row = [jnp.exp2((piece - top) * LOG2_SCALE) for piece in pieces]
        total = row[0]
        for weight in row[1:]:
            total = total + weight
        totals.append(total.sum(axis=1, keepdims=True))
        weights.append(jnp.concatenate([w.astype(jnp.bfloat16) for w in row], axis=1))
    results = []
    for (_, parts), weight, top, total in zip(problems, weights, tops, totals):
        values = jnp.concatenate([v for _, v, _ in parts], axis=0)
        blended = jnp.dot(weight, values, preferred_element_type=jnp.float32)
        results.append((blended * (1.0 / total), top * LOG2_SCALE + jnp.log2(total)))
    return results


def head_cols(head):
    return slice(head * DH, (head + 1) * DH)


def stat_rows(heads):
    return (4, 16) if heads <= 4 else (8, 32)


def write_stats(out, stats, heads):
    pad, count = stat_rows(heads)
    rows = stats.shape[0]
    packed, rest = 0.0, stats
    for part in range(3):
        piece = rest.astype(jnp.bfloat16).astype(jnp.float32)
        rest = rest - piece
        packed = packed + (pltpu.roll(piece, part * pad, 1) if part else piece)
    out[rows:, :] = jnp.zeros((count, out.shape[1]), out.dtype)
    out[rows:, :rows] = packed.T[:count].astype(out.dtype)


def read_stats(ref, heads):
    pad, count = stat_rows(heads)
    rows = ref.shape[0] - count
    packed = ref[rows:, :rows].astype(jnp.float32)
    padding = jnp.zeros((DH - count, rows), jnp.float32)
    packed = jnp.concatenate([packed, padding], axis=0).T
    return packed + pltpu.roll(packed, DH - pad, 1) + pltpu.roll(packed, DH - 2 * pad, 1)


def pair(ref, col, block):
    rows = ref.shape[0] // 2
    cols = head_cols(col)
    return (
        ref[block * BS : (block + 1) * BS, cols],
        ref[rows + block * BS : rows + (block + 1) * BS, cols],
    )


NEAR_STEP = {1: 1, 2: 2, 3: 4}
AWAY_STEP = {0: 3, 1: 1, 2: 4, 3: 6}
RELAY_STEP = {1: 3, 2: 5, 3: 6}
CROSS_STEP = 2
FAR_STEP = 5


class Stage:
    def __init__(self, kind, refs):
        frame, sign, pair_is_away = frame_ids()
        self.kind, self.refs, self.pair_is_away = kind, refs, pair_is_away
        self.sign, self.frame = sign, frame
        self.source = frame if kind == "own" else frame + sign
        self.counts = {}

    def count(self, distance):
        if distance not in self.counts:
            target = self.frame + distance * self.sign
            self.counts[distance] = entry(self.refs["table"], self.source, target)
        return self.counts[distance]

    def choose(self, first, second):
        return tuple(jnp.where(self.pair_is_away, a, b) for a, b in zip(first, second))

    def major(self, step, place, block):
        a, b = self.refs["a%d" % step], self.refs["b%d" % step]
        return self.choose(pair(a, place, block), pair(b, place, block))

    def minor(self, step, place, block):
        a, b = self.refs["a%d" % step], self.refs["b%d" % step]
        return self.choose(pair(b, place, block), pair(a, place, block))

    def near_first(self, group, place):
        if group == 3:
            return pair(self.refs["first4"], place, 0)
        first = self.refs["first2"]
        if group == 1:
            return pair(first, place, 0)
        return self.choose(pair(first, 2 * GROUP + place, 0), pair(first, GROUP + place, 0))

    def cross_first(self, place):
        first = self.refs["first2"]
        return self.choose(pair(first, GROUP + place, 0), pair(first, 2 * GROUP + place, 0))

    def parts(self, group, place, block, blocks):
        refs, own = self.refs, self.kind == "own"
        keys, values = refs["keys:%d" % group], refs["values:%d" % group]
        sib_keys, sib_values = refs["sib_keys:%d" % group], refs["sib_values:%d" % group]
        cols = head_cols(place)
        last = block + 1 == blocks
        if own:
            parts = [
                (keys[:, cols], values[:, cols], None),
                (sib_keys[:, cols], sib_values[:, cols], None),
            ]
        else:
            mine = slice(block * BS, (block + 1) * BS)
            after = slice((block + 1) * BS, (block + 2) * BS)
            valid = self.count(0) > 1
            parts = [(keys[mine, cols], values[mine, cols], None)]
            if last:
                parts.append((sib_keys[:BS, cols], sib_values[:BS, cols], valid))
            else:
                parts.append((keys[after, cols], values[after, cols], valid))
        parts.append((*self.major(AWAY_STEP[group], place, block), self.count(-2) > 0))
        if group == 0:
            count = self.count(-1)
            parts.append((*self.major(CROSS_STEP, place, block), count > 0))
            if own:
                follow = (
                    self.cross_first(place) if last else self.major(CROSS_STEP, place, block + 1)
                )
                parts.append((*follow, count > 1))
                parts.append((*self.major(FAR_STEP, place, block), self.count(-3) > 0))
        else:
            count = self.count(2)
            near = NEAR_STEP[group]
            parts.append((*self.minor(near, place, block), count > 0))
            if not own:
                follow = (
                    self.near_first(group, place) if last else self.minor(near, place, block + 1)
                )
                parts.append((*follow, count > 1))
                parts.append((*self.minor(RELAY_STEP[group], place, block), self.count(4) > 0))
        return parts


def stage_kernel(kind, groups, names, *refs):
    outs = refs[len(names) :]
    refs = dict(zip(names, refs))
    stage = Stage(kind, refs)
    out = outs[0]
    rows = refs["query:%d" % groups[0]].shape[0]
    blocks = rows // BS
    heads = GROUP * len(groups)
    items = [(lane, block) for lane in range(heads) for block in range(blocks)]
    sums = {}
    for at in range(0, len(items), BATCH):
        problems = []
        for lane, block in items[at : at + BATCH]:
            group, place = groups[lane // GROUP], lane % GROUP
            query = refs["query:%d" % group][block * BS : (block + 1) * BS, head_cols(place)]
            problems.append((query, stage.parts(group, place, block, blocks)))
        for (lane, block), (blended, logsum) in zip(items[at : at + BATCH], attend(problems)):
            out[block * BS : (block + 1) * BS, head_cols(lane)] = blended.astype(out.dtype)
            sums[lane, block] = logsum
    lanes = lax.broadcasted_iota(jnp.int32, (rows, DH), 1)
    stats = jnp.zeros((rows, DH), jnp.float32)
    for lane in range(heads):
        column = jnp.concatenate([sums[lane, block] for block in range(blocks)], axis=0)
        stats = jnp.where(lanes == lane, column, stats)
    if kind == "own":
        outs[1][...] = stats
    else:
        write_stats(out, stats, heads)


def whole(shape):
    return pl.BlockSpec(shape, lambda i: (0,) * len(shape))


def run_stage(kind, groups, source):
    rows = source["query"].shape[0]
    heads = GROUP * len(groups)
    names, operands, specs = ["table"], [source["table"]], [pl.BlockSpec(memory_space=pltpu.SMEM)]

    def add(name, value, spec):
        if name not in names:
            names.append(name)
            operands.append(value)
            specs.append(spec)

    def column(name, group, count):
        index = functools.partial(lambda g, i: (0, g), group)
        add("%s:%d" % (name, group), local[name], pl.BlockSpec((count, GROUP * DH), index))

    local = dict(source)
    local["query"] = source["query" if kind == "own" else "partner_query"]
    for group in groups:
        column("query", group, rows)
        column("keys", group, rows)
        column("values", group, rows)
        column("sib_keys", group, rows if kind == "own" else BS)
        column("sib_values", group, rows if kind == "own" else BS)
        steps = [AWAY_STEP[group]]
        firsts = []
        if group == 0:
            steps.append(CROSS_STEP)
            if kind == "own":
                steps.append(FAR_STEP)
                firsts = ["first2"]
        else:
            steps.append(NEAR_STEP[group])
            if kind == "partner":
                steps.append(RELAY_STEP[group])
                firsts = ["first4" if group == 3 else "first2"]
        for name in [side + str(step) for step in steps for side in "ab"] + firsts:
            add(name, source[name], whole(source[name].shape))
    if kind == "own":
        outs = [
            jax.ShapeDtypeStruct((rows, heads * DH), jnp.float32),
            jax.ShapeDtypeStruct((rows, DH), jnp.float32),
        ]
    else:
        outs = [jax.ShapeDtypeStruct((rows + stat_rows(heads)[1], heads * DH), jnp.bfloat16)]
    work = heads * rows * 6 * BS * DH
    return pl.pallas_call(
        functools.partial(stage_kernel, kind, groups, tuple(names)),
        grid=(1,),
        in_specs=specs,
        out_specs=[whole(s.shape) for s in outs],
        out_shape=outs,
        compiler_params=pltpu.CompilerParams(vmem_limit_bytes=24 * MIB),
        cost_estimate=pl.CostEstimate(
            flops=4 * work, bytes_accessed=4 * MIB, transcendentals=work // DH
        ),
        name="%s_%s" % (kind, "_".join(str(g) for g in groups)),
    )(*operands)


def tie_kernel(*refs):
    del refs


def tie(before, *payloads):
    anywhere = pl.BlockSpec(memory_space=pl.ANY)
    return pl.pallas_call(
        tie_kernel,
        in_specs=[anywhere] * (len(before) + len(payloads)),
        out_specs=[anywhere] * len(payloads),
        out_shape=[jax.ShapeDtypeStruct(p.shape, p.dtype) for p in payloads],
        input_output_aliases={len(before) + i: i for i in range(len(payloads))},
        name="tie",
    )(*before, *payloads)


def project_kernel(packets, has_base, *refs):
    refs = list(refs)
    weight = refs.pop(0)
    packed = []
    for groups in packets:
        owns = [(refs.pop(0), refs.pop(0)) for _ in groups]
        packed.append((owns, refs.pop(0)))
    base = refs.pop(0) if has_base else None
    out, attended, buffer, sems = refs
    depth = buffer.shape[0]
    first = min(g for groups in packets for g in groups) * GROUP * DH
    tiles = range(buffer.shape[1] // TILE)
    copies = [
        pltpu.make_async_copy(
            weight.at[first : first + depth, tile * TILE : (tile + 1) * TILE],
            buffer.at[:, tile * TILE : (tile + 1) * TILE],
            sems.at[tile],
        )
        for tile in tiles
    ]
    for copy in copies:
        copy.start()
    rows = out.shape[0]
    lanes = lax.broadcasted_iota(jnp.int32, (rows, DH), 1)
    for groups, (owns, part) in zip(packets, packed):
        heads = GROUP * len(owns)
        own_sum = owns[0][1][...]
        for index in range(1, len(owns)):
            shifted = pltpu.roll(owns[index][1][...], index * GROUP, 1)
            own_sum = jnp.where(lanes < index * GROUP, own_sum, shifted)
        part_sum = read_stats(part, heads)
        top = jnp.maximum(own_sum, part_sum)
        own_weight = jnp.exp2(own_sum - top)
        part_weight = jnp.exp2(part_sum - top)
        inverse = 1.0 / (own_weight + part_weight)
        own_weight = own_weight * inverse
        part_weight = part_weight * inverse
        for place in range(heads):
            own = owns[place // GROUP][0][:, head_cols(place % GROUP)]
            other = part[:rows, head_cols(place)].astype(jnp.float32)
            mixed = (
                own_weight[:, place : place + 1] * own
                + part_weight[:, place : place + 1] * other
            )
            at = groups[place // GROUP] * GROUP + place % GROUP
            cols = slice(at * DH - first, (at + 1) * DH - first)
            attended[:, cols] = mixed.astype(attended.dtype)
    for tile, copy in zip(tiles, copies):
        cols = slice(tile * TILE, (tile + 1) * TILE)
        copy.wait()
        product = jnp.dot(attended[...], buffer[:, cols], preferred_element_type=jnp.float32)
        if has_base:
            product = product + base[:, cols]
        out[:, cols] = product.astype(out.dtype)


def project(packets, owns, parts, weight, base, dtype):
    rows, columns = owns[packets[0][0]][0].shape[0], weight.shape[1]
    depth = GROUP * DH * sum(len(groups) for groups in packets)
    operands = []
    for groups, part in zip(packets, parts):
        for group in groups:
            operands += owns[group]
        operands.append(part)
    if base is not None:
        operands.append(base)
    return pl.pallas_call(
        functools.partial(project_kernel, packets, base is not None),
        grid=(1,),
        in_specs=[pl.BlockSpec(memory_space=pltpu.HBM)] + [whole(x.shape) for x in operands],
        out_specs=whole((rows, columns)),
        out_shape=jax.ShapeDtypeStruct((rows, columns), dtype),
        scratch_shapes=[
            pltpu.VMEM((rows, depth), jnp.bfloat16),
            pltpu.VMEM((depth, columns), jnp.bfloat16),
            pltpu.SemaphoreType.DMA((columns // TILE,)),
        ],
        compiler_params=pltpu.CompilerParams(vmem_limit_bytes=32 * MIB),
        cost_estimate=pl.CostEstimate(
            flops=2 * rows * depth * columns, bytes_accessed=8 * MIB, transcendentals=0
        ),
        name="merge_and_project",
    )(weight, *operands)


def per_device(queries, key_tokens, value_tokens, radial_table, out_weight):
    frames = lax.axis_size("frame")
    cores = lax.axis_size("head")
    rows = queries.shape[0]
    _, _, pair_is_away = frame_ids()

    def moves(target):
        return [(f, target(f)) for f in range(frames) if 0 <= target(f) < frames]

    partner_moves = moves(lambda f: f ^ 1)
    a_moves = moves(lambda f: f ^ 2)
    b_moves = moves(lambda f: f + 2 if f & 2 else f - 2)
    core_moves = [(c, cores - 1 - c) for c in range(cores)]

    def pack(group):
        cols = slice(group * GROUP * DH, (group + 1) * GROUP * DH)
        return jnp.concatenate([key_tokens[:, cols], value_tokens[:, cols]], axis=0)

    def firsts(*packed):
        return jnp.concatenate(
            [
                jnp.concatenate([p[at : at + BS] for p in packed], axis=1)
                for at in (0, rows)
            ],
            axis=0,
        )

    def choose(first, second):
        return jnp.where(pair_is_away, first, second)

    got = {"table": radial_table, "query": queries, "keys": key_tokens, "values": value_tokens}

    def step(number, to_a, to_b):
        got["a%d" % number] = lax.ppermute(to_a, "frame", a_moves)
        got["b%d" % number] = lax.ppermute(to_b, "frame", b_moves)
        return got["a%d" % number], got["b%d" % number]

    a1, b1 = step(1, pack(1), pack(1))
    cross = lax.ppermute(pack(0), "frame", partner_moves)
    got["partner_query"] = lax.ppermute(queries, "frame", partner_moves)
    got["sib_keys"] = lax.ppermute(key_tokens, "head", core_moves)
    got["sib_values"] = lax.ppermute(value_tokens, "head", core_moves)
    all_weight = lax.all_gather(out_weight, "head", axis=0, tiled=True)
    a2, b2 = step(2, choose(pack(2), cross), choose(cross, pack(2)))
    a3, b3 = step(3, choose(b1, pack(0)), choose(pack(0), a1))
    got["first2"] = lax.ppermute(firsts(choose(b1, a1), a2, b2), "head", core_moves)
    own = {1: run_stage("own", (1,), got)}
    to_a4, to_b4 = tie(
        (got["partner_query"], got["sib_keys"], got["sib_values"]),
        choose(pack(3), pack(2)),
        choose(pack(2), pack(3)),
    )
    a4, b4 = step(4, to_a4, to_b4)
    (low,) = run_stage("partner", (0, 1), got)
    step(5, b2, a2)
    got["first4"] = lax.ppermute(firsts(choose(b4, a4)), "head", core_moves)
    to_a6, to_b6 = tie((low, own[1][1]), choose(b4, pack(3)), choose(pack(3), a4))
    low = lax.ppermute(low, "frame", partner_moves)
    step(6, to_a6, to_b6)
    (middle,) = run_stage("partner", (2,), got)
    middle = lax.ppermute(middle, "frame", partner_moves)
    own[0] = run_stage("own", (0,), got)
    own[2] = run_stage("own", (2,), got)
    (high,) = run_stage("partner", (3,), got)
    high = lax.ppermute(high, "frame", partner_moves)
    own[3] = run_stage("own", (3,), got)
    base = project(((0, 1), (2,)), own, (low, middle), all_weight, None, jnp.float32)
    return project(((3,),), own, (high,), all_weight, base, jnp.bfloat16)


def solution(mesh):
    in_specs = (
        P(("clip", "frame", "head"), None),
        P(("clip", "frame", "head"), None),
        P(("clip", "frame", "head"), None),
        P(),
        P("head", None),
    )
    out_specs = P(("clip", "frame", "head"), None)
    return jax.shard_map(
        per_device, mesh=mesh, in_specs=in_specs, out_specs=out_specs, check_vma=False
    )
```

```python
import functools
import math

import jax
import jax.numpy as jnp
from jax import lax
from jax.experimental import pallas as pl
from jax.experimental.pallas import tpu as pltpu
from jax.sharding import PartitionSpec as P

DH = 128
BS = 128
CROSS = 3
BATCH = 6
TILE = 768
NEG = -1e30
LOG2_SCALE = math.log2(math.e) / math.sqrt(DH)
MIB = 1024 * 1024


def frame_ids():
    frame = lax.axis_index("frame")
    sign = 1 - 2 * lax.rem(frame, 2)
    pair_is_away = lax.rem(lax.div(frame, 2) + lax.rem(frame, 2), 2) == 1
    return frame, sign, pair_is_away


def entry(table_ref, query_frame, key_frame):
    frames = table_ref.shape[0]
    inside = (key_frame >= 0) & (key_frame < frames)
    count = table_ref[query_frame, jnp.clip(key_frame, 0, frames - 1)]
    return jnp.where(inside, count, 0)


def attend(problems):
    scores = []
    for query, parts in problems:
        keys = jnp.concatenate([k for k, _, _ in parts], axis=0)
        raw = lax.dot_general(
            query, keys, (((1,), (1,)), ((), ())), preferred_element_type=jnp.float32
        )
        pieces, at = [], 0
        for k, _, valid in parts:
            for _ in range(k.shape[0] // BS):
                piece = raw[:, at : at + BS]
                pieces.append(piece if valid is None else jnp.where(valid, piece, NEG))
                at += BS
        scores.append(pieces)
    tops = []
    for pieces in scores:
        best = pieces[0]
        for piece in pieces[1:]:
            best = jnp.maximum(best, piece)
        tops.append(best.max(axis=1, keepdims=True))
    weights, totals = [], []
    for pieces, top in zip(scores, tops):
        row = [jnp.exp2((piece - top) * LOG2_SCALE) for piece in pieces]
        total = row[0]
        for weight in row[1:]:
            total = total + weight
        totals.append(total.sum(axis=1, keepdims=True))
        weights.append(jnp.concatenate([w.astype(jnp.bfloat16) for w in row], axis=1))
    results = []
    for (_, parts), weight, top, total in zip(problems, weights, tops, totals):
        values = jnp.concatenate([v for _, v, _ in parts], axis=0)
        blended = jnp.dot(weight, values, preferred_element_type=jnp.float32)
        results.append((blended * (1.0 / total), top * LOG2_SCALE + jnp.log2(total)))
    return results


def attend_heads(group, blocks, problem, out):
    rows = blocks * BS
    heads = range(*group)
    lanes = lax.broadcasted_iota(jnp.int32, (rows, DH), 1)
    stats = jnp.zeros((rows, DH), jnp.float32)
    items = [(place, head, block) for place, head in enumerate(heads) for block in range(blocks)]
    sums = {}
    for at in range(0, len(items), BATCH):
        chunk = items[at : at + BATCH]
        results = attend([problem(head, block) for _, head, block in chunk])
        for (place, head, block), (blended, logsum) in zip(chunk, results):
            out[block * BS : (block + 1) * BS, head_cols(place)] = blended.astype(out.dtype)
            sums[place, block] = logsum
    for place in range(len(heads)):
        column = jnp.concatenate([sums[place, block] for block in range(blocks)], axis=0)
        stats = jnp.where(lanes == place, column, stats)
    return stats


def head_cols(head):
    return slice(head * DH, (head + 1) * DH)


def stat_rows(heads):
    return (4, 16) if heads <= 4 else (8, 32)


def write_stats(out, stats, heads):
    pad, count = stat_rows(heads)
    rows = stats.shape[0]
    packed, rest = 0.0, stats
    for part in range(3):
        piece = rest.astype(jnp.bfloat16).astype(jnp.float32)
        rest = rest - piece
        packed = packed + (pltpu.roll(piece, part * pad, 1) if part else piece)
    out[rows:, :] = jnp.zeros((count, out.shape[1]), out.dtype)
    out[rows:, :rows] = packed.T[:count].astype(out.dtype)


def read_stats(ref, heads):
    pad, count = stat_rows(heads)
    rows = ref.shape[0] - count
    packed = ref[rows:, :rows].astype(jnp.float32)
    padding = jnp.zeros((DH - count, rows), jnp.float32)
    packed = jnp.concatenate([packed, padding], axis=0).T
    return packed + pltpu.roll(packed, DH - pad, 1) + pltpu.roll(packed, DH - 2 * pad, 1)


def pair(ref, col, block):
    rows = ref.shape[0] // 2
    cols = head_cols(col)
    return (
        ref[block * BS : (block + 1) * BS, cols],
        ref[rows + block * BS : rows + (block + 1) * BS, cols],
    )


class Buffers:
    def __init__(self, refs, pair_is_away):
        self.refs = refs
        self.pair_is_away = pair_is_away

    def choose(self, first, second):
        return tuple(jnp.where(self.pair_is_away, a, b) for a, b in zip(first, second))

    def major(self, step, col, block):
        a, b = self.refs["a%d" % step], self.refs["b%d" % step]
        return self.choose(pair(a, col, block), pair(b, col, block))

    def minor(self, step, col, block):
        a, b = self.refs["a%d" % step], self.refs["b%d" % step]
        return self.choose(pair(b, col, block), pair(a, col, block))

    def away(self, head, block):
        return self.major(1, head, block) if head < 6 else self.major(3, head - 6, block)

    def near(self, head, block):
        return self.minor(1, head - 3, block) if head < 9 else self.minor(2, head - 9, block)

    def near_first(self, head):
        if head < 9:
            return pair(self.refs["first1"], head - 3, 0)
        first = self.refs["first2"]
        return self.choose(pair(first, CROSS + head - 9, 0), pair(first, head - 9, 0))

    def cross_first(self, head):
        first = self.refs["first2"]
        return self.choose(pair(first, head, 0), pair(first, CROSS + head, 0))

    def relay(self, head, block):
        return self.minor(3, head - 3, block) if head < 9 else self.minor(4, head - 9, block)


def partner_kernel(group, names, table_ref, query, keys, values, sib_keys, sib_values, *rest):
    frame, sign, pair_is_away = frame_ids()
    buffers = Buffers(dict(zip(names, rest)), pair_is_away)
    out = rest[-1]
    rows = query.shape[0]
    blocks = rows // BS
    partner = frame + sign
    own_count = entry(table_ref, partner, frame)
    near_count = entry(table_ref, partner, frame + 2 * sign)
    away_valid = entry(table_ref, partner, frame - 2 * sign) > 0
    relay_valid = entry(table_ref, partner, frame + 4 * sign) > 0
    cross_valid = entry(table_ref, partner, frame - sign) > 0

    def problem(head, block):
        mine = slice(block * BS, (block + 1) * BS)
        cols = head_cols(head)
        last = block + 1 == blocks
        parts = [(keys[mine, cols], values[mine, cols], None)]
        if last:
            parts.append((sib_keys[:BS, cols], sib_values[:BS, cols], own_count > 1))
        else:
            after = slice((block + 1) * BS, (block + 2) * BS)
            parts.append((keys[after, cols], values[after, cols], own_count > 1))
        parts.append((*buffers.away(head, block), away_valid))
        if head < CROSS:
            parts.append((*buffers.major(2, head, block), cross_valid))
        else:
            parts.append((*buffers.near(head, block), near_count > 0))
            after = buffers.near_first(head) if last else buffers.near(head, block + 1)
            parts.append((*after, near_count > 1))
            parts.append((*buffers.relay(head, block), relay_valid))
        return query[mine, cols], parts

    stats = attend_heads(group, blocks, problem, out)
    write_stats(out, stats, group[1] - group[0])


def own_kernel(group, names, table_ref, query, keys, values, sib_keys, sib_values, *rest):
    frame, sign, pair_is_away = frame_ids()
    buffers = Buffers(dict(zip(names, rest)), pair_is_away)
    out, out_stats = rest[-2:]
    rows = query.shape[0]
    blocks = rows // BS
    near_valid = entry(table_ref, frame, frame + 2 * sign) > 0
    away_valid = entry(table_ref, frame, frame - 2 * sign) > 0
    cross_count = entry(table_ref, frame, frame - sign)
    far_valid = entry(table_ref, frame, frame - 3 * sign) > 0

    def problem(head, block):
        mine = slice(block * BS, (block + 1) * BS)
        cols = head_cols(head)
        parts = [
            (keys[:, cols], values[:, cols], None),
            (sib_keys[:, cols], sib_values[:, cols], None),
            (*buffers.away(head, block), away_valid),
        ]
        if head < CROSS:
            last = block + 1 == blocks
            parts.append((*buffers.major(2, head, block), cross_count > 0))
            after = buffers.cross_first(head) if last else buffers.major(2, head, block + 1)
            parts.append((*after, cross_count > 1))
            parts.append((*buffers.major(4, head, block), far_valid))
        else:
            parts.append((*buffers.near(head, block), near_valid))
        return query[mine, cols], parts

    out_stats[...] = attend_heads(group, blocks, problem, out)


def project_kernel(own_groups, part_groups, *refs):
    refs = list(refs)
    weight = refs.pop(0)
    owns = [(group, refs.pop(0), refs.pop(0)) for group in own_groups]
    parts = [(group, refs.pop(0)) for group in part_groups]
    out, attended = refs
    rows = out.shape[0]
    lanes = lax.broadcasted_iota(jnp.int32, (rows, DH), 1)
    own_at, part_at = {}, {}
    own_sum = part_sum = jnp.zeros((rows, DH), jnp.float32)
    for (first, last), own, stats in owns:
        shifted = pltpu.roll(stats[...], first, 1) if first else stats[...]
        own_sum = jnp.where((lanes >= first) & (lanes < last), shifted, own_sum)
        own_at.update({head: (own, head - first) for head in range(first, last)})
    for (first, last), part in parts:
        stats = read_stats(part, last - first)
        shifted = pltpu.roll(stats, first, 1) if first else stats
        part_sum = jnp.where((lanes >= first) & (lanes < last), shifted, part_sum)
        part_at.update({head: (part, head - first) for head in range(first, last)})
    top = jnp.maximum(own_sum, part_sum)
    own_weight = jnp.exp2(own_sum - top)
    part_weight = jnp.exp2(part_sum - top)
    inverse = 1.0 / (own_weight + part_weight)
    own_weight = own_weight * inverse
    part_weight = part_weight * inverse
    for head in sorted(own_at):
        own, own_place = own_at[head]
        part, part_place = part_at[head]
        mixed = own_weight[:, head : head + 1] * own[:, head_cols(own_place)] + part_weight[
            :, head : head + 1
        ] * part[:rows, head_cols(part_place)].astype(jnp.float32)
        attended[:, head_cols(head)] = mixed.astype(attended.dtype)
    for at in range(0, out.shape[1], TILE):
        out[:, at : at + TILE] = jnp.dot(
            attended[...], weight[:, at : at + TILE], preferred_element_type=jnp.float32
        ).astype(out.dtype)


def run(body, name, table, operands, out_shapes, flops, after=()):
    in_vmem = pl.BlockSpec(memory_space=pltpu.VMEM)
    return pl.pallas_call(
        body,
        in_specs=[pl.BlockSpec(memory_space=pltpu.SMEM)]
        + [in_vmem] * len(operands)
        + [pl.BlockSpec(memory_space=pl.ANY)] * len(after),
        out_specs=[in_vmem] * len(out_shapes),
        out_shape=out_shapes,
        compiler_params=pltpu.CompilerParams(vmem_limit_bytes=24 * MIB),
        cost_estimate=pl.CostEstimate(
            flops=flops, bytes_accessed=MIB, transcendentals=flops // 512
        ),
        name=name,
    )(table, *operands, *after)


def tie_kernel(*refs):
    del refs


def tie(before, *payloads):
    anywhere = pl.BlockSpec(memory_space=pl.ANY)
    return pl.pallas_call(
        tie_kernel,
        in_specs=[anywhere] * (len(before) + len(payloads)),
        out_specs=[anywhere] * len(payloads),
        out_shape=[jax.ShapeDtypeStruct(p.shape, p.dtype) for p in payloads],
        input_output_aliases={len(before) + i: i for i in range(len(payloads))},
        name="tie",
    )(*before, *payloads)


def project(own_groups, part_groups, weight, operands):
    in_vmem = pl.BlockSpec(memory_space=pltpu.VMEM)
    rows = operands[0].shape[0]
    depth, columns = weight.shape
    return pl.pallas_call(
        functools.partial(project_kernel, own_groups, part_groups),
        in_specs=[in_vmem] * (1 + len(operands)),
        out_specs=in_vmem,
        out_shape=jax.ShapeDtypeStruct((rows, columns), jnp.bfloat16),
        scratch_shapes=[pltpu.VMEM((rows, depth), jnp.bfloat16)],
        compiler_params=pltpu.CompilerParams(vmem_limit_bytes=24 * MIB),
        cost_estimate=pl.CostEstimate(
            flops=2 * rows * depth * columns, bytes_accessed=12 * MIB, transcendentals=0
        ),
        name="merge_and_project",
    )(weight, *operands)


def per_device(queries, key_tokens, value_tokens, radial_table, out_weight):
    frames = lax.axis_size("frame")
    cores = lax.axis_size("head")
    rows = queries.shape[0]
    _, _, pair_is_away = frame_ids()

    def moves(target):
        return [(f, target(f)) for f in range(frames) if 0 <= target(f) < frames]

    partner_moves = moves(lambda f: f ^ 1)
    a_moves = moves(lambda f: f ^ 2)
    b_moves = moves(lambda f: f + 2 if f & 2 else f - 2)
    core_moves = [(c, cores - 1 - c) for c in range(cores)]

    def pack(first, last):
        cols = slice(first * DH, last * DH)
        return jnp.concatenate([key_tokens[:, cols], value_tokens[:, cols]], axis=0)

    def firsts(packed):
        return jnp.concatenate([packed[:BS], packed[rows : rows + BS]], axis=0)

    def choose(first, second):
        return jnp.where(pair_is_away, first, second)

    cross = lax.ppermute(pack(0, 3), "frame", partner_moves)
    a1 = lax.ppermute(choose(pack(3, 9), pack(0, 6)), "frame", a_moves)
    b1 = lax.ppermute(choose(pack(0, 6), pack(3, 9)), "frame", b_moves)
    partner_query = lax.ppermute(queries, "frame", partner_moves)
    sib_keys = lax.ppermute(key_tokens, "head", core_moves)
    sib_values = lax.ppermute(value_tokens, "head", core_moves)
    all_weight = lax.all_gather(out_weight, "head", axis=0, tiled=True)
    to_a2, to_b2 = tie(
        (sib_keys, sib_values), choose(pack(9, 12), cross), choose(cross, pack(9, 12))
    )
    a2 = lax.ppermute(to_a2, "frame", a_moves)
    b2 = lax.ppermute(to_b2, "frame", b_moves)
    a3 = lax.ppermute(choose(b1, pack(6, 12)), "frame", a_moves)
    b3 = lax.ppermute(choose(pack(6, 12), a1), "frame", b_moves)
    first1 = lax.ppermute(firsts(choose(b1, a1)), "head", core_moves)
    first2 = lax.ppermute(firsts(jnp.concatenate([a2, b2], axis=1)), "head", core_moves)
    refs = {"a1": a1, "a2": a2, "a3": a3, "b1": b1, "b2": b2, "b3": b3}
    refs.update({"first1": first1, "first2": first2})
    local = (key_tokens, value_tokens, sib_keys, sib_values)

    def partner_part(group, names, after=()):
        heads = group[1] - group[0]
        shape = jax.ShapeDtypeStruct((rows + stat_rows(heads)[1], heads * DH), jnp.bfloat16)
        (part,) = run(
            functools.partial(partner_kernel, group, names),
            "partner_part",
            radial_table,
            (partner_query, *local, *(refs[n] for n in names)),
            [shape],
            heads * rows * 6 * BS * DH * 4,
            after,
        )
        return part

    def own_part(group, names):
        heads = group[1] - group[0]
        return run(
            functools.partial(own_kernel, group, names),
            "own_part",
            radial_table,
            (queries, *local, *(refs[n] for n in names)),
            [
                jax.ShapeDtypeStruct((rows, heads * DH), jnp.float32),
                jax.ShapeDtypeStruct((rows, DH), jnp.float32),
            ],
            heads * rows * 6 * BS * DH * 4,
        )

    own_groups = ((0, 3), (3, 6), (6, 12))
    part_groups = ((0, 3), (3, 9), (9, 12))
    part_low = partner_part((0, 3), ("a1", "b1", "a2", "b2"), (all_weight[:16, :DH],))
    own_early = own_part((3, 6), ("a1", "b1"))
    to_a4, to_b4 = tie((part_low, own_early[1]), b2, a2)
    part_low = lax.ppermute(part_low, "frame", partner_moves)
    refs["a4"] = lax.ppermute(to_a4, "frame", a_moves)
    refs["b4"] = lax.ppermute(to_b4, "frame", b_moves)
    part_middle = partner_part((3, 9), ("a1", "b1", "a3", "b3", "first1"))
    part_middle = lax.ppermute(part_middle, "frame", partner_moves)
    own_late = own_part((6, 12), ("a1", "b1", "a2", "b2", "a3", "b3"))
    part_high = partner_part(
        (9, 12), ("a2", "b2", "a3", "b3", "a4", "b4", "first2"), (own_late[1],)
    )
    part_high = lax.ppermute(part_high, "frame", partner_moves)
    own_low = own_part((0, 3), ("a1", "b1", "a2", "b2", "a4", "b4", "first2"))
    return project(
        own_groups,
        part_groups,
        all_weight,
        (*own_low, *own_early, *own_late, part_low, part_middle, part_high),
    )


def solution(mesh):
    in_specs = (
        P(("clip", "frame", "head"), None),
        P(("clip", "frame", "head"), None),
        P(("clip", "frame", "head"), None),
        P(),
        P("head", None),
    )
    out_specs = P(("clip", "frame", "head"), None)
    return jax.shard_map(
        per_device, mesh=mesh, in_specs=in_specs, out_specs=out_specs, check_vma=False
    )
```

```python
import functools
import math

import jax
import jax.numpy as jnp
from jax import lax
from jax.experimental import pallas as pl
from jax.experimental.pallas import tpu as pltpu
from jax.sharding import PartitionSpec as P

DH = 128
BS = 128
CROSS = 3
BATCH = 4
TILE = 768
NEG = -1e30
LOG2_SCALE = math.log2(math.e) / math.sqrt(DH)
MIB = 1024 * 1024


def frame_ids():
    frame = lax.axis_index("frame")
    return frame, 1 - 2 * lax.rem(frame, 2)


def entry(table_ref, query_frame, key_frame):
    frames = table_ref.shape[0]
    inside = (key_frame >= 0) & (key_frame < frames)
    count = table_ref[query_frame, jnp.clip(key_frame, 0, frames - 1)]
    return jnp.where(inside, count, 0)


def attend(problems):
    scores = []
    for query, parts in problems:
        row = []
        for keys, _, valid in parts:
            raw = lax.dot_general(
                query, keys, (((1,), (1,)), ((), ())), preferred_element_type=jnp.float32
            )
            row.append(raw if valid is None else jnp.where(valid, raw, NEG))
        scores.append(row)
    tops = []
    for row in scores:
        best = None
        for raw in row:
            for at in range(0, raw.shape[1], BS):
                piece = raw[:, at : at + BS]
                best = piece if best is None else jnp.maximum(best, piece)
        tops.append(best.max(axis=1, keepdims=True))
    weights = [
        [jnp.exp2((raw - top) * LOG2_SCALE) for raw in row] for row, top in zip(scores, tops)
    ]
    totals = []
    for row in weights:
        total = None
        for weight in row:
            for at in range(0, weight.shape[1], BS):
                piece = weight[:, at : at + BS]
                total = piece if total is None else total + piece
        totals.append(total.sum(axis=1, keepdims=True))
    results = []
    for (_, parts), row, top, total in zip(problems, weights, tops, totals):
        blended = 0.0
        for (_, values, _), weight in zip(parts, row):
            blended = blended + jnp.dot(
                weight.astype(jnp.bfloat16), values, preferred_element_type=jnp.float32
            )
        results.append((blended / total, top * LOG2_SCALE + jnp.log2(total)))
    return results


def attend_heads(group, blocks, problem, out):
    rows = blocks * BS
    heads = range(*group)
    lanes = lax.broadcasted_iota(jnp.int32, (rows, DH), 1)
    stats = jnp.zeros((rows, DH), jnp.float32)
    items = [(place, head, block) for place, head in enumerate(heads) for block in range(blocks)]
    sums = {}
    for at in range(0, len(items), BATCH):
        chunk = items[at : at + BATCH]
        results = attend([problem(head, block) for _, head, block in chunk])
        for (place, head, block), (blended, logsum) in zip(chunk, results):
            out[block * BS : (block + 1) * BS, head_cols(place)] = blended.astype(out.dtype)
            sums[place, block] = logsum
    for place in range(len(heads)):
        column = jnp.concatenate([sums[place, block] for block in range(blocks)], axis=0)
        stats = jnp.where(lanes == place, column, stats)
    return stats


def head_cols(head):
    return slice(head * DH, (head + 1) * DH)


def stat_rows(heads):
    return (4, 16) if heads <= 4 else (8, 32)


def write_stats(out, stats, heads):
    pad, count = stat_rows(heads)
    rows = stats.shape[0]
    packed, rest = 0.0, stats
    for part in range(3):
        piece = rest.astype(jnp.bfloat16).astype(jnp.float32)
        rest = rest - piece
        packed = packed + (pltpu.roll(piece, part * pad, 1) if part else piece)
    out[rows:, :] = jnp.zeros((count, out.shape[1]), out.dtype)
    out[rows:, :rows] = packed.T[:count].astype(out.dtype)


def read_stats(ref, heads):
    pad, count = stat_rows(heads)
    rows = ref.shape[0] - count
    packed = ref[rows:, :rows].astype(jnp.float32)
    padding = jnp.zeros((DH - count, rows), jnp.float32)
    packed = jnp.concatenate([packed, padding], axis=0).T
    return packed + pltpu.roll(packed, DH - pad, 1) + pltpu.roll(packed, DH - 2 * pad, 1)


def pair(ref, col, block):
    rows = ref.shape[0] // 2
    cols = head_cols(col)
    return (
        ref[block * BS : (block + 1) * BS, cols],
        ref[rows + block * BS : rows + (block + 1) * BS, cols],
    )


class Buffers:
    def __init__(self, refs):
        self.refs = refs

    def cross(self, head, block):
        return pair(self.refs["major2"], head, block)

    def far(self, head, block):
        return pair(self.refs["major4"], head, block)

    def away(self, head, block):
        if head < 6:
            return pair(self.refs["major1"], head, block)
        return pair(self.refs["major3"], head - 6, block)

    def near(self, head, block):
        if head < 9:
            return pair(self.refs["minor1"], head - 3, block)
        return pair(self.refs["minor2"], head - 9, block)

    def near_first(self, head):
        if head < 9:
            return pair(self.refs["first1"], head - 3, 0)
        return pair(self.refs["first2"], head - 9, 0)

    def cross_first(self, head):
        return pair(self.refs["first2"], CROSS + head, 0)

    def relay(self, head, block):
        if head < 9:
            return pair(self.refs["minor3"], head - 3, block)
        return pair(self.refs["minor4"], head - 9, block)


def partner_kernel(group, names, table_ref, query, keys, values, sib_keys, sib_values, *rest):
    frame, sign = frame_ids()
    buffers = Buffers(dict(zip(names, rest)))
    out = rest[-1]
    rows = query.shape[0]
    blocks = rows // BS
    partner = frame + sign
    own_count = entry(table_ref, partner, frame)
    near_count = entry(table_ref, partner, frame + 2 * sign)
    away_valid = entry(table_ref, partner, frame - 2 * sign) > 0
    relay_valid = entry(table_ref, partner, frame + 4 * sign) > 0
    cross_valid = entry(table_ref, partner, frame - sign) > 0

    def problem(head, block):
        mine = slice(block * BS, (block + 1) * BS)
        cols = head_cols(head)
        last = block + 1 == blocks
        parts = [(keys[mine, cols], values[mine, cols], None)]
        if last:
            parts.append((sib_keys[:BS, cols], sib_values[:BS, cols], own_count > 1))
        else:
            after = slice((block + 1) * BS, (block + 2) * BS)
            parts.append((keys[after, cols], values[after, cols], own_count > 1))
        parts.append((*buffers.away(head, block), away_valid))
        if head < CROSS:
            parts.append((*buffers.cross(head, block), cross_valid))
        else:
            parts.append((*buffers.near(head, block), near_count > 0))
            after = buffers.near_first(head) if last else buffers.near(head, block + 1)
            parts.append((*after, near_count > 1))
            parts.append((*buffers.relay(head, block), relay_valid))
        return query[mine, cols], parts

    stats = attend_heads(group, blocks, problem, out)
    write_stats(out, stats, group[1] - group[0])


def own_kernel(group, names, table_ref, query, keys, values, sib_keys, sib_values, *rest):
    frame, sign = frame_ids()
    buffers = Buffers(dict(zip(names, rest)))
    out, out_stats = rest[-2:]
    rows = query.shape[0]
    blocks = rows // BS
    near_valid = entry(table_ref, frame, frame + 2 * sign) > 0
    away_valid = entry(table_ref, frame, frame - 2 * sign) > 0
    cross_count = entry(table_ref, frame, frame - sign)
    far_valid = entry(table_ref, frame, frame - 3 * sign) > 0

    def problem(head, block):
        mine = slice(block * BS, (block + 1) * BS)
        cols = head_cols(head)
        parts = [
            (keys[:, cols], values[:, cols], None),
            (sib_keys[:, cols], sib_values[:, cols], None),
            (*buffers.away(head, block), away_valid),
        ]
        if head < CROSS:
            last = block + 1 == blocks
            parts.append((*buffers.cross(head, block), cross_count > 0))
            after = buffers.cross_first(head) if last else buffers.cross(head, block + 1)
            parts.append((*after, cross_count > 1))
            parts.append((*buffers.far(head, block), far_valid))
        else:
            parts.append((*buffers.near(head, block), near_valid))
        return query[mine, cols], parts

    out_stats[...] = attend_heads(group, blocks, problem, out)


def project_kernel(own_groups, part_groups, *refs):
    refs = list(refs)
    weight = refs.pop(0)
    owns = [(group, refs.pop(0), refs.pop(0)) for group in own_groups]
    parts = [(group, refs.pop(0)) for group in part_groups]
    out, attended = refs
    rows = out.shape[0]
    lanes = lax.broadcasted_iota(jnp.int32, (rows, DH), 1)
    own_at, part_at = {}, {}
    own_sum = part_sum = jnp.zeros((rows, DH), jnp.float32)
    for (first, last), own, stats in owns:
        shifted = pltpu.roll(stats[...], first, 1) if first else stats[...]
        own_sum = jnp.where((lanes >= first) & (lanes < last), shifted, own_sum)
        own_at.update({head: (own, head - first) for head in range(first, last)})
    for (first, last), part in parts:
        stats = read_stats(part, last - first)
        shifted = pltpu.roll(stats, first, 1) if first else stats
        part_sum = jnp.where((lanes >= first) & (lanes < last), shifted, part_sum)
        part_at.update({head: (part, head - first) for head in range(first, last)})
    top = jnp.maximum(own_sum, part_sum)
    own_weight = jnp.exp2(own_sum - top)
    part_weight = jnp.exp2(part_sum - top)
    inverse = 1.0 / (own_weight + part_weight)
    own_weight = own_weight * inverse
    part_weight = part_weight * inverse
    for head in sorted(own_at):
        own, own_place = own_at[head]
        part, part_place = part_at[head]
        mixed = own_weight[:, head : head + 1] * own[:, head_cols(own_place)] + part_weight[
            :, head : head + 1
        ] * part[:rows, head_cols(part_place)].astype(jnp.float32)
        attended[:, head_cols(head)] = mixed.astype(attended.dtype)
    for at in range(0, out.shape[1], TILE):
        out[:, at : at + TILE] = jnp.dot(
            attended[...], weight[:, at : at + TILE], preferred_element_type=jnp.float32
        ).astype(out.dtype)


def whole(shape):
    return pl.BlockSpec(shape, lambda i: (0,) * len(shape))


def run(body, name, table, operands, out_shapes, flops, after=()):
    return pl.pallas_call(
        body,
        grid=(1,),
        in_specs=[pl.BlockSpec(memory_space=pltpu.SMEM)]
        + [whole(x.shape) for x in operands]
        + [pl.BlockSpec(memory_space=pl.ANY)] * len(after),
        out_specs=[whole(s.shape) for s in out_shapes],
        out_shape=out_shapes,
        compiler_params=pltpu.CompilerParams(vmem_limit_bytes=24 * MIB),
        cost_estimate=pl.CostEstimate(
            flops=flops, bytes_accessed=MIB, transcendentals=flops // 512
        ),
        name=name,
    )(table, *operands, *after)


def tie_kernel(*refs):
    del refs


def tie(before, *payloads):
    anywhere = pl.BlockSpec(memory_space=pl.ANY)
    return pl.pallas_call(
        tie_kernel,
        in_specs=[anywhere] * (len(before) + len(payloads)),
        out_specs=[anywhere] * len(payloads),
        out_shape=[jax.ShapeDtypeStruct(p.shape, p.dtype) for p in payloads],
        input_output_aliases={len(before) + i: i for i in range(len(payloads))},
        name="tie",
    )(*before, *payloads)


def project(own_groups, part_groups, weight, operands):
    rows = operands[0].shape[0]
    depth, columns = weight.shape
    return pl.pallas_call(
        functools.partial(project_kernel, own_groups, part_groups),
        grid=(1,),
        in_specs=[whole(x.shape) for x in (weight, *operands)],
        out_specs=whole((rows, columns)),
        out_shape=jax.ShapeDtypeStruct((rows, columns), jnp.bfloat16),
        scratch_shapes=[pltpu.VMEM((rows, depth), jnp.bfloat16)],
        compiler_params=pltpu.CompilerParams(vmem_limit_bytes=24 * MIB),
        cost_estimate=pl.CostEstimate(
            flops=2 * rows * depth * columns, bytes_accessed=12 * MIB, transcendentals=0
        ),
        name="merge_and_project",
    )(weight, *operands)


def per_device(queries, key_tokens, value_tokens, radial_table, out_weight):
    frames = lax.axis_size("frame")
    cores = lax.axis_size("head")
    rows = queries.shape[0]

    def moves(target):
        return [(f, target(f)) for f in range(frames) if 0 <= target(f) < frames]

    partner_moves = moves(lambda f: f ^ 1)
    near_moves = moves(lambda f: f - 2 if f % 2 == 0 else f + 2)
    away_moves = moves(lambda f: f + 2 if f % 2 == 0 else f - 2)
    core_moves = [(c, cores - 1 - c) for c in range(cores)]

    def pack(first, last):
        cols = slice(first * DH, last * DH)
        return jnp.concatenate([key_tokens[:, cols], value_tokens[:, cols]], axis=0)

    def firsts(*packed):
        return jnp.concatenate(
            [jnp.concatenate([p[at : at + BS] for p in packed], axis=1) for at in (0, rows)],
            axis=0,
        )

    cross = lax.ppermute(pack(0, 3), "frame", partner_moves)
    major1 = lax.ppermute(pack(0, 6), "frame", away_moves)
    minor1 = lax.ppermute(pack(3, 9), "frame", near_moves)
    sib_keys = lax.ppermute(key_tokens, "head", core_moves)
    sib_values = lax.ppermute(value_tokens, "head", core_moves)
    partner_query = lax.ppermute(queries, "frame", partner_moves)
    all_weight = lax.all_gather(out_weight, "head", axis=0, tiled=True)
    cross, to_minor2 = tie((sib_keys, sib_values), cross, pack(9, 12))
    minor2 = lax.ppermute(to_minor2, "frame", near_moves)
    major2 = lax.ppermute(cross, "frame", away_moves)
    (to_major3,) = tie((major1,), pack(6, 12))
    major3 = lax.ppermute(to_major3, "frame", away_moves)
    minor3 = lax.ppermute(minor1, "frame", near_moves)
    first1 = lax.ppermute(firsts(minor1), "head", core_moves)
    major4 = lax.ppermute(major2, "frame", away_moves)
    minor4 = lax.ppermute(minor2, "frame", near_moves)
    first2 = lax.ppermute(firsts(minor2, major2), "head", core_moves)
    refs = {
        "major1": major1,
        "major2": major2,
        "major3": major3,
        "major4": major4,
        "minor1": minor1,
        "minor2": minor2,
        "minor3": minor3,
        "minor4": minor4,
        "first1": first1,
        "first2": first2,
    }
    local = (key_tokens, value_tokens, sib_keys, sib_values)

    def partner_part(group, names, after=()):
        heads = group[1] - group[0]
        shape = jax.ShapeDtypeStruct((rows + stat_rows(heads)[1], heads * DH), jnp.bfloat16)
        (part,) = run(
            functools.partial(partner_kernel, group, names),
            "partner_part",
            radial_table,
            (partner_query, *local, *(refs[n] for n in names)),
            [shape],
            heads * rows * 6 * BS * DH * 4,
            after,
        )
        return part

    def own_part(group, names, after=()):
        heads = group[1] - group[0]
        return run(
            functools.partial(own_kernel, group, names),
            "own_part",
            radial_table,
            (queries, *local, *(refs[n] for n in names)),
            [
                jax.ShapeDtypeStruct((rows, heads * DH), jnp.float32),
                jax.ShapeDtypeStruct((rows, DH), jnp.float32),
            ],
            heads * rows * 6 * BS * DH * 4,
            after,
        )

    own_groups = ((0, 3), (3, 6), (6, 12))
    part_groups = ((0, 3), (3, 9), (9, 12))
    part_low = partner_part((0, 3), ("major1", "major2"), (all_weight[:16, :DH],))
    own_early = own_part((3, 6), ("major1", "minor1"))
    part_middle = partner_part(
        (3, 9), ("major1", "major3", "minor1", "minor3", "first1"), (part_low, own_early[1])
    )
    part_low = lax.ppermute(part_low, "frame", partner_moves)
    part_middle = lax.ppermute(part_middle, "frame", partner_moves)
    own_late = own_part((6, 12), ("major3", "minor1", "minor2"))
    part_high = partner_part(
        (9, 12), ("major3", "minor2", "minor4", "first2"), (own_late[1], major4, part_low)
    )
    part_high = lax.ppermute(part_high, "frame", partner_moves)
    own_low = own_part((0, 3), ("major1", "major2", "major4", "first2"))
    return project(
        own_groups,
        part_groups,
        all_weight,
        (*own_low, *own_early, *own_late, part_low, part_middle, part_high),
    )


def solution(mesh):
    in_specs = (
        P(("clip", "frame", "head"), None),
        P(("clip", "frame", "head"), None),
        P(("clip", "frame", "head"), None),
        P(),
        P("head", None),
    )
    out_specs = P(("clip", "frame", "head"), None)
    return jax.shard_map(
        per_device, mesh=mesh, in_specs=in_specs, out_specs=out_specs, check_vma=False
    )
```

```python
import functools
import math

import jax
import jax.numpy as jnp
from jax import lax
from jax.experimental import pallas as pl
from jax.experimental.pallas import tpu as pltpu
from jax.sharding import PartitionSpec as P

DH = 128
BS = 128
CROSS = 3
BATCH = 4
TILE = 768
NEG = -1e30
LOG2_SCALE = math.log2(math.e) / math.sqrt(DH)
MIB = 1024 * 1024


def frame_ids():
    frame = lax.axis_index("frame")
    return frame, 1 - 2 * lax.rem(frame, 2)


def entry(table_ref, query_frame, key_frame):
    frames = table_ref.shape[0]
    inside = (key_frame >= 0) & (key_frame < frames)
    count = table_ref[query_frame, jnp.clip(key_frame, 0, frames - 1)]
    return jnp.where(inside, count, 0)


def attend(problems):
    scores = []
    for query, parts in problems:
        row = []
        for keys, _, valid in parts:
            raw = lax.dot_general(
                query, keys, (((1,), (1,)), ((), ())), preferred_element_type=jnp.float32
            )
            row.append(raw if valid is None else jnp.where(valid, raw, NEG))
        scores.append(row)
    tops = []
    for row in scores:
        best = None
        for raw in row:
            for at in range(0, raw.shape[1], BS):
                piece = raw[:, at : at + BS]
                best = piece if best is None else jnp.maximum(best, piece)
        tops.append(best.max(axis=1, keepdims=True))
    weights = [
        [jnp.exp2((raw - top) * LOG2_SCALE) for raw in row] for row, top in zip(scores, tops)
    ]
    totals = []
    for row in weights:
        total = None
        for weight in row:
            for at in range(0, weight.shape[1], BS):
                piece = weight[:, at : at + BS]
                total = piece if total is None else total + piece
        totals.append(total.sum(axis=1, keepdims=True))
    results = []
    for (_, parts), row, top, total in zip(problems, weights, tops, totals):
        blended = 0.0
        for (_, values, _), weight in zip(parts, row):
            blended = blended + jnp.dot(
                weight.astype(jnp.bfloat16), values, preferred_element_type=jnp.float32
            )
        results.append((blended / total, top * LOG2_SCALE + jnp.log2(total)))
    return results


def attend_heads(group, blocks, problem, out):
    rows = blocks * BS
    heads = range(*group)
    lanes = lax.broadcasted_iota(jnp.int32, (rows, DH), 1)
    stats = jnp.zeros((rows, DH), jnp.float32)
    items = [(place, head, block) for place, head in enumerate(heads) for block in range(blocks)]
    sums = {}
    for at in range(0, len(items), BATCH):
        chunk = items[at : at + BATCH]
        results = attend([problem(head, block) for _, head, block in chunk])
        for (place, head, block), (blended, logsum) in zip(chunk, results):
            out[block * BS : (block + 1) * BS, head_cols(place)] = blended.astype(out.dtype)
            sums[place, block] = logsum
    for place in range(len(heads)):
        column = jnp.concatenate([sums[place, block] for block in range(blocks)], axis=0)
        stats = jnp.where(lanes == place, column, stats)
    return stats


def head_cols(head):
    return slice(head * DH, (head + 1) * DH)


def stat_rows(heads):
    return (4, 16) if heads <= 4 else (8, 32)


def write_stats(out, stats, heads):
    pad, count = stat_rows(heads)
    rows = stats.shape[0]
    packed, rest = 0.0, stats
    for part in range(3):
        piece = rest.astype(jnp.bfloat16).astype(jnp.float32)
        rest = rest - piece
        packed = packed + (pltpu.roll(piece, part * pad, 1) if part else piece)
    out[rows:, :] = jnp.zeros((count, out.shape[1]), out.dtype)
    out[rows:, :rows] = packed.T[:count].astype(out.dtype)


def read_stats(ref, heads):
    pad, count = stat_rows(heads)
    rows = ref.shape[0] - count
    packed = ref[rows:, :rows].astype(jnp.float32)
    padding = jnp.zeros((DH - count, rows), jnp.float32)
    packed = jnp.concatenate([packed, padding], axis=0).T
    return packed + pltpu.roll(packed, DH - pad, 1) + pltpu.roll(packed, DH - 2 * pad, 1)


def pair(ref, col, block):
    rows = ref.shape[0] // 2
    cols = head_cols(col)
    return (
        ref[block * BS : (block + 1) * BS, cols],
        ref[rows + block * BS : rows + (block + 1) * BS, cols],
    )


class Buffers:
    def __init__(self, refs):
        self.refs = refs

    def cross(self, head, block):
        return pair(self.refs["major2"], head, block)

    def far(self, head, block):
        return pair(self.refs["major4"], head, block)

    def away(self, head, block):
        if head < 6:
            return pair(self.refs["major1"], head, block)
        return pair(self.refs["major3"], head - 6, block)

    def near(self, head, block):
        if head < 9:
            return pair(self.refs["minor1"], head - 3, block)
        return pair(self.refs["minor2"], head - 9, block)

    def near_first(self, head):
        if head < 9:
            return pair(self.refs["first1"], head - 3, 0)
        return pair(self.refs["first2"], head - 9, 0)

    def cross_first(self, head):
        return pair(self.refs["first2"], CROSS + head, 0)

    def relay(self, head, block):
        if head < 9:
            return pair(self.refs["minor3"], head - 3, block)
        return pair(self.refs["minor4"], head - 9, block)


def partner_kernel(group, names, table_ref, query, keys, values, sib_keys, sib_values, *rest):
    frame, sign = frame_ids()
    buffers = Buffers(dict(zip(names, rest)))
    out = rest[-1]
    rows = query.shape[0]
    blocks = rows // BS
    partner = frame + sign
    own_count = entry(table_ref, partner, frame)
    near_count = entry(table_ref, partner, frame + 2 * sign)
    away_valid = entry(table_ref, partner, frame - 2 * sign) > 0
    relay_valid = entry(table_ref, partner, frame + 4 * sign) > 0
    cross_valid = entry(table_ref, partner, frame - sign) > 0

    def problem(head, block):
        mine = slice(block * BS, (block + 1) * BS)
        cols = head_cols(head)
        last = block + 1 == blocks
        parts = [(keys[mine, cols], values[mine, cols], None)]
        if last:
            parts.append((sib_keys[:BS, cols], sib_values[:BS, cols], own_count > 1))
        else:
            after = slice((block + 1) * BS, (block + 2) * BS)
            parts.append((keys[after, cols], values[after, cols], own_count > 1))
        parts.append((*buffers.away(head, block), away_valid))
        if head < CROSS:
            parts.append((*buffers.cross(head, block), cross_valid))
        else:
            parts.append((*buffers.near(head, block), near_count > 0))
            after = buffers.near_first(head) if last else buffers.near(head, block + 1)
            parts.append((*after, near_count > 1))
            parts.append((*buffers.relay(head, block), relay_valid))
        return query[mine, cols], parts

    stats = attend_heads(group, blocks, problem, out)
    write_stats(out, stats, group[1] - group[0])


def own_kernel(group, names, table_ref, query, keys, values, sib_keys, sib_values, *rest):
    frame, sign = frame_ids()
    buffers = Buffers(dict(zip(names, rest)))
    out, out_stats = rest[-2:]
    rows = query.shape[0]
    blocks = rows // BS
    near_valid = entry(table_ref, frame, frame + 2 * sign) > 0
    away_valid = entry(table_ref, frame, frame - 2 * sign) > 0
    cross_count = entry(table_ref, frame, frame - sign)
    far_valid = entry(table_ref, frame, frame - 3 * sign) > 0

    def problem(head, block):
        mine = slice(block * BS, (block + 1) * BS)
        cols = head_cols(head)
        parts = [
            (keys[:, cols], values[:, cols], None),
            (sib_keys[:, cols], sib_values[:, cols], None),
            (*buffers.away(head, block), away_valid),
        ]
        if head < CROSS:
            last = block + 1 == blocks
            parts.append((*buffers.cross(head, block), cross_count > 0))
            after = buffers.cross_first(head) if last else buffers.cross(head, block + 1)
            parts.append((*after, cross_count > 1))
            parts.append((*buffers.far(head, block), far_valid))
        else:
            parts.append((*buffers.near(head, block), near_valid))
        return query[mine, cols], parts

    out_stats[...] = attend_heads(group, blocks, problem, out)


def project_kernel(own_groups, part_groups, *refs):
    refs = list(refs)
    weight = refs.pop(0)
    owns = [(group, refs.pop(0), refs.pop(0)) for group in own_groups]
    parts = [(group, refs.pop(0)) for group in part_groups]
    out, attended = refs
    rows = out.shape[0]
    lanes = lax.broadcasted_iota(jnp.int32, (rows, DH), 1)
    own_at, part_at = {}, {}
    own_sum = part_sum = jnp.zeros((rows, DH), jnp.float32)
    for (first, last), own, stats in owns:
        shifted = pltpu.roll(stats[...], first, 1) if first else stats[...]
        own_sum = jnp.where((lanes >= first) & (lanes < last), shifted, own_sum)
        own_at.update({head: (own, head - first) for head in range(first, last)})
    for (first, last), part in parts:
        stats = read_stats(part, last - first)
        shifted = pltpu.roll(stats, first, 1) if first else stats
        part_sum = jnp.where((lanes >= first) & (lanes < last), shifted, part_sum)
        part_at.update({head: (part, head - first) for head in range(first, last)})
    top = jnp.maximum(own_sum, part_sum)
    own_weight = jnp.exp2(own_sum - top)
    part_weight = jnp.exp2(part_sum - top)
    inverse = 1.0 / (own_weight + part_weight)
    own_weight = own_weight * inverse
    part_weight = part_weight * inverse
    for head in sorted(own_at):
        own, own_place = own_at[head]
        part, part_place = part_at[head]
        mixed = own_weight[:, head : head + 1] * own[:, head_cols(own_place)] + part_weight[
            :, head : head + 1
        ] * part[:rows, head_cols(part_place)].astype(jnp.float32)
        attended[:, head_cols(head)] = mixed.astype(attended.dtype)
    for at in range(0, out.shape[1], TILE):
        out[:, at : at + TILE] = jnp.dot(
            attended[...], weight[:, at : at + TILE], preferred_element_type=jnp.float32
        ).astype(out.dtype)


def whole(shape):
    return pl.BlockSpec(shape, lambda i: (0,) * len(shape))


def run(body, name, table, operands, out_shapes, flops, after=()):
    return pl.pallas_call(
        body,
        grid=(1,),
        in_specs=[pl.BlockSpec(memory_space=pltpu.SMEM)]
        + [whole(x.shape) for x in operands]
        + [pl.BlockSpec(memory_space=pl.ANY)] * len(after),
        out_specs=[whole(s.shape) for s in out_shapes],
        out_shape=out_shapes,
        compiler_params=pltpu.CompilerParams(vmem_limit_bytes=8 * MIB),
        cost_estimate=pl.CostEstimate(
            flops=flops, bytes_accessed=MIB, transcendentals=flops // 512
        ),
        name=name,
    )(table, *operands, *after)


def tie_kernel(*refs):
    del refs


def tie(before, *payloads):
    anywhere = pl.BlockSpec(memory_space=pl.ANY)
    return pl.pallas_call(
        tie_kernel,
        in_specs=[anywhere] * (len(before) + len(payloads)),
        out_specs=[anywhere] * len(payloads),
        out_shape=[jax.ShapeDtypeStruct(p.shape, p.dtype) for p in payloads],
        input_output_aliases={len(before) + i: i for i in range(len(payloads))},
        compiler_params=pltpu.CompilerParams(vmem_limit_bytes=MIB),
        name="tie",
    )(*before, *payloads)


def project(own_groups, part_groups, weight, operands):
    rows = operands[0].shape[0]
    depth, columns = weight.shape
    return pl.pallas_call(
        functools.partial(project_kernel, own_groups, part_groups),
        grid=(1,),
        in_specs=[whole(x.shape) for x in (weight, *operands)],
        out_specs=whole((rows, columns)),
        out_shape=jax.ShapeDtypeStruct((rows, columns), jnp.bfloat16),
        scratch_shapes=[pltpu.VMEM((rows, depth), jnp.bfloat16)],
        compiler_params=pltpu.CompilerParams(vmem_limit_bytes=8 * MIB),
        cost_estimate=pl.CostEstimate(
            flops=2 * rows * depth * columns, bytes_accessed=12 * MIB, transcendentals=0
        ),
        name="merge_and_project",
    )(weight, *operands)


def per_device(queries, key_tokens, value_tokens, radial_table, out_weight):
    frames = lax.axis_size("frame")
    cores = lax.axis_size("head")
    rows = queries.shape[0]

    def moves(target):
        return [(f, target(f)) for f in range(frames) if 0 <= target(f) < frames]

    partner_moves = moves(lambda f: f ^ 1)
    near_moves = moves(lambda f: f - 2 if f % 2 == 0 else f + 2)
    away_moves = moves(lambda f: f + 2 if f % 2 == 0 else f - 2)
    core_moves = [(c, cores - 1 - c) for c in range(cores)]

    def pack(first, last):
        cols = slice(first * DH, last * DH)
        return jnp.concatenate([key_tokens[:, cols], value_tokens[:, cols]], axis=0)

    def firsts(*packed):
        return jnp.concatenate(
            [jnp.concatenate([p[at : at + BS] for p in packed], axis=1) for at in (0, rows)],
            axis=0,
        )

    cross = lax.ppermute(pack(0, 3), "frame", partner_moves)
    major1 = lax.ppermute(pack(0, 6), "frame", away_moves)
    minor1 = lax.ppermute(pack(3, 9), "frame", near_moves)
    sib_keys = lax.ppermute(key_tokens, "head", core_moves)
    sib_values = lax.ppermute(value_tokens, "head", core_moves)
    partner_query = lax.ppermute(queries, "frame", partner_moves)
    all_weight = lax.all_gather(out_weight, "head", axis=0, tiled=True)
    cross, to_minor2 = tie((sib_keys, sib_values), cross, pack(9, 12))
    minor2 = lax.ppermute(to_minor2, "frame", near_moves)
    major2 = lax.ppermute(cross, "frame", away_moves)
    (to_major3,) = tie((major1,), pack(6, 12))
    major3 = lax.ppermute(to_major3, "frame", away_moves)
    minor3 = lax.ppermute(minor1, "frame", near_moves)
    first1 = lax.ppermute(firsts(minor1), "head", core_moves)
    major4 = lax.ppermute(major2, "frame", away_moves)
    minor4 = lax.ppermute(minor2, "frame", near_moves)
    first2 = lax.ppermute(firsts(minor2, major2), "head", core_moves)
    refs = {
        "major1": major1,
        "major2": major2,
        "major3": major3,
        "major4": major4,
        "minor1": minor1,
        "minor2": minor2,
        "minor3": minor3,
        "minor4": minor4,
        "first1": first1,
        "first2": first2,
    }
    local = (key_tokens, value_tokens, sib_keys, sib_values)

    def partner_part(group, names, after=()):
        heads = group[1] - group[0]
        shape = jax.ShapeDtypeStruct((rows + stat_rows(heads)[1], heads * DH), jnp.bfloat16)
        (part,) = run(
            functools.partial(partner_kernel, group, names),
            "partner_part",
            radial_table,
            (partner_query, *local, *(refs[n] for n in names)),
            [shape],
            heads * rows * 6 * BS * DH * 4,
            after,
        )
        return part

    def own_part(group, names, after=()):
        heads = group[1] - group[0]
        return run(
            functools.partial(own_kernel, group, names),
            "own_part",
            radial_table,
            (queries, *local, *(refs[n] for n in names)),
            [
                jax.ShapeDtypeStruct((rows, heads * DH), jnp.float32),
                jax.ShapeDtypeStruct((rows, DH), jnp.float32),
            ],
            heads * rows * 6 * BS * DH * 4,
            after,
        )

    own_groups = ((0, 3), (3, 6), (6, 12))
    part_groups = ((0, 3), (3, 9), (9, 12))
    part_low = partner_part((0, 3), ("major1", "major2"), (all_weight[:16, :DH],))
    own_early = own_part((3, 6), ("major1", "minor1"))
    part_middle = partner_part(
        (3, 9), ("major1", "major3", "minor1", "minor3", "first1"), (part_low, own_early[1])
    )
    part_low = lax.ppermute(part_low, "frame", partner_moves)
    part_middle = lax.ppermute(part_middle, "frame", partner_moves)
    own_late = own_part((6, 12), ("major3", "minor1", "minor2"))
    part_high = partner_part(
        (9, 12), ("major3", "minor2", "minor4", "first2"), (own_late[1], major4, part_low)
    )
    part_high = lax.ppermute(part_high, "frame", partner_moves)
    own_low = own_part((0, 3), ("major1", "major2", "major4", "first2"))
    return project(
        own_groups,
        part_groups,
        all_weight,
        (*own_low, *own_early, *own_late, part_low, part_middle, part_high),
    )


def solution(mesh):
    in_specs = (
        P(("clip", "frame", "head"), None),
        P(("clip", "frame", "head"), None),
        P(("clip", "frame", "head"), None),
        P(),
        P("head", None),
    )
    out_specs = P(("clip", "frame", "head"), None)
    return jax.shard_map(
        per_device, mesh=mesh, in_specs=in_specs, out_specs=out_specs, check_vma=False
    )
```

```python
import functools
import math

import jax
import jax.numpy as jnp
from jax import lax
from jax.experimental import pallas as pl
from jax.experimental.pallas import tpu as pltpu
from jax.sharding import PartitionSpec as P

DH = 128
BS = 128
CROSS = 3
BATCH = 4
TILE = 768
NEG = -1e30
LOG2_SCALE = math.log2(math.e) / math.sqrt(DH)
MIB = 1024 * 1024


def frame_ids():
    frame = lax.axis_index("frame")
    return frame, 1 - 2 * lax.rem(frame, 2)


def entry(table_ref, query_frame, key_frame):
    frames = table_ref.shape[0]
    inside = (key_frame >= 0) & (key_frame < frames)
    count = table_ref[query_frame, jnp.clip(key_frame, 0, frames - 1)]
    return jnp.where(inside, count, 0)


def attend(problems):
    scores = []
    for query, parts in problems:
        row = []
        for keys, _, valid in parts:
            raw = lax.dot_general(
                query, keys, (((1,), (1,)), ((), ())), preferred_element_type=jnp.float32
            )
            row.append(raw if valid is None else jnp.where(valid, raw, NEG))
        scores.append(row)
    tops = []
    for row in scores:
        best = None
        for raw in row:
            for at in range(0, raw.shape[1], BS):
                piece = raw[:, at : at + BS]
                best = piece if best is None else jnp.maximum(best, piece)
        tops.append(best.max(axis=1, keepdims=True))
    weights = [
        [jnp.exp2((raw - top) * LOG2_SCALE) for raw in row] for row, top in zip(scores, tops)
    ]
    totals = []
    for row in weights:
        total = None
        for weight in row:
            for at in range(0, weight.shape[1], BS):
                piece = weight[:, at : at + BS]
                total = piece if total is None else total + piece
        totals.append(total.sum(axis=1, keepdims=True))
    results = []
    for (_, parts), row, top, total in zip(problems, weights, tops, totals):
        blended = 0.0
        for (_, values, _), weight in zip(parts, row):
            blended = blended + jnp.dot(
                weight.astype(jnp.bfloat16), values, preferred_element_type=jnp.float32
            )
        results.append((blended / total, top * LOG2_SCALE + jnp.log2(total)))
    return results


def attend_heads(group, blocks, problem, out):
    rows = blocks * BS
    heads = range(*group)
    lanes = lax.broadcasted_iota(jnp.int32, (rows, DH), 1)
    stats = jnp.zeros((rows, DH), jnp.float32)
    items = [(place, head, block) for place, head in enumerate(heads) for block in range(blocks)]
    sums = {}
    for at in range(0, len(items), BATCH):
        chunk = items[at : at + BATCH]
        results = attend([problem(head, block) for _, head, block in chunk])
        for (place, head, block), (blended, logsum) in zip(chunk, results):
            out[block * BS : (block + 1) * BS, head_cols(place)] = blended.astype(out.dtype)
            sums[place, block] = logsum
    for place in range(len(heads)):
        column = jnp.concatenate([sums[place, block] for block in range(blocks)], axis=0)
        stats = jnp.where(lanes == place, column, stats)
    return stats


def head_cols(head):
    return slice(head * DH, (head + 1) * DH)


def stat_rows(heads):
    return (4, 16) if heads <= 4 else (8, 32)


def write_stats(out, stats, heads):
    pad, count = stat_rows(heads)
    rows = stats.shape[0]
    packed, rest = 0.0, stats
    for part in range(3):
        piece = rest.astype(jnp.bfloat16).astype(jnp.float32)
        rest = rest - piece
        packed = packed + (pltpu.roll(piece, part * pad, 1) if part else piece)
    out[rows:, :] = jnp.zeros((count, out.shape[1]), out.dtype)
    out[rows:, :rows] = packed.T[:count].astype(out.dtype)


def read_stats(ref, heads):
    pad, count = stat_rows(heads)
    rows = ref.shape[0] - count
    packed = ref[rows:, :rows].astype(jnp.float32)
    padding = jnp.zeros((DH - count, rows), jnp.float32)
    packed = jnp.concatenate([packed, padding], axis=0).T
    return packed + pltpu.roll(packed, DH - pad, 1) + pltpu.roll(packed, DH - 2 * pad, 1)


def pair(ref, col, block):
    rows = ref.shape[0] // 2
    cols = head_cols(col)
    return (
        ref[block * BS : (block + 1) * BS, cols],
        ref[rows + block * BS : rows + (block + 1) * BS, cols],
    )


class Buffers:
    def __init__(self, refs):
        self.refs = refs

    def cross(self, head, block):
        return pair(self.refs["major2"], head, block)

    def far(self, head, block):
        return pair(self.refs["major4"], head, block)

    def away(self, head, block):
        if head < 6:
            return pair(self.refs["major1"], head, block)
        return pair(self.refs["major3"], head - 6, block)

    def near(self, head, block):
        if head < 9:
            return pair(self.refs["minor1"], head - 3, block)
        return pair(self.refs["minor2"], head - 9, block)

    def near_first(self, head):
        return pair(self.refs["nearest"], head - 3, 0)

    def cross_first(self, head):
        return pair(self.refs["nearest"], 9 + head, 0)

    def relay(self, head, block):
        if head < 9:
            return pair(self.refs["minor3"], head - 3, block)
        return pair(self.refs["minor4"], head - 9, block)


def partner_kernel(group, names, table_ref, query, keys, values, sib_keys, sib_values, *rest):
    frame, sign = frame_ids()
    buffers = Buffers(dict(zip(names, rest)))
    out = rest[-1]
    rows = query.shape[0]
    blocks = rows // BS
    partner = frame + sign
    own_count = entry(table_ref, partner, frame)
    near_count = entry(table_ref, partner, frame + 2 * sign)
    away_valid = entry(table_ref, partner, frame - 2 * sign) > 0
    relay_valid = entry(table_ref, partner, frame + 4 * sign) > 0
    cross_valid = entry(table_ref, partner, frame - sign) > 0

    def problem(head, block):
        mine = slice(block * BS, (block + 1) * BS)
        cols = head_cols(head)
        last = block + 1 == blocks
        parts = [(keys[mine, cols], values[mine, cols], None)]
        if last:
            parts.append((sib_keys[:BS, cols], sib_values[:BS, cols], own_count > 1))
        else:
            after = slice((block + 1) * BS, (block + 2) * BS)
            parts.append((keys[after, cols], values[after, cols], own_count > 1))
        parts.append((*buffers.away(head, block), away_valid))
        if head < CROSS:
            parts.append((*buffers.cross(head, block), cross_valid))
        else:
            parts.append((*buffers.near(head, block), near_count > 0))
            after = buffers.near_first(head) if last else buffers.near(head, block + 1)
            parts.append((*after, near_count > 1))
            parts.append((*buffers.relay(head, block), relay_valid))
        return query[mine, cols], parts

    stats = attend_heads(group, blocks, problem, out)
    write_stats(out, stats, group[1] - group[0])


def own_kernel(group, names, table_ref, query, keys, values, sib_keys, sib_values, *rest):
    frame, sign = frame_ids()
    buffers = Buffers(dict(zip(names, rest)))
    out, out_stats = rest[-2:]
    rows = query.shape[0]
    blocks = rows // BS
    near_valid = entry(table_ref, frame, frame + 2 * sign) > 0
    away_valid = entry(table_ref, frame, frame - 2 * sign) > 0
    cross_count = entry(table_ref, frame, frame - sign)
    far_valid = entry(table_ref, frame, frame - 3 * sign) > 0

    def problem(head, block):
        mine = slice(block * BS, (block + 1) * BS)
        cols = head_cols(head)
        parts = [
            (keys[:, cols], values[:, cols], None),
            (sib_keys[:, cols], sib_values[:, cols], None),
            (*buffers.away(head, block), away_valid),
        ]
        if head < CROSS:
            last = block + 1 == blocks
            parts.append((*buffers.cross(head, block), cross_count > 0))
            after = buffers.cross_first(head) if last else buffers.cross(head, block + 1)
            parts.append((*after, cross_count > 1))
            parts.append((*buffers.far(head, block), far_valid))
        else:
            parts.append((*buffers.near(head, block), near_valid))
        return query[mine, cols], parts

    out_stats[...] = attend_heads(group, blocks, problem, out)


def project_kernel(own_groups, part_groups, chunks, *refs):
    refs = list(refs)
    weights = [refs.pop(0) for _ in range(chunks)]
    sib_weights = [refs.pop(0) for _ in range(chunks)]
    owns = [(group, refs.pop(0), refs.pop(0)) for group in own_groups]
    parts = [(group, refs.pop(0)) for group in part_groups]
    out, attended = refs
    rows = out.shape[0]
    lanes = lax.broadcasted_iota(jnp.int32, (rows, DH), 1)
    own_at, part_at = {}, {}
    own_sum = part_sum = jnp.zeros((rows, DH), jnp.float32)
    for (first, last), own, stats in owns:
        shifted = pltpu.roll(stats[...], first, 1) if first else stats[...]
        own_sum = jnp.where((lanes >= first) & (lanes < last), shifted, own_sum)
        own_at.update({head: (own, head - first) for head in range(first, last)})
    for (first, last), part in parts:
        stats = read_stats(part, last - first)
        shifted = pltpu.roll(stats, first, 1) if first else stats
        part_sum = jnp.where((lanes >= first) & (lanes < last), shifted, part_sum)
        part_at.update({head: (part, head - first) for head in range(first, last)})
    top = jnp.maximum(own_sum, part_sum)
    own_weight = jnp.exp2(own_sum - top)
    part_weight = jnp.exp2(part_sum - top)
    inverse = 1.0 / (own_weight + part_weight)
    own_weight = own_weight * inverse
    part_weight = part_weight * inverse
    for head in sorted(own_at):
        own, own_place = own_at[head]
        part, part_place = part_at[head]
        mixed = own_weight[:, head : head + 1] * own[:, head_cols(own_place)] + part_weight[
            :, head : head + 1
        ] * part[:rows, head_cols(part_place)].astype(jnp.float32)
        attended[:, head_cols(head)] = mixed.astype(attended.dtype)
    core = lax.axis_index("head")
    chunk = weights[0].shape[0]
    pieces = []
    for index in range(chunks):
        for weight, side in ((weights[index], core), (sib_weights[index], 1 - core)):
            at = pl.multiple_of((side * chunks + index) * chunk, DH)
            pieces.append((attended[:, pl.ds(at, chunk)], weight))
    for at in range(0, out.shape[1], TILE):
        product = 0.0
        for piece, weight in pieces:
            product = product + jnp.dot(
                piece, weight[:, at : at + TILE], preferred_element_type=jnp.float32
            )
        out[:, at : at + TILE] = product.astype(out.dtype)


def whole(shape):
    return pl.BlockSpec(shape, lambda i: (0,) * len(shape))


def run(body, name, table, operands, out_shapes, flops, after=()):
    return pl.pallas_call(
        body,
        grid=(1,),
        in_specs=[pl.BlockSpec(memory_space=pltpu.SMEM)]
        + [whole(x.shape) for x in operands]
        + [pl.BlockSpec(memory_space=pl.ANY)] * len(after),
        out_specs=[whole(s.shape) for s in out_shapes],
        out_shape=out_shapes,
        compiler_params=pltpu.CompilerParams(vmem_limit_bytes=8 * MIB),
        cost_estimate=pl.CostEstimate(
            flops=flops, bytes_accessed=MIB, transcendentals=flops // 512
        ),
        name=name,
    )(table, *operands, *after)


def tie_kernel(*refs):
    del refs


def tie(before, *payloads):
    before = tuple(before)
    anywhere = pl.BlockSpec(memory_space=pl.ANY)
    return pl.pallas_call(
        tie_kernel,
        in_specs=[anywhere] * (len(before) + len(payloads)),
        out_specs=[anywhere] * len(payloads),
        out_shape=[jax.ShapeDtypeStruct(p.shape, p.dtype) for p in payloads],
        input_output_aliases={len(before) + i: i for i in range(len(payloads))},
        compiler_params=pltpu.CompilerParams(vmem_limit_bytes=MIB),
        name="tie",
    )(*before, *payloads)


def project(own_groups, part_groups, weights, operands):
    rows, columns = operands[0].shape[0], weights[0].shape[1]
    depth = sum(weight.shape[0] for weight in weights)
    return pl.pallas_call(
        functools.partial(project_kernel, own_groups, part_groups, len(weights) // 2),
        grid=(1,),
        in_specs=[whole(x.shape) for x in (*weights, *operands)],
        out_specs=whole((rows, columns)),
        out_shape=jax.ShapeDtypeStruct((rows, columns), jnp.bfloat16),
        scratch_shapes=[pltpu.VMEM((rows, depth), jnp.bfloat16)],
        compiler_params=pltpu.CompilerParams(vmem_limit_bytes=8 * MIB),
        cost_estimate=pl.CostEstimate(
            flops=2 * rows * depth * columns, bytes_accessed=12 * MIB, transcendentals=0
        ),
        name="merge_and_project",
    )(*weights, *operands)


def per_device(queries, key_tokens, value_tokens, radial_table, out_weight):
    frames = lax.axis_size("frame")
    cores = lax.axis_size("head")
    rows = queries.shape[0]

    def moves(target):
        return [(f, target(f)) for f in range(frames) if 0 <= target(f) < frames]

    partner_moves = moves(lambda f: f ^ 1)
    near_moves = moves(lambda f: f - 2 if f % 2 == 0 else f + 2)
    away_moves = moves(lambda f: f + 2 if f % 2 == 0 else f - 2)
    cross_moves = moves(lambda f: f - 1 if f % 2 == 0 else f + 1)
    core_moves = [(c, cores - 1 - c) for c in range(cores)]

    def pack(first, last):
        cols = slice(first * DH, last * DH)
        return jnp.concatenate([key_tokens[:, cols], value_tokens[:, cols]], axis=0)

    def firsts(*packed):
        return jnp.concatenate(
            [jnp.concatenate([p[at : at + BS] for p in packed], axis=1) for at in (0, rows)],
            axis=0,
        )

    major1 = lax.ppermute(pack(0, 6), "frame", away_moves)
    minor1 = lax.ppermute(pack(3, 9), "frame", near_moves)
    sib_keys = lax.ppermute(key_tokens, "head", core_moves)
    sib_values = lax.ppermute(value_tokens, "head", core_moves)
    own_weight = [out_weight]
    sib_weight = [lax.ppermute(out_weight, "head", core_moves)]
    to_minor2, to_major2, to_partner = tie(
        (sib_keys, sib_values, *sib_weight), pack(9, 12), pack(0, 3), queries
    )
    partner_query = lax.ppermute(to_partner, "frame", partner_moves)
    minor2 = lax.ppermute(to_minor2, "frame", near_moves)
    major2 = lax.ppermute(to_major2, "frame", cross_moves)
    minor3 = lax.ppermute(minor1, "frame", near_moves)
    (to_major3,) = tie((major1,), pack(6, 12))
    major3 = lax.ppermute(to_major3, "frame", away_moves)
    major4 = lax.ppermute(major2, "frame", away_moves)
    minor4 = lax.ppermute(minor2, "frame", near_moves)
    nearest = lax.ppermute(firsts(minor1, minor2, major2), "head", core_moves)
    refs = {
        "major1": major1,
        "major2": major2,
        "major3": major3,
        "major4": major4,
        "minor1": minor1,
        "minor2": minor2,
        "minor3": minor3,
        "minor4": minor4,
        "nearest": nearest,
    }
    local = (key_tokens, value_tokens, sib_keys, sib_values)

    def partner_part(group, names, after=()):
        heads = group[1] - group[0]
        shape = jax.ShapeDtypeStruct((rows + stat_rows(heads)[1], heads * DH), jnp.bfloat16)
        (part,) = run(
            functools.partial(partner_kernel, group, names),
            "partner_part",
            radial_table,
            (partner_query, *local, *(refs[n] for n in names)),
            [shape],
            heads * rows * 6 * BS * DH * 4,
            after,
        )
        return part

    def own_part(group, names, after=()):
        heads = group[1] - group[0]
        return run(
            functools.partial(own_kernel, group, names),
            "own_part",
            radial_table,
            (queries, *local, *(refs[n] for n in names)),
            [
                jax.ShapeDtypeStruct((rows, heads * DH), jnp.float32),
                jax.ShapeDtypeStruct((rows, DH), jnp.float32),
            ],
            heads * rows * 6 * BS * DH * 4,
            after,
        )

    own_groups = ((0, 3), (3, 6), (6, 12))
    part_groups = ((0, 3), (3, 9), (9, 12))
    part_low = partner_part((0, 3), ("major1", "major2"))
    own_early = own_part((3, 6), ("major1", "minor1"))
    part_middle = partner_part(
        (3, 9), ("major1", "major3", "minor1", "minor3", "nearest"), (part_low, own_early[1])
    )
    part_low = lax.ppermute(part_low, "frame", partner_moves)
    part_middle = lax.ppermute(part_middle, "frame", partner_moves)
    own_late = own_part((6, 12), ("major3", "minor1", "minor2"))
    part_high = partner_part(
        (9, 12), ("major3", "minor2", "minor4", "nearest"), (own_late[1], major4, part_low, *sib_weight)
    )
    part_high = lax.ppermute(part_high, "frame", partner_moves)
    own_low = own_part((0, 3), ("major1", "major2", "major4", "nearest"))
    return project(
        own_groups,
        part_groups,
        (*own_weight, *sib_weight),
        (*own_low, *own_early, *own_late, part_low, part_middle, part_high),
    )


def solution(mesh):
    in_specs = (
        P(("clip", "frame", "head"), None),
        P(("clip", "frame", "head"), None),
        P(("clip", "frame", "head"), None),
        P(),
        P("head", None),
    )
    out_specs = P(("clip", "frame", "head"), None)
    return jax.shard_map(
        per_device, mesh=mesh, in_specs=in_specs, out_specs=out_specs, check_vma=False
    )
```

```python
import functools
import math

import jax
import jax.numpy as jnp
from jax import lax
from jax.experimental import pallas as pl
from jax.experimental.pallas import tpu as pltpu
from jax.sharding import PartitionSpec as P

DH = 128
BS = 128
CROSS = 3
BATCH = 4
TILE = 768
NEG = -1e30
LOG2_SCALE = math.log2(math.e) / math.sqrt(DH)
MIB = 1024 * 1024


def frame_ids():
    frame = lax.axis_index("frame")
    return frame, 1 - 2 * lax.rem(frame, 2)


def entry(table_ref, query_frame, key_frame):
    frames = table_ref.shape[0]
    inside = (key_frame >= 0) & (key_frame < frames)
    count = table_ref[query_frame, jnp.clip(key_frame, 0, frames - 1)]
    return jnp.where(inside, count, 0)


def attend(problems):
    scores = []
    for query, parts in problems:
        row = []
        for keys, _, valid in parts:
            raw = lax.dot_general(
                query, keys, (((1,), (1,)), ((), ())), preferred_element_type=jnp.float32
            )
            row.append(raw if valid is None else jnp.where(valid, raw, NEG))
        scores.append(row)
    tops = []
    for row in scores:
        best = None
        for raw in row:
            for at in range(0, raw.shape[1], BS):
                piece = raw[:, at : at + BS]
                best = piece if best is None else jnp.maximum(best, piece)
        tops.append(best.max(axis=1, keepdims=True))
    weights = [
        [jnp.exp2((raw - top) * LOG2_SCALE) for raw in row] for row, top in zip(scores, tops)
    ]
    totals = []
    for row in weights:
        total = None
        for weight in row:
            for at in range(0, weight.shape[1], BS):
                piece = weight[:, at : at + BS]
                total = piece if total is None else total + piece
        totals.append(total.sum(axis=1, keepdims=True))
    results = []
    for (_, parts), row, top, total in zip(problems, weights, tops, totals):
        blended = 0.0
        for (_, values, _), weight in zip(parts, row):
            blended = blended + jnp.dot(
                weight.astype(jnp.bfloat16), values, preferred_element_type=jnp.float32
            )
        results.append((blended / total, top * LOG2_SCALE + jnp.log2(total)))
    return results


def attend_heads(group, blocks, problem, out):
    rows = blocks * BS
    heads = range(*group)
    lanes = lax.broadcasted_iota(jnp.int32, (rows, DH), 1)
    stats = jnp.zeros((rows, DH), jnp.float32)
    items = [(place, head, block) for place, head in enumerate(heads) for block in range(blocks)]
    sums = {}
    for at in range(0, len(items), BATCH):
        chunk = items[at : at + BATCH]
        results = attend([problem(head, block) for _, head, block in chunk])
        for (place, head, block), (blended, logsum) in zip(chunk, results):
            out[block * BS : (block + 1) * BS, head_cols(place)] = blended.astype(out.dtype)
            sums[place, block] = logsum
    for place in range(len(heads)):
        column = jnp.concatenate([sums[place, block] for block in range(blocks)], axis=0)
        stats = jnp.where(lanes == place, column, stats)
    return stats


def head_cols(head):
    return slice(head * DH, (head + 1) * DH)


def stat_rows(heads):
    return (4, 16) if heads <= 4 else (8, 32)


def write_stats(out, stats, heads):
    pad, count = stat_rows(heads)
    rows = stats.shape[0]
    packed, rest = 0.0, stats
    for part in range(3):
        piece = rest.astype(jnp.bfloat16).astype(jnp.float32)
        rest = rest - piece
        packed = packed + (pltpu.roll(piece, part * pad, 1) if part else piece)
    out[rows:, :] = jnp.zeros((count, out.shape[1]), out.dtype)
    out[rows:, :rows] = packed.T[:count].astype(out.dtype)


def read_stats(ref, heads):
    pad, count = stat_rows(heads)
    rows = ref.shape[0] - count
    packed = ref[rows:, :rows].astype(jnp.float32)
    padding = jnp.zeros((DH - count, rows), jnp.float32)
    packed = jnp.concatenate([packed, padding], axis=0).T
    return packed + pltpu.roll(packed, DH - pad, 1) + pltpu.roll(packed, DH - 2 * pad, 1)


def pair(ref, col, block):
    rows = ref.shape[0] // 2
    cols = head_cols(col)
    return (
        ref[block * BS : (block + 1) * BS, cols],
        ref[rows + block * BS : rows + (block + 1) * BS, cols],
    )


class Buffers:
    def __init__(self, refs):
        self.refs = refs

    def cross(self, head, block):
        return pair(self.refs["major2"], head, block)

    def far(self, head, block):
        return pair(self.refs["major4"], head, block)

    def away(self, head, block):
        if head < 6:
            return pair(self.refs["major1"], head, block)
        return pair(self.refs["major3"], head - 6, block)

    def near(self, head, block):
        if head < 9:
            return pair(self.refs["minor1"], head - 3, block)
        return pair(self.refs["minor2"], head - 9, block)

    def near_first(self, head):
        return pair(self.refs["nearest"], head - 3, 0)

    def cross_first(self, head):
        return pair(self.refs["nearest"], 9 + head, 0)

    def relay(self, head, block):
        if head < 9:
            return pair(self.refs["minor3"], head - 3, block)
        return pair(self.refs["minor4"], head - 9, block)


def partner_kernel(group, names, table_ref, query, keys, values, sib_keys, sib_values, *rest):
    frame, sign = frame_ids()
    buffers = Buffers(dict(zip(names, rest)))
    out = rest[-1]
    rows = query.shape[0]
    blocks = rows // BS
    partner = frame + sign
    own_count = entry(table_ref, partner, frame)
    near_count = entry(table_ref, partner, frame + 2 * sign)
    away_valid = entry(table_ref, partner, frame - 2 * sign) > 0
    relay_valid = entry(table_ref, partner, frame + 4 * sign) > 0
    cross_valid = entry(table_ref, partner, frame - sign) > 0

    def problem(head, block):
        mine = slice(block * BS, (block + 1) * BS)
        cols = head_cols(head)
        last = block + 1 == blocks
        parts = [(keys[mine, cols], values[mine, cols], None)]
        if last:
            parts.append((sib_keys[:BS, cols], sib_values[:BS, cols], own_count > 1))
        else:
            after = slice((block + 1) * BS, (block + 2) * BS)
            parts.append((keys[after, cols], values[after, cols], own_count > 1))
        parts.append((*buffers.away(head, block), away_valid))
        if head < CROSS:
            parts.append((*buffers.cross(head, block), cross_valid))
        else:
            parts.append((*buffers.near(head, block), near_count > 0))
            after = buffers.near_first(head) if last else buffers.near(head, block + 1)
            parts.append((*after, near_count > 1))
            parts.append((*buffers.relay(head, block), relay_valid))
        return query[mine, cols], parts

    stats = attend_heads(group, blocks, problem, out)
    write_stats(out, stats, group[1] - group[0])


def own_kernel(group, names, table_ref, query, keys, values, sib_keys, sib_values, *rest):
    frame, sign = frame_ids()
    buffers = Buffers(dict(zip(names, rest)))
    out, out_stats = rest[-2:]
    rows = query.shape[0]
    blocks = rows // BS
    near_valid = entry(table_ref, frame, frame + 2 * sign) > 0
    away_valid = entry(table_ref, frame, frame - 2 * sign) > 0
    cross_count = entry(table_ref, frame, frame - sign)
    far_valid = entry(table_ref, frame, frame - 3 * sign) > 0

    def problem(head, block):
        mine = slice(block * BS, (block + 1) * BS)
        cols = head_cols(head)
        parts = [
            (keys[:, cols], values[:, cols], None),
            (sib_keys[:, cols], sib_values[:, cols], None),
            (*buffers.away(head, block), away_valid),
        ]
        if head < CROSS:
            last = block + 1 == blocks
            parts.append((*buffers.cross(head, block), cross_count > 0))
            after = buffers.cross_first(head) if last else buffers.cross(head, block + 1)
            parts.append((*after, cross_count > 1))
            parts.append((*buffers.far(head, block), far_valid))
        else:
            parts.append((*buffers.near(head, block), near_valid))
        return query[mine, cols], parts

    out_stats[...] = attend_heads(group, blocks, problem, out)


def project_kernel(own_groups, part_groups, chunks, *refs):
    refs = list(refs)
    weights = [refs.pop(0) for _ in range(chunks)]
    sib_weights = [refs.pop(0) for _ in range(chunks)]
    owns = [(group, refs.pop(0), refs.pop(0)) for group in own_groups]
    parts = [(group, refs.pop(0)) for group in part_groups]
    out, attended = refs
    rows = out.shape[0]
    lanes = lax.broadcasted_iota(jnp.int32, (rows, DH), 1)
    own_at, part_at = {}, {}
    own_sum = part_sum = jnp.zeros((rows, DH), jnp.float32)
    for (first, last), own, stats in owns:
        shifted = pltpu.roll(stats[...], first, 1) if first else stats[...]
        own_sum = jnp.where((lanes >= first) & (lanes < last), shifted, own_sum)
        own_at.update({head: (own, head - first) for head in range(first, last)})
    for (first, last), part in parts:
        stats = read_stats(part, last - first)
        shifted = pltpu.roll(stats, first, 1) if first else stats
        part_sum = jnp.where((lanes >= first) & (lanes < last), shifted, part_sum)
        part_at.update({head: (part, head - first) for head in range(first, last)})
    top = jnp.maximum(own_sum, part_sum)
    own_weight = jnp.exp2(own_sum - top)
    part_weight = jnp.exp2(part_sum - top)
    inverse = 1.0 / (own_weight + part_weight)
    own_weight = own_weight * inverse
    part_weight = part_weight * inverse
    for head in sorted(own_at):
        own, own_place = own_at[head]
        part, part_place = part_at[head]
        mixed = own_weight[:, head : head + 1] * own[:, head_cols(own_place)] + part_weight[
            :, head : head + 1
        ] * part[:rows, head_cols(part_place)].astype(jnp.float32)
        attended[:, head_cols(head)] = mixed.astype(attended.dtype)
    core = lax.axis_index("head")
    chunk = weights[0].shape[0]
    pieces = []
    for index in range(chunks):
        for weight, side in ((weights[index], core), (sib_weights[index], 1 - core)):
            at = pl.multiple_of((side * chunks + index) * chunk, DH)
            pieces.append((attended[:, pl.ds(at, chunk)], weight))
    for at in range(0, out.shape[1], TILE):
        product = 0.0
        for piece, weight in pieces:
            product = product + jnp.dot(
                piece, weight[:, at : at + TILE], preferred_element_type=jnp.float32
            )
        out[:, at : at + TILE] = product.astype(out.dtype)


def whole(shape):
    return pl.BlockSpec(shape, lambda i: (0,) * len(shape))


def run(body, name, table, operands, out_shapes, flops, after=()):
    return pl.pallas_call(
        body,
        grid=(1,),
        in_specs=[pl.BlockSpec(memory_space=pltpu.SMEM)]
        + [whole(x.shape) for x in operands]
        + [pl.BlockSpec(memory_space=pl.ANY)] * len(after),
        out_specs=[whole(s.shape) for s in out_shapes],
        out_shape=out_shapes,
        compiler_params=pltpu.CompilerParams(vmem_limit_bytes=8 * MIB),
        cost_estimate=pl.CostEstimate(
            flops=flops, bytes_accessed=MIB, transcendentals=flops // 512
        ),
        name=name,
    )(table, *operands, *after)


def tie_kernel(*refs):
    del refs


def tie(before, *payloads):
    before = tuple(before)
    anywhere = pl.BlockSpec(memory_space=pl.ANY)
    return pl.pallas_call(
        tie_kernel,
        in_specs=[anywhere] * (len(before) + len(payloads)),
        out_specs=[anywhere] * len(payloads),
        out_shape=[jax.ShapeDtypeStruct(p.shape, p.dtype) for p in payloads],
        input_output_aliases={len(before) + i: i for i in range(len(payloads))},
        compiler_params=pltpu.CompilerParams(vmem_limit_bytes=MIB),
        name="tie",
    )(*before, *payloads)


def project(own_groups, part_groups, weights, operands):
    rows, columns = operands[0].shape[0], weights[0].shape[1]
    depth = sum(weight.shape[0] for weight in weights)
    return pl.pallas_call(
        functools.partial(project_kernel, own_groups, part_groups, len(weights) // 2),
        grid=(1,),
        in_specs=[whole(x.shape) for x in (*weights, *operands)],
        out_specs=whole((rows, columns)),
        out_shape=jax.ShapeDtypeStruct((rows, columns), jnp.bfloat16),
        scratch_shapes=[pltpu.VMEM((rows, depth), jnp.bfloat16)],
        compiler_params=pltpu.CompilerParams(vmem_limit_bytes=8 * MIB),
        cost_estimate=pl.CostEstimate(
            flops=2 * rows * depth * columns, bytes_accessed=12 * MIB, transcendentals=0
        ),
        name="merge_and_project",
    )(*weights, *operands)


def per_device(queries, key_tokens, value_tokens, radial_table, out_weight):
    frames = lax.axis_size("frame")
    cores = lax.axis_size("head")
    rows = queries.shape[0]

    def moves(target):
        return [(f, target(f)) for f in range(frames) if 0 <= target(f) < frames]

    partner_moves = moves(lambda f: f ^ 1)
    near_moves = moves(lambda f: f - 2 if f % 2 == 0 else f + 2)
    away_moves = moves(lambda f: f + 2 if f % 2 == 0 else f - 2)
    cross_moves = moves(lambda f: f - 1 if f % 2 == 0 else f + 1)
    core_moves = [(c, cores - 1 - c) for c in range(cores)]

    def pack(first, last):
        cols = slice(first * DH, last * DH)
        return jnp.concatenate([key_tokens[:, cols], value_tokens[:, cols]], axis=0)

    def firsts(*packed):
        return jnp.concatenate(
            [jnp.concatenate([p[at : at + BS] for p in packed], axis=1) for at in (0, rows)],
            axis=0,
        )

    sib_keys = lax.ppermute(key_tokens, "head", core_moves)
    sib_values = lax.ppermute(value_tokens, "head", core_moves)
    major1 = lax.ppermute(pack(0, 6), "frame", away_moves)
    minor1 = lax.ppermute(pack(3, 9), "frame", near_moves)
    to_minor2, to_major2, to_sib = tie(
        (sib_keys, sib_values), pack(9, 12), pack(0, 3), out_weight
    )
    own_weight = [to_sib]
    sib_weight = [lax.ppermute(to_sib, "head", core_moves)]
    (to_partner,) = tie(sib_weight, queries)
    partner_query = lax.ppermute(to_partner, "frame", partner_moves)
    minor2 = lax.ppermute(to_minor2, "frame", near_moves)
    major2 = lax.ppermute(to_major2, "frame", cross_moves)
    minor3 = lax.ppermute(minor1, "frame", near_moves)
    (to_major3,) = tie((major2,), pack(6, 12))
    major3 = lax.ppermute(to_major3, "frame", away_moves)
    major4 = lax.ppermute(major2, "frame", away_moves)
    minor4 = lax.ppermute(minor2, "frame", near_moves)
    (to_nearest,) = tie((partner_query,), firsts(minor1, minor2, major2))
    nearest = lax.ppermute(to_nearest, "head", core_moves)
    refs = {
        "major1": major1,
        "major2": major2,
        "major3": major3,
        "major4": major4,
        "minor1": minor1,
        "minor2": minor2,
        "minor3": minor3,
        "minor4": minor4,
        "nearest": nearest,
    }
    local = (key_tokens, value_tokens, sib_keys, sib_values)

    def partner_part(group, names, after=()):
        heads = group[1] - group[0]
        shape = jax.ShapeDtypeStruct((rows + stat_rows(heads)[1], heads * DH), jnp.bfloat16)
        (part,) = run(
            functools.partial(partner_kernel, group, names),
            "partner_part",
            radial_table,
            (partner_query, *local, *(refs[n] for n in names)),
            [shape],
            heads * rows * 6 * BS * DH * 4,
            after,
        )
        return part

    def own_part(group, names, after=()):
        heads = group[1] - group[0]
        return run(
            functools.partial(own_kernel, group, names),
            "own_part",
            radial_table,
            (queries, *local, *(refs[n] for n in names)),
            [
                jax.ShapeDtypeStruct((rows, heads * DH), jnp.float32),
                jax.ShapeDtypeStruct((rows, DH), jnp.float32),
            ],
            heads * rows * 6 * BS * DH * 4,
            after,
        )

    own_groups = ((0, 3), (3, 6), (6, 12))
    part_groups = ((0, 3), (3, 9), (9, 12))
    part_low = partner_part((0, 3), ("major1", "major2"))
    own_early = own_part((3, 6), ("major1", "minor1"))
    part_middle = partner_part(
        (3, 9), ("major1", "major3", "minor1", "minor3", "nearest"), (part_low, own_early[1])
    )
    part_low = lax.ppermute(part_low, "frame", partner_moves)
    part_middle = lax.ppermute(part_middle, "frame", partner_moves)
    own_late = own_part((6, 12), ("major3", "minor1", "minor2"))
    part_high = partner_part(
        (9, 12), ("major3", "minor2", "minor4", "nearest"), (own_late[1], major4, part_low, *sib_weight)
    )
    part_high = lax.ppermute(part_high, "frame", partner_moves)
    own_low = own_part((0, 3), ("major1", "major2", "major4", "nearest"))
    return project(
        own_groups,
        part_groups,
        (*own_weight, *sib_weight),
        (*own_low, *own_early, *own_late, part_low, part_middle, part_high),
    )


def solution(mesh):
    in_specs = (
        P(("clip", "frame", "head"), None),
        P(("clip", "frame", "head"), None),
        P(("clip", "frame", "head"), None),
        P(),
        P("head", None),
    )
    out_specs = P(("clip", "frame", "head"), None)
    return jax.shard_map(
        per_device, mesh=mesh, in_specs=in_specs, out_specs=out_specs, check_vma=False
    )
```

```python
import functools
import math

import jax
import jax.numpy as jnp
from jax import lax
from jax.experimental import pallas as pl
from jax.experimental.pallas import tpu as pltpu
from jax.sharding import PartitionSpec as P

DH = 128
BS = 128
CROSS = 3
BATCH = 4
TILE = 768
NEG = -1e30
LOG2_SCALE = math.log2(math.e) / math.sqrt(DH)
MIB = 1024 * 1024


def frame_ids():
    frame = lax.axis_index("frame")
    return frame, 1 - 2 * lax.rem(frame, 2)


def entry(table_ref, query_frame, key_frame):
    frames = table_ref.shape[0]
    inside = (key_frame >= 0) & (key_frame < frames)
    count = table_ref[query_frame, jnp.clip(key_frame, 0, frames - 1)]
    return jnp.where(inside, count, 0)


def attend(problems):
    scores = []
    for query, parts in problems:
        row = []
        for keys, _, valid in parts:
            raw = lax.dot_general(
                query, keys, (((1,), (1,)), ((), ())), preferred_element_type=jnp.float32
            )
            row.append(raw if valid is None else jnp.where(valid, raw, NEG))
        scores.append(row)
    tops = []
    for row in scores:
        best = None
        for raw in row:
            for at in range(0, raw.shape[1], BS):
                piece = raw[:, at : at + BS]
                best = piece if best is None else jnp.maximum(best, piece)
        tops.append(best.max(axis=1, keepdims=True))
    weights = [
        [jnp.exp2((raw - top) * LOG2_SCALE) for raw in row] for row, top in zip(scores, tops)
    ]
    totals = []
    for row in weights:
        total = None
        for weight in row:
            for at in range(0, weight.shape[1], BS):
                piece = weight[:, at : at + BS]
                total = piece if total is None else total + piece
        totals.append(total.sum(axis=1, keepdims=True))
    results = []
    for (_, parts), row, top, total in zip(problems, weights, tops, totals):
        blended = 0.0
        for (_, values, _), weight in zip(parts, row):
            blended = blended + jnp.dot(
                weight.astype(jnp.bfloat16), values, preferred_element_type=jnp.float32
            )
        results.append((blended / total, top * LOG2_SCALE + jnp.log2(total)))
    return results


def attend_heads(group, blocks, problem, out):
    rows = blocks * BS
    heads = range(*group)
    lanes = lax.broadcasted_iota(jnp.int32, (rows, DH), 1)
    stats = jnp.zeros((rows, DH), jnp.float32)
    items = [(place, head, block) for place, head in enumerate(heads) for block in range(blocks)]
    sums = {}
    for at in range(0, len(items), BATCH):
        chunk = items[at : at + BATCH]
        results = attend([problem(head, block) for _, head, block in chunk])
        for (place, head, block), (blended, logsum) in zip(chunk, results):
            out[block * BS : (block + 1) * BS, head_cols(place)] = blended.astype(out.dtype)
            sums[place, block] = logsum
    for place in range(len(heads)):
        column = jnp.concatenate([sums[place, block] for block in range(blocks)], axis=0)
        stats = jnp.where(lanes == place, column, stats)
    return stats


def head_cols(head):
    return slice(head * DH, (head + 1) * DH)


def stat_rows(heads):
    return (4, 16) if heads <= 4 else (8, 32)


def write_stats(out, stats, heads):
    pad, count = stat_rows(heads)
    rows = stats.shape[0]
    packed, rest = 0.0, stats
    for part in range(3):
        piece = rest.astype(jnp.bfloat16).astype(jnp.float32)
        rest = rest - piece
        packed = packed + (pltpu.roll(piece, part * pad, 1) if part else piece)
    out[rows:, :] = jnp.zeros((count, out.shape[1]), out.dtype)
    out[rows:, :rows] = packed.T[:count].astype(out.dtype)


def read_stats(ref, heads):
    pad, count = stat_rows(heads)
    rows = ref.shape[0] - count
    packed = ref[rows:, :rows].astype(jnp.float32)
    padding = jnp.zeros((DH - count, rows), jnp.float32)
    packed = jnp.concatenate([packed, padding], axis=0).T
    return packed + pltpu.roll(packed, DH - pad, 1) + pltpu.roll(packed, DH - 2 * pad, 1)


def pair(ref, col, block):
    rows = ref.shape[0] // 2
    cols = head_cols(col)
    return (
        ref[block * BS : (block + 1) * BS, cols],
        ref[rows + block * BS : rows + (block + 1) * BS, cols],
    )


class Buffers:
    def __init__(self, refs):
        self.refs = refs

    def cross(self, head, block):
        return pair(self.refs["major2"], head, block)

    def far(self, head, block):
        return pair(self.refs["major4"], head, block)

    def away(self, head, block):
        if head < 6:
            return pair(self.refs["major1"], head, block)
        return pair(self.refs["major3"], head - 6, block)

    def near(self, head, block):
        if head < 9:
            return pair(self.refs["minor1"], head - 3, block)
        return pair(self.refs["minor2"], head - 9, block)

    def near_first(self, head):
        return pair(self.refs["nearest"], head - 3, 0)

    def cross_first(self, head):
        return pair(self.refs["nearest"], 9 + head, 0)

    def relay(self, head, block):
        if head < 9:
            return pair(self.refs["minor3"], head - 3, block)
        return pair(self.refs["minor4"], head - 9, block)


def partner_kernel(group, names, table_ref, query, keys, values, sib_keys, sib_values, *rest):
    frame, sign = frame_ids()
    buffers = Buffers(dict(zip(names, rest)))
    out = rest[-1]
    rows = query.shape[0]
    blocks = rows // BS
    partner = frame + sign
    own_count = entry(table_ref, partner, frame)
    near_count = entry(table_ref, partner, frame + 2 * sign)
    away_valid = entry(table_ref, partner, frame - 2 * sign) > 0
    relay_valid = entry(table_ref, partner, frame + 4 * sign) > 0
    cross_valid = entry(table_ref, partner, frame - sign) > 0

    def problem(head, block):
        mine = slice(block * BS, (block + 1) * BS)
        cols = head_cols(head)
        last = block + 1 == blocks
        parts = [(keys[mine, cols], values[mine, cols], None)]
        if last:
            parts.append((sib_keys[:BS, cols], sib_values[:BS, cols], own_count > 1))
        else:
            after = slice((block + 1) * BS, (block + 2) * BS)
            parts.append((keys[after, cols], values[after, cols], own_count > 1))
        parts.append((*buffers.away(head, block), away_valid))
        if head < CROSS:
            parts.append((*buffers.cross(head, block), cross_valid))
        else:
            parts.append((*buffers.near(head, block), near_count > 0))
            after = buffers.near_first(head) if last else buffers.near(head, block + 1)
            parts.append((*after, near_count > 1))
            parts.append((*buffers.relay(head, block), relay_valid))
        return query[mine, cols], parts

    stats = attend_heads(group, blocks, problem, out)
    write_stats(out, stats, group[1] - group[0])


def own_kernel(group, names, table_ref, query, keys, values, sib_keys, sib_values, *rest):
    frame, sign = frame_ids()
    buffers = Buffers(dict(zip(names, rest)))
    out, out_stats = rest[-2:]
    rows = query.shape[0]
    blocks = rows // BS
    near_valid = entry(table_ref, frame, frame + 2 * sign) > 0
    away_valid = entry(table_ref, frame, frame - 2 * sign) > 0
    cross_count = entry(table_ref, frame, frame - sign)
    far_valid = entry(table_ref, frame, frame - 3 * sign) > 0

    def problem(head, block):
        mine = slice(block * BS, (block + 1) * BS)
        cols = head_cols(head)
        parts = [
            (keys[:, cols], values[:, cols], None),
            (sib_keys[:, cols], sib_values[:, cols], None),
            (*buffers.away(head, block), away_valid),
        ]
        if head < CROSS:
            last = block + 1 == blocks
            parts.append((*buffers.cross(head, block), cross_count > 0))
            after = buffers.cross_first(head) if last else buffers.cross(head, block + 1)
            parts.append((*after, cross_count > 1))
            parts.append((*buffers.far(head, block), far_valid))
        else:
            parts.append((*buffers.near(head, block), near_valid))
        return query[mine, cols], parts

    out_stats[...] = attend_heads(group, blocks, problem, out)


def project_kernel(own_groups, part_groups, chunks, *refs):
    refs = list(refs)
    weights = [refs.pop(0) for _ in range(chunks)]
    sib_weights = [refs.pop(0) for _ in range(chunks)]
    owns = [(group, refs.pop(0), refs.pop(0)) for group in own_groups]
    parts = [(group, refs.pop(0)) for group in part_groups]
    out, attended = refs
    rows = out.shape[0]
    lanes = lax.broadcasted_iota(jnp.int32, (rows, DH), 1)
    own_at, part_at = {}, {}
    own_sum = part_sum = jnp.zeros((rows, DH), jnp.float32)
    for (first, last), own, stats in owns:
        shifted = pltpu.roll(stats[...], first, 1) if first else stats[...]
        own_sum = jnp.where((lanes >= first) & (lanes < last), shifted, own_sum)
        own_at.update({head: (own, head - first) for head in range(first, last)})
    for (first, last), part in parts:
        stats = read_stats(part, last - first)
        shifted = pltpu.roll(stats, first, 1) if first else stats
        part_sum = jnp.where((lanes >= first) & (lanes < last), shifted, part_sum)
        part_at.update({head: (part, head - first) for head in range(first, last)})
    top = jnp.maximum(own_sum, part_sum)
    own_weight = jnp.exp2(own_sum - top)
    part_weight = jnp.exp2(part_sum - top)
    inverse = 1.0 / (own_weight + part_weight)
    own_weight = own_weight * inverse
    part_weight = part_weight * inverse
    for head in sorted(own_at):
        own, own_place = own_at[head]
        part, part_place = part_at[head]
        mixed = own_weight[:, head : head + 1] * own[:, head_cols(own_place)] + part_weight[
            :, head : head + 1
        ] * part[:rows, head_cols(part_place)].astype(jnp.float32)
        attended[:, head_cols(head)] = mixed.astype(attended.dtype)
    core = lax.axis_index("head")
    chunk = weights[0].shape[0]
    pieces = []
    for index in range(chunks):
        for weight, side in ((weights[index], core), (sib_weights[index], 1 - core)):
            at = pl.multiple_of((side * chunks + index) * chunk, DH)
            pieces.append((attended[:, pl.ds(at, chunk)], weight))
    for at in range(0, out.shape[1], TILE):
        product = 0.0
        for piece, weight in pieces:
            product = product + jnp.dot(
                piece, weight[:, at : at + TILE], preferred_element_type=jnp.float32
            )
        out[:, at : at + TILE] = product.astype(out.dtype)


def whole(shape):
    return pl.BlockSpec(shape, lambda i: (0,) * len(shape))


def run(body, name, table, operands, out_shapes, flops, after=()):
    return pl.pallas_call(
        body,
        grid=(1,),
        in_specs=[pl.BlockSpec(memory_space=pltpu.SMEM)]
        + [whole(x.shape) for x in operands]
        + [pl.BlockSpec(memory_space=pl.ANY)] * len(after),
        out_specs=[whole(s.shape) for s in out_shapes],
        out_shape=out_shapes,
        compiler_params=pltpu.CompilerParams(vmem_limit_bytes=8 * MIB),
        cost_estimate=pl.CostEstimate(
            flops=flops, bytes_accessed=MIB, transcendentals=flops // 512
        ),
        name=name,
    )(table, *operands, *after)


def tie_kernel(*refs):
    del refs


def tie(before, *payloads):
    before = tuple(before)
    anywhere = pl.BlockSpec(memory_space=pl.ANY)
    return pl.pallas_call(
        tie_kernel,
        in_specs=[anywhere] * (len(before) + len(payloads)),
        out_specs=[anywhere] * len(payloads),
        out_shape=[jax.ShapeDtypeStruct(p.shape, p.dtype) for p in payloads],
        input_output_aliases={len(before) + i: i for i in range(len(payloads))},
        compiler_params=pltpu.CompilerParams(vmem_limit_bytes=MIB),
        name="tie",
    )(*before, *payloads)


def project(own_groups, part_groups, weights, operands):
    rows, columns = operands[0].shape[0], weights[0].shape[1]
    depth = sum(weight.shape[0] for weight in weights)
    return pl.pallas_call(
        functools.partial(project_kernel, own_groups, part_groups, len(weights) // 2),
        grid=(1,),
        in_specs=[whole(x.shape) for x in (*weights, *operands)],
        out_specs=whole((rows, columns)),
        out_shape=jax.ShapeDtypeStruct((rows, columns), jnp.bfloat16),
        scratch_shapes=[pltpu.VMEM((rows, depth), jnp.bfloat16)],
        compiler_params=pltpu.CompilerParams(vmem_limit_bytes=8 * MIB),
        cost_estimate=pl.CostEstimate(
            flops=2 * rows * depth * columns, bytes_accessed=12 * MIB, transcendentals=0
        ),
        name="merge_and_project",
    )(*weights, *operands)


def per_device(queries, key_tokens, value_tokens, radial_table, out_weight):
    frames = lax.axis_size("frame")
    cores = lax.axis_size("head")
    rows = queries.shape[0]

    def moves(target):
        return [(f, target(f)) for f in range(frames) if 0 <= target(f) < frames]

    partner_moves = moves(lambda f: f ^ 1)
    near_moves = moves(lambda f: f - 2 if f % 2 == 0 else f + 2)
    away_moves = moves(lambda f: f + 2 if f % 2 == 0 else f - 2)
    cross_moves = moves(lambda f: f - 1 if f % 2 == 0 else f + 1)
    core_moves = [(c, cores - 1 - c) for c in range(cores)]

    def pack(first, last):
        cols = slice(first * DH, last * DH)
        return jnp.concatenate([key_tokens[:, cols], value_tokens[:, cols]], axis=0)

    def firsts(*packed):
        return jnp.concatenate(
            [jnp.concatenate([p[at : at + BS] for p in packed], axis=1) for at in (0, rows)],
            axis=0,
        )

    major1 = lax.ppermute(pack(0, 6), "frame", away_moves)
    minor1 = lax.ppermute(pack(3, 9), "frame", near_moves)
    own_weight = [out_weight]
    sib_weight = [lax.ppermute(out_weight, "head", core_moves)]
    cross = lax.ppermute(pack(0, 3), "frame", partner_moves)
    (to_minor2,) = tie((cross, *sib_weight), pack(9, 12))
    minor2 = lax.ppermute(to_minor2, "frame", near_moves)
    (to_partner,) = tie(sib_weight, queries)
    partner_query = lax.ppermute(to_partner, "frame", partner_moves)
    major2 = lax.ppermute(cross, "frame", away_moves)
    minor3 = lax.ppermute(minor1, "frame", near_moves)
    (to_major3,) = tie((major1,), pack(6, 12))
    major3 = lax.ppermute(to_major3, "frame", away_moves)
    major4 = lax.ppermute(major2, "frame", away_moves)
    minor4 = lax.ppermute(minor2, "frame", near_moves)
    to_sib_keys, to_sib_values = tie((minor2,), key_tokens, value_tokens)
    sib_keys = lax.ppermute(to_sib_keys, "head", core_moves)
    sib_values = lax.ppermute(to_sib_values, "head", core_moves)
    (to_nearest,) = tie((partner_query,), firsts(minor1, minor2, major2))
    nearest = lax.ppermute(to_nearest, "head", core_moves)
    refs = {
        "major1": major1,
        "major2": major2,
        "major3": major3,
        "major4": major4,
        "minor1": minor1,
        "minor2": minor2,
        "minor3": minor3,
        "minor4": minor4,
        "nearest": nearest,
    }
    local = (key_tokens, value_tokens, sib_keys, sib_values)

    def partner_part(group, names, after=()):
        heads = group[1] - group[0]
        shape = jax.ShapeDtypeStruct((rows + stat_rows(heads)[1], heads * DH), jnp.bfloat16)
        (part,) = run(
            functools.partial(partner_kernel, group, names),
            "partner_part",
            radial_table,
            (partner_query, *local, *(refs[n] for n in names)),
            [shape],
            heads * rows * 6 * BS * DH * 4,
            after,
        )
        return part

    def own_part(group, names, after=()):
        heads = group[1] - group[0]
        return run(
            functools.partial(own_kernel, group, names),
            "own_part",
            radial_table,
            (queries, *local, *(refs[n] for n in names)),
            [
                jax.ShapeDtypeStruct((rows, heads * DH), jnp.float32),
                jax.ShapeDtypeStruct((rows, DH), jnp.float32),
            ],
            heads * rows * 6 * BS * DH * 4,
            after,
        )

    own_groups = ((0, 3), (3, 6), (6, 12))
    part_groups = ((0, 3), (3, 9), (9, 12))
    part_low = partner_part((0, 3), ("major1", "major2"))
    own_early = own_part((3, 6), ("major1", "minor1"))
    part_middle = partner_part(
        (3, 9), ("major1", "major3", "minor1", "minor3", "nearest"), (part_low, own_early[1])
    )
    part_low = lax.ppermute(part_low, "frame", partner_moves)
    part_middle = lax.ppermute(part_middle, "frame", partner_moves)
    own_late = own_part((6, 12), ("major3", "minor1", "minor2"))
    part_high = partner_part(
        (9, 12), ("major3", "minor2", "minor4", "nearest"), (own_late[1], major4, part_low, *sib_weight)
    )
    part_high = lax.ppermute(part_high, "frame", partner_moves)
    own_low = own_part((0, 3), ("major1", "major2", "major4", "nearest"))
    return project(
        own_groups,
        part_groups,
        (*own_weight, *sib_weight),
        (*own_low, *own_early, *own_late, part_low, part_middle, part_high),
    )


def solution(mesh):
    in_specs = (
        P(("clip", "frame", "head"), None),
        P(("clip", "frame", "head"), None),
        P(("clip", "frame", "head"), None),
        P(),
        P("head", None),
    )
    out_specs = P(("clip", "frame", "head"), None)
    return jax.shard_map(
        per_device, mesh=mesh, in_specs=in_specs, out_specs=out_specs, check_vma=False
    )
```

```python
import functools
import math

import jax
import jax.numpy as jnp
from jax import lax
from jax.experimental import pallas as pl
from jax.experimental.pallas import tpu as pltpu
from jax.sharding import PartitionSpec as P

DH = 128
BS = 128
CROSS = 3
BATCH = 4
TILE = 768
NEG = -1e30
LOG2_SCALE = math.log2(math.e) / math.sqrt(DH)
MIB = 1024 * 1024


def frame_ids():
    frame = lax.axis_index("frame")
    return frame, 1 - 2 * lax.rem(frame, 2)


def entry(table_ref, query_frame, key_frame):
    frames = table_ref.shape[0]
    inside = (key_frame >= 0) & (key_frame < frames)
    count = table_ref[query_frame, jnp.clip(key_frame, 0, frames - 1)]
    return jnp.where(inside, count, 0)


def attend(problems):
    scores = []
    for query, parts in problems:
        row = []
        for keys, _, valid in parts:
            raw = lax.dot_general(
                query, keys, (((1,), (1,)), ((), ())), preferred_element_type=jnp.float32
            )
            row.append(raw if valid is None else jnp.where(valid, raw, NEG))
        scores.append(row)
    tops = []
    for row in scores:
        best = None
        for raw in row:
            for at in range(0, raw.shape[1], BS):
                piece = raw[:, at : at + BS]
                best = piece if best is None else jnp.maximum(best, piece)
        tops.append(best.max(axis=1, keepdims=True))
    weights = [
        [jnp.exp2((raw - top) * LOG2_SCALE) for raw in row] for row, top in zip(scores, tops)
    ]
    totals = []
    for row in weights:
        total = None
        for weight in row:
            for at in range(0, weight.shape[1], BS):
                piece = weight[:, at : at + BS]
                total = piece if total is None else total + piece
        totals.append(total.sum(axis=1, keepdims=True))
    results = []
    for (_, parts), row, top, total in zip(problems, weights, tops, totals):
        blended = 0.0
        for (_, values, _), weight in zip(parts, row):
            blended = blended + jnp.dot(
                weight.astype(jnp.bfloat16), values, preferred_element_type=jnp.float32
            )
        results.append((blended / total, top * LOG2_SCALE + jnp.log2(total)))
    return results


def attend_heads(group, blocks, problem, out):
    rows = blocks * BS
    heads = range(*group)
    lanes = lax.broadcasted_iota(jnp.int32, (rows, DH), 1)
    stats = jnp.zeros((rows, DH), jnp.float32)
    items = [(place, head, block) for place, head in enumerate(heads) for block in range(blocks)]
    sums = {}
    for at in range(0, len(items), BATCH):
        chunk = items[at : at + BATCH]
        results = attend([problem(head, block) for _, head, block in chunk])
        for (place, head, block), (blended, logsum) in zip(chunk, results):
            out[block * BS : (block + 1) * BS, head_cols(place)] = blended.astype(out.dtype)
            sums[place, block] = logsum
    for place in range(len(heads)):
        column = jnp.concatenate([sums[place, block] for block in range(blocks)], axis=0)
        stats = jnp.where(lanes == place, column, stats)
    return stats


def head_cols(head):
    return slice(head * DH, (head + 1) * DH)


def stat_rows(heads):
    return (4, 16) if heads <= 4 else (8, 32)


def write_stats(out, stats, heads):
    pad, count = stat_rows(heads)
    rows = stats.shape[0]
    packed, rest = 0.0, stats
    for part in range(3):
        piece = rest.astype(jnp.bfloat16).astype(jnp.float32)
        rest = rest - piece
        packed = packed + (pltpu.roll(piece, part * pad, 1) if part else piece)
    out[rows:, :] = jnp.zeros((count, out.shape[1]), out.dtype)
    out[rows:, :rows] = packed.T[:count].astype(out.dtype)


def read_stats(ref, heads):
    pad, count = stat_rows(heads)
    rows = ref.shape[0] - count
    packed = ref[rows:, :rows].astype(jnp.float32)
    padding = jnp.zeros((DH - count, rows), jnp.float32)
    packed = jnp.concatenate([packed, padding], axis=0).T
    return packed + pltpu.roll(packed, DH - pad, 1) + pltpu.roll(packed, DH - 2 * pad, 1)


def pair(ref, col, block):
    rows = ref.shape[0] // 2
    cols = head_cols(col)
    return (
        ref[block * BS : (block + 1) * BS, cols],
        ref[rows + block * BS : rows + (block + 1) * BS, cols],
    )


class Buffers:
    def __init__(self, refs):
        self.refs = refs

    def cross(self, head, block):
        return pair(self.refs["major2"], head, block)

    def far(self, head, block):
        return pair(self.refs["major4"], head, block)

    def away(self, head, block):
        if head < 6:
            return pair(self.refs["major1"], head, block)
        return pair(self.refs["major3"], head - 6, block)

    def near(self, head, block):
        if head < 9:
            return pair(self.refs["minor1"], head - 3, block)
        return pair(self.refs["minor2"], head - 9, block)

    def near_first(self, head):
        return pair(self.refs["nearest"], head - 3, 0)

    def cross_first(self, head):
        return pair(self.refs["nearest"], 9 + head, 0)

    def relay(self, head, block):
        if head < 9:
            return pair(self.refs["minor3"], head - 3, block)
        return pair(self.refs["minor4"], head - 9, block)


def partner_kernel(group, names, table_ref, query, keys, values, sib_keys, sib_values, *rest):
    frame, sign = frame_ids()
    buffers = Buffers(dict(zip(names, rest)))
    out = rest[-1]
    rows = query.shape[0]
    blocks = rows // BS
    partner = frame + sign
    own_count = entry(table_ref, partner, frame)
    near_count = entry(table_ref, partner, frame + 2 * sign)
    away_valid = entry(table_ref, partner, frame - 2 * sign) > 0
    relay_valid = entry(table_ref, partner, frame + 4 * sign) > 0
    cross_valid = entry(table_ref, partner, frame - sign) > 0

    def problem(head, block):
        mine = slice(block * BS, (block + 1) * BS)
        cols = head_cols(head)
        last = block + 1 == blocks
        parts = [(keys[mine, cols], values[mine, cols], None)]
        if last:
            parts.append((sib_keys[:BS, cols], sib_values[:BS, cols], own_count > 1))
        else:
            after = slice((block + 1) * BS, (block + 2) * BS)
            parts.append((keys[after, cols], values[after, cols], own_count > 1))
        parts.append((*buffers.away(head, block), away_valid))
        if head < CROSS:
            parts.append((*buffers.cross(head, block), cross_valid))
        else:
            parts.append((*buffers.near(head, block), near_count > 0))
            after = buffers.near_first(head) if last else buffers.near(head, block + 1)
            parts.append((*after, near_count > 1))
            parts.append((*buffers.relay(head, block), relay_valid))
        return query[mine, cols], parts

    stats = attend_heads(group, blocks, problem, out)
    write_stats(out, stats, group[1] - group[0])


def own_kernel(group, names, table_ref, query, keys, values, sib_keys, sib_values, *rest):
    frame, sign = frame_ids()
    buffers = Buffers(dict(zip(names, rest)))
    out, out_stats = rest[-2:]
    rows = query.shape[0]
    blocks = rows // BS
    near_valid = entry(table_ref, frame, frame + 2 * sign) > 0
    away_valid = entry(table_ref, frame, frame - 2 * sign) > 0
    cross_count = entry(table_ref, frame, frame - sign)
    far_valid = entry(table_ref, frame, frame - 3 * sign) > 0

    def problem(head, block):
        mine = slice(block * BS, (block + 1) * BS)
        cols = head_cols(head)
        parts = [
            (keys[:, cols], values[:, cols], None),
            (sib_keys[:, cols], sib_values[:, cols], None),
            (*buffers.away(head, block), away_valid),
        ]
        if head < CROSS:
            last = block + 1 == blocks
            parts.append((*buffers.cross(head, block), cross_count > 0))
            after = buffers.cross_first(head) if last else buffers.cross(head, block + 1)
            parts.append((*after, cross_count > 1))
            parts.append((*buffers.far(head, block), far_valid))
        else:
            parts.append((*buffers.near(head, block), near_valid))
        return query[mine, cols], parts

    out_stats[...] = attend_heads(group, blocks, problem, out)


def project_kernel(own_groups, part_groups, chunks, *refs):
    refs = list(refs)
    weights = [refs.pop(0) for _ in range(chunks)]
    sib_weights = [refs.pop(0) for _ in range(chunks)]
    owns = [(group, refs.pop(0), refs.pop(0)) for group in own_groups]
    parts = [(group, refs.pop(0)) for group in part_groups]
    out, attended = refs
    rows = out.shape[0]
    lanes = lax.broadcasted_iota(jnp.int32, (rows, DH), 1)
    own_at, part_at = {}, {}
    own_sum = part_sum = jnp.zeros((rows, DH), jnp.float32)
    for (first, last), own, stats in owns:
        shifted = pltpu.roll(stats[...], first, 1) if first else stats[...]
        own_sum = jnp.where((lanes >= first) & (lanes < last), shifted, own_sum)
        own_at.update({head: (own, head - first) for head in range(first, last)})
    for (first, last), part in parts:
        stats = read_stats(part, last - first)
        shifted = pltpu.roll(stats, first, 1) if first else stats
        part_sum = jnp.where((lanes >= first) & (lanes < last), shifted, part_sum)
        part_at.update({head: (part, head - first) for head in range(first, last)})
    top = jnp.maximum(own_sum, part_sum)
    own_weight = jnp.exp2(own_sum - top)
    part_weight = jnp.exp2(part_sum - top)
    inverse = 1.0 / (own_weight + part_weight)
    own_weight = own_weight * inverse
    part_weight = part_weight * inverse
    for head in sorted(own_at):
        own, own_place = own_at[head]
        part, part_place = part_at[head]
        mixed = own_weight[:, head : head + 1] * own[:, head_cols(own_place)] + part_weight[
            :, head : head + 1
        ] * part[:rows, head_cols(part_place)].astype(jnp.float32)
        attended[:, head_cols(head)] = mixed.astype(attended.dtype)
    core = lax.axis_index("head")
    chunk = weights[0].shape[0]
    pieces = []
    for index in range(chunks):
        for weight, side in ((weights[index], core), (sib_weights[index], 1 - core)):
            at = pl.multiple_of((side * chunks + index) * chunk, DH)
            pieces.append((attended[:, pl.ds(at, chunk)], weight))
    for at in range(0, out.shape[1], TILE):
        product = 0.0
        for piece, weight in pieces:
            product = product + jnp.dot(
                piece, weight[:, at : at + TILE], preferred_element_type=jnp.float32
            )
        out[:, at : at + TILE] = product.astype(out.dtype)


def whole(shape):
    return pl.BlockSpec(shape, lambda i: (0,) * len(shape))


def run(body, name, table, operands, out_shapes, flops, after=()):
    return pl.pallas_call(
        body,
        grid=(1,),
        in_specs=[pl.BlockSpec(memory_space=pltpu.SMEM)]
        + [whole(x.shape) for x in operands]
        + [pl.BlockSpec(memory_space=pl.ANY)] * len(after),
        out_specs=[whole(s.shape) for s in out_shapes],
        out_shape=out_shapes,
        compiler_params=pltpu.CompilerParams(vmem_limit_bytes=8 * MIB),
        cost_estimate=pl.CostEstimate(
            flops=flops, bytes_accessed=MIB, transcendentals=flops // 512
        ),
        name=name,
    )(table, *operands, *after)


def tie_kernel(*refs):
    del refs


def tie(before, *payloads):
    before = tuple(before)
    anywhere = pl.BlockSpec(memory_space=pl.ANY)
    return pl.pallas_call(
        tie_kernel,
        in_specs=[anywhere] * (len(before) + len(payloads)),
        out_specs=[anywhere] * len(payloads),
        out_shape=[jax.ShapeDtypeStruct(p.shape, p.dtype) for p in payloads],
        input_output_aliases={len(before) + i: i for i in range(len(payloads))},
        compiler_params=pltpu.CompilerParams(vmem_limit_bytes=MIB),
        name="tie",
    )(*before, *payloads)


def project(own_groups, part_groups, weights, operands):
    rows, columns = operands[0].shape[0], weights[0].shape[1]
    depth = sum(weight.shape[0] for weight in weights)
    return pl.pallas_call(
        functools.partial(project_kernel, own_groups, part_groups, len(weights) // 2),
        grid=(1,),
        in_specs=[whole(x.shape) for x in (*weights, *operands)],
        out_specs=whole((rows, columns)),
        out_shape=jax.ShapeDtypeStruct((rows, columns), jnp.bfloat16),
        scratch_shapes=[pltpu.VMEM((rows, depth), jnp.bfloat16)],
        compiler_params=pltpu.CompilerParams(vmem_limit_bytes=8 * MIB),
        cost_estimate=pl.CostEstimate(
            flops=2 * rows * depth * columns, bytes_accessed=12 * MIB, transcendentals=0
        ),
        name="merge_and_project",
    )(*weights, *operands)


def per_device(queries, key_tokens, value_tokens, radial_table, out_weight):
    frames = lax.axis_size("frame")
    cores = lax.axis_size("head")
    rows = queries.shape[0]

    def moves(target):
        return [(f, target(f)) for f in range(frames) if 0 <= target(f) < frames]

    partner_moves = moves(lambda f: f ^ 1)
    near_moves = moves(lambda f: f - 2 if f % 2 == 0 else f + 2)
    away_moves = moves(lambda f: f + 2 if f % 2 == 0 else f - 2)
    cross_moves = moves(lambda f: f - 1 if f % 2 == 0 else f + 1)
    core_moves = [(c, cores - 1 - c) for c in range(cores)]

    def pack(first, last):
        cols = slice(first * DH, last * DH)
        return jnp.concatenate([key_tokens[:, cols], value_tokens[:, cols]], axis=0)

    def firsts(*packed):
        return jnp.concatenate(
            [jnp.concatenate([p[at : at + BS] for p in packed], axis=1) for at in (0, rows)],
            axis=0,
        )

    major1 = lax.ppermute(pack(0, 6), "frame", away_moves)
    minor1 = lax.ppermute(pack(3, 9), "frame", near_moves)
    own_weight = [out_weight]
    sib_weight = [lax.ppermute(out_weight, "head", core_moves)]
    cross = lax.ppermute(pack(0, 3), "frame", partner_moves)
    cross, to_minor2 = tie(sib_weight, cross, pack(9, 12))
    minor2 = lax.ppermute(to_minor2, "frame", near_moves)
    partner_query = lax.ppermute(queries, "frame", partner_moves)
    major2 = lax.ppermute(cross, "frame", away_moves)
    minor3 = lax.ppermute(minor1, "frame", near_moves)
    (to_major3,) = tie((major1,), pack(6, 12))
    major3 = lax.ppermute(to_major3, "frame", away_moves)
    major4 = lax.ppermute(major2, "frame", away_moves)
    minor4 = lax.ppermute(minor2, "frame", near_moves)
    to_sib_keys, to_sib_values = tie((major2,), key_tokens, value_tokens)
    sib_keys = lax.ppermute(to_sib_keys, "head", core_moves)
    sib_values = lax.ppermute(to_sib_values, "head", core_moves)
    nearest = lax.ppermute(firsts(minor1, minor2, major2), "head", core_moves)
    refs = {
        "major1": major1,
        "major2": major2,
        "major3": major3,
        "major4": major4,
        "minor1": minor1,
        "minor2": minor2,
        "minor3": minor3,
        "minor4": minor4,
        "nearest": nearest,
    }
    local = (key_tokens, value_tokens, sib_keys, sib_values)

    def partner_part(group, names, after=()):
        heads = group[1] - group[0]
        shape = jax.ShapeDtypeStruct((rows + stat_rows(heads)[1], heads * DH), jnp.bfloat16)
        (part,) = run(
            functools.partial(partner_kernel, group, names),
            "partner_part",
            radial_table,
            (partner_query, *local, *(refs[n] for n in names)),
            [shape],
            heads * rows * 6 * BS * DH * 4,
            after,
        )
        return part

    def own_part(group, names, after=()):
        heads = group[1] - group[0]
        return run(
            functools.partial(own_kernel, group, names),
            "own_part",
            radial_table,
            (queries, *local, *(refs[n] for n in names)),
            [
                jax.ShapeDtypeStruct((rows, heads * DH), jnp.float32),
                jax.ShapeDtypeStruct((rows, DH), jnp.float32),
            ],
            heads * rows * 6 * BS * DH * 4,
            after,
        )

    own_groups = ((0, 3), (3, 6), (6, 12))
    part_groups = ((0, 3), (3, 9), (9, 12))
    part_low = partner_part((0, 3), ("major1", "major2"))
    own_early = own_part((3, 6), ("major1", "minor1"))
    part_middle = partner_part(
        (3, 9), ("major1", "major3", "minor1", "minor3", "nearest"), (part_low, own_early[1])
    )
    part_low = lax.ppermute(part_low, "frame", partner_moves)
    part_middle = lax.ppermute(part_middle, "frame", partner_moves)
    own_late = own_part((6, 12), ("major3", "minor1", "minor2"))
    part_high = partner_part(
        (9, 12), ("major3", "minor2", "minor4", "nearest"), (own_late[1], major4, part_low, *sib_weight)
    )
    part_high = lax.ppermute(part_high, "frame", partner_moves)
    own_low = own_part((0, 3), ("major1", "major2", "major4", "nearest"))
    return project(
        own_groups,
        part_groups,
        (*own_weight, *sib_weight),
        (*own_low, *own_early, *own_late, part_low, part_middle, part_high),
    )


def solution(mesh):
    in_specs = (
        P(("clip", "frame", "head"), None),
        P(("clip", "frame", "head"), None),
        P(("clip", "frame", "head"), None),
        P(),
        P("head", None),
    )
    out_specs = P(("clip", "frame", "head"), None)
    return jax.shard_map(
        per_device, mesh=mesh, in_specs=in_specs, out_specs=out_specs, check_vma=False
    )
```

```python
import functools
import math

import jax
import jax.numpy as jnp
from jax import lax
from jax.experimental import pallas as pl
from jax.experimental.pallas import tpu as pltpu
from jax.sharding import PartitionSpec as P

DH = 128
BS = 128
CROSS = 3
BATCH = 4
TILE = 768
NEG = -1e30
LOG2_SCALE = math.log2(math.e) / math.sqrt(DH)
MIB = 1024 * 1024


def frame_ids():
    frame = lax.axis_index("frame")
    return frame, 1 - 2 * lax.rem(frame, 2)


def entry(table_ref, query_frame, key_frame):
    frames = table_ref.shape[0]
    inside = (key_frame >= 0) & (key_frame < frames)
    count = table_ref[query_frame, jnp.clip(key_frame, 0, frames - 1)]
    return jnp.where(inside, count, 0)


def attend(problems):
    scores = []
    for query, parts in problems:
        row = []
        for keys, _, valid in parts:
            raw = lax.dot_general(
                query, keys, (((1,), (1,)), ((), ())), preferred_element_type=jnp.float32
            )
            row.append(raw if valid is None else jnp.where(valid, raw, NEG))
        scores.append(row)
    tops = []
    for row in scores:
        best = None
        for raw in row:
            for at in range(0, raw.shape[1], BS):
                piece = raw[:, at : at + BS]
                best = piece if best is None else jnp.maximum(best, piece)
        tops.append(best.max(axis=1, keepdims=True))
    weights = [
        [jnp.exp2((raw - top) * LOG2_SCALE) for raw in row] for row, top in zip(scores, tops)
    ]
    totals = []
    for row in weights:
        total = None
        for weight in row:
            for at in range(0, weight.shape[1], BS):
                piece = weight[:, at : at + BS]
                total = piece if total is None else total + piece
        totals.append(total.sum(axis=1, keepdims=True))
    results = []
    for (_, parts), row, top, total in zip(problems, weights, tops, totals):
        blended = 0.0
        for (_, values, _), weight in zip(parts, row):
            blended = blended + jnp.dot(
                weight.astype(jnp.bfloat16), values, preferred_element_type=jnp.float32
            )
        results.append((blended / total, top * LOG2_SCALE + jnp.log2(total)))
    return results


def attend_heads(group, blocks, problem, out):
    rows = blocks * BS
    heads = range(*group)
    lanes = lax.broadcasted_iota(jnp.int32, (rows, DH), 1)
    stats = jnp.zeros((rows, DH), jnp.float32)
    items = [(place, head, block) for place, head in enumerate(heads) for block in range(blocks)]
    sums = {}
    for at in range(0, len(items), BATCH):
        chunk = items[at : at + BATCH]
        results = attend([problem(head, block) for _, head, block in chunk])
        for (place, head, block), (blended, logsum) in zip(chunk, results):
            out[block * BS : (block + 1) * BS, head_cols(place)] = blended.astype(out.dtype)
            sums[place, block] = logsum
    for place in range(len(heads)):
        column = jnp.concatenate([sums[place, block] for block in range(blocks)], axis=0)
        stats = jnp.where(lanes == place, column, stats)
    return stats


def head_cols(head):
    return slice(head * DH, (head + 1) * DH)


def stat_rows(heads):
    return (4, 16) if heads <= 4 else (8, 32)


def write_stats(out, stats, heads):
    pad, count = stat_rows(heads)
    rows = stats.shape[0]
    packed, rest = 0.0, stats
    for part in range(3):
        piece = rest.astype(jnp.bfloat16).astype(jnp.float32)
        rest = rest - piece
        packed = packed + (pltpu.roll(piece, part * pad, 1) if part else piece)
    out[rows:, :] = jnp.zeros((count, out.shape[1]), out.dtype)
    out[rows:, :rows] = packed.T[:count].astype(out.dtype)


def read_stats(ref, heads):
    pad, count = stat_rows(heads)
    rows = ref.shape[0] - count
    packed = ref[rows:, :rows].astype(jnp.float32)
    padding = jnp.zeros((DH - count, rows), jnp.float32)
    packed = jnp.concatenate([packed, padding], axis=0).T
    return packed + pltpu.roll(packed, DH - pad, 1) + pltpu.roll(packed, DH - 2 * pad, 1)


def pair(ref, col, block):
    rows = ref.shape[0] // 2
    cols = head_cols(col)
    return (
        ref[block * BS : (block + 1) * BS, cols],
        ref[rows + block * BS : rows + (block + 1) * BS, cols],
    )


class Buffers:
    def __init__(self, refs):
        self.refs = refs

    def cross(self, head, block):
        return pair(self.refs["major2"], head, block)

    def far(self, head, block):
        return pair(self.refs["major4"], head, block)

    def away(self, head, block):
        if head < 6:
            return pair(self.refs["major1"], head, block)
        return pair(self.refs["major3"], head - 6, block)

    def near(self, head, block):
        if head < 9:
            return pair(self.refs["minor1"], head - 3, block)
        return pair(self.refs["minor2"], head - 9, block)

    def near_first(self, head):
        return pair(self.refs["nearest"], head - 3, 0)

    def cross_first(self, head):
        return pair(self.refs["nearest"], 9 + head, 0)

    def relay(self, head, block):
        if head < 9:
            return pair(self.refs["minor3"], head - 3, block)
        return pair(self.refs["minor4"], head - 9, block)


def partner_kernel(group, names, table_ref, query, keys, values, sib_keys, sib_values, *rest):
    frame, sign = frame_ids()
    buffers = Buffers(dict(zip(names, rest)))
    out = rest[-1]
    rows = query.shape[0]
    blocks = rows // BS
    partner = frame + sign
    own_count = entry(table_ref, partner, frame)
    near_count = entry(table_ref, partner, frame + 2 * sign)
    away_valid = entry(table_ref, partner, frame - 2 * sign) > 0
    relay_valid = entry(table_ref, partner, frame + 4 * sign) > 0
    cross_valid = entry(table_ref, partner, frame - sign) > 0

    def problem(head, block):
        mine = slice(block * BS, (block + 1) * BS)
        cols = head_cols(head)
        last = block + 1 == blocks
        parts = [(keys[mine, cols], values[mine, cols], None)]
        if last:
            parts.append((sib_keys[:BS, cols], sib_values[:BS, cols], own_count > 1))
        else:
            after = slice((block + 1) * BS, (block + 2) * BS)
            parts.append((keys[after, cols], values[after, cols], own_count > 1))
        parts.append((*buffers.away(head, block), away_valid))
        if head < CROSS:
            parts.append((*buffers.cross(head, block), cross_valid))
        else:
            parts.append((*buffers.near(head, block), near_count > 0))
            after = buffers.near_first(head) if last else buffers.near(head, block + 1)
            parts.append((*after, near_count > 1))
            parts.append((*buffers.relay(head, block), relay_valid))
        return query[mine, cols], parts

    stats = attend_heads(group, blocks, problem, out)
    write_stats(out, stats, group[1] - group[0])


def own_kernel(group, names, table_ref, query, keys, values, sib_keys, sib_values, *rest):
    frame, sign = frame_ids()
    buffers = Buffers(dict(zip(names, rest)))
    out, out_stats = rest[-2:]
    rows = query.shape[0]
    blocks = rows // BS
    near_valid = entry(table_ref, frame, frame + 2 * sign) > 0
    away_valid = entry(table_ref, frame, frame - 2 * sign) > 0
    cross_count = entry(table_ref, frame, frame - sign)
    far_valid = entry(table_ref, frame, frame - 3 * sign) > 0

    def problem(head, block):
        mine = slice(block * BS, (block + 1) * BS)
        cols = head_cols(head)
        parts = [
            (keys[:, cols], values[:, cols], None),
            (sib_keys[:, cols], sib_values[:, cols], None),
            (*buffers.away(head, block), away_valid),
        ]
        if head < CROSS:
            last = block + 1 == blocks
            parts.append((*buffers.cross(head, block), cross_count > 0))
            after = buffers.cross_first(head) if last else buffers.cross(head, block + 1)
            parts.append((*after, cross_count > 1))
            parts.append((*buffers.far(head, block), far_valid))
        else:
            parts.append((*buffers.near(head, block), near_valid))
        return query[mine, cols], parts

    out_stats[...] = attend_heads(group, blocks, problem, out)


def project_kernel(own_groups, part_groups, chunks, *refs):
    refs = list(refs)
    weights = [refs.pop(0) for _ in range(chunks)]
    sib_weights = [refs.pop(0) for _ in range(chunks)]
    owns = [(group, refs.pop(0), refs.pop(0)) for group in own_groups]
    parts = [(group, refs.pop(0)) for group in part_groups]
    out, attended = refs
    rows = out.shape[0]
    lanes = lax.broadcasted_iota(jnp.int32, (rows, DH), 1)
    own_at, part_at = {}, {}
    own_sum = part_sum = jnp.zeros((rows, DH), jnp.float32)
    for (first, last), own, stats in owns:
        shifted = pltpu.roll(stats[...], first, 1) if first else stats[...]
        own_sum = jnp.where((lanes >= first) & (lanes < last), shifted, own_sum)
        own_at.update({head: (own, head - first) for head in range(first, last)})
    for (first, last), part in parts:
        stats = read_stats(part, last - first)
        shifted = pltpu.roll(stats, first, 1) if first else stats
        part_sum = jnp.where((lanes >= first) & (lanes < last), shifted, part_sum)
        part_at.update({head: (part, head - first) for head in range(first, last)})
    top = jnp.maximum(own_sum, part_sum)
    own_weight = jnp.exp2(own_sum - top)
    part_weight = jnp.exp2(part_sum - top)
    inverse = 1.0 / (own_weight + part_weight)
    own_weight = own_weight * inverse
    part_weight = part_weight * inverse
    for head in sorted(own_at):
        own, own_place = own_at[head]
        part, part_place = part_at[head]
        mixed = own_weight[:, head : head + 1] * own[:, head_cols(own_place)] + part_weight[
            :, head : head + 1
        ] * part[:rows, head_cols(part_place)].astype(jnp.float32)
        attended[:, head_cols(head)] = mixed.astype(attended.dtype)
    core = lax.axis_index("head")
    chunk = weights[0].shape[0]
    pieces = []
    for index in range(chunks):
        for weight, side in ((weights[index], core), (sib_weights[index], 1 - core)):
            at = pl.multiple_of((side * chunks + index) * chunk, DH)
            pieces.append((attended[:, pl.ds(at, chunk)], weight))
    for at in range(0, out.shape[1], TILE):
        product = 0.0
        for piece, weight in pieces:
            product = product + jnp.dot(
                piece, weight[:, at : at + TILE], preferred_element_type=jnp.float32
            )
        out[:, at : at + TILE] = product.astype(out.dtype)


def whole(shape):
    return pl.BlockSpec(shape, lambda i: (0,) * len(shape))


def run(body, name, table, operands, out_shapes, flops, after=()):
    return pl.pallas_call(
        body,
        grid=(1,),
        in_specs=[pl.BlockSpec(memory_space=pltpu.SMEM)]
        + [whole(x.shape) for x in operands]
        + [pl.BlockSpec(memory_space=pl.ANY)] * len(after),
        out_specs=[whole(s.shape) for s in out_shapes],
        out_shape=out_shapes,
        compiler_params=pltpu.CompilerParams(vmem_limit_bytes=8 * MIB),
        cost_estimate=pl.CostEstimate(
            flops=flops, bytes_accessed=MIB, transcendentals=flops // 512
        ),
        name=name,
    )(table, *operands, *after)


def tie_kernel(*refs):
    del refs


def tie(before, *payloads):
    before = tuple(before)
    anywhere = pl.BlockSpec(memory_space=pl.ANY)
    return pl.pallas_call(
        tie_kernel,
        in_specs=[anywhere] * (len(before) + len(payloads)),
        out_specs=[anywhere] * len(payloads),
        out_shape=[jax.ShapeDtypeStruct(p.shape, p.dtype) for p in payloads],
        input_output_aliases={len(before) + i: i for i in range(len(payloads))},
        compiler_params=pltpu.CompilerParams(vmem_limit_bytes=MIB),
        name="tie",
    )(*before, *payloads)


def project(own_groups, part_groups, weights, operands):
    rows, columns = operands[0].shape[0], weights[0].shape[1]
    depth = sum(weight.shape[0] for weight in weights)
    return pl.pallas_call(
        functools.partial(project_kernel, own_groups, part_groups, len(weights) // 2),
        grid=(1,),
        in_specs=[whole(x.shape) for x in (*weights, *operands)],
        out_specs=whole((rows, columns)),
        out_shape=jax.ShapeDtypeStruct((rows, columns), jnp.bfloat16),
        scratch_shapes=[pltpu.VMEM((rows, depth), jnp.bfloat16)],
        compiler_params=pltpu.CompilerParams(vmem_limit_bytes=8 * MIB),
        cost_estimate=pl.CostEstimate(
            flops=2 * rows * depth * columns, bytes_accessed=12 * MIB, transcendentals=0
        ),
        name="merge_and_project",
    )(*weights, *operands)


def per_device(queries, key_tokens, value_tokens, radial_table, out_weight):
    frames = lax.axis_size("frame")
    cores = lax.axis_size("head")
    rows = queries.shape[0]

    def moves(target):
        return [(f, target(f)) for f in range(frames) if 0 <= target(f) < frames]

    partner_moves = moves(lambda f: f ^ 1)
    near_moves = moves(lambda f: f - 2 if f % 2 == 0 else f + 2)
    away_moves = moves(lambda f: f + 2 if f % 2 == 0 else f - 2)
    cross_moves = moves(lambda f: f - 1 if f % 2 == 0 else f + 1)
    core_moves = [(c, cores - 1 - c) for c in range(cores)]

    def pack(first, last):
        cols = slice(first * DH, last * DH)
        return jnp.concatenate([key_tokens[:, cols], value_tokens[:, cols]], axis=0)

    def firsts(*packed):
        return jnp.concatenate(
            [jnp.concatenate([p[at : at + BS] for p in packed], axis=1) for at in (0, rows)],
            axis=0,
        )

    major1 = lax.ppermute(pack(0, 6), "frame", away_moves)
    minor1 = lax.ppermute(pack(3, 9), "frame", near_moves)
    own_weight = [out_weight]
    sib_weight = [lax.ppermute(out_weight, "head", core_moves)]
    cross = lax.ppermute(pack(0, 3), "frame", partner_moves)
    cross, to_minor2 = tie(sib_weight, cross, pack(9, 12))
    minor2 = lax.ppermute(to_minor2, "frame", near_moves)
    partner_query = lax.ppermute(queries, "frame", partner_moves)
    major2 = lax.ppermute(cross, "frame", away_moves)
    minor3 = lax.ppermute(minor1, "frame", near_moves)
    (to_major3,) = tie((major1,), pack(6, 12))
    major3 = lax.ppermute(to_major3, "frame", away_moves)
    major4 = lax.ppermute(major2, "frame", away_moves)
    minor4 = lax.ppermute(minor2, "frame", near_moves)
    to_sib_keys, to_sib_values = tie((major2, minor2), key_tokens, value_tokens)
    sib_keys = lax.ppermute(to_sib_keys, "head", core_moves)
    sib_values = lax.ppermute(to_sib_values, "head", core_moves)
    nearest = lax.ppermute(firsts(minor1, minor2, major2), "head", core_moves)
    refs = {
        "major1": major1,
        "major2": major2,
        "major3": major3,
        "major4": major4,
        "minor1": minor1,
        "minor2": minor2,
        "minor3": minor3,
        "minor4": minor4,
        "nearest": nearest,
    }
    local = (key_tokens, value_tokens, sib_keys, sib_values)

    def partner_part(group, names, after=()):
        heads = group[1] - group[0]
        shape = jax.ShapeDtypeStruct((rows + stat_rows(heads)[1], heads * DH), jnp.bfloat16)
        (part,) = run(
            functools.partial(partner_kernel, group, names),
            "partner_part",
            radial_table,
            (partner_query, *local, *(refs[n] for n in names)),
            [shape],
            heads * rows * 6 * BS * DH * 4,
            after,
        )
        return part

    def own_part(group, names, after=()):
        heads = group[1] - group[0]
        return run(
            functools.partial(own_kernel, group, names),
            "own_part",
            radial_table,
            (queries, *local, *(refs[n] for n in names)),
            [
                jax.ShapeDtypeStruct((rows, heads * DH), jnp.float32),
                jax.ShapeDtypeStruct((rows, DH), jnp.float32),
            ],
            heads * rows * 6 * BS * DH * 4,
            after,
        )

    own_groups = ((0, 3), (3, 6), (6, 12))
    part_groups = ((0, 3), (3, 9), (9, 12))
    part_low = partner_part((0, 3), ("major1", "major2"))
    own_early = own_part((3, 6), ("major1", "minor1"))
    own_late = own_part((6, 12), ("major3", "minor1", "minor2"))
    part_middle = partner_part(
        (3, 9), ("major1", "major3", "minor1", "minor3", "nearest"), (part_low, own_early[1], own_late[1])
    )
    part_low = lax.ppermute(part_low, "frame", partner_moves)
    part_middle = lax.ppermute(part_middle, "frame", partner_moves)
    part_high = partner_part(
        (9, 12), ("major3", "minor2", "minor4", "nearest"), (own_late[1], major4, part_low, *sib_weight)
    )
    part_high = lax.ppermute(part_high, "frame", partner_moves)
    own_low = own_part((0, 3), ("major1", "major2", "major4", "nearest"))
    return project(
        own_groups,
        part_groups,
        (*own_weight, *sib_weight),
        (*own_low, *own_early, *own_late, part_low, part_middle, part_high),
    )


def solution(mesh):
    in_specs = (
        P(("clip", "frame", "head"), None),
        P(("clip", "frame", "head"), None),
        P(("clip", "frame", "head"), None),
        P(),
        P("head", None),
    )
    out_specs = P(("clip", "frame", "head"), None)
    return jax.shard_map(
        per_device, mesh=mesh, in_specs=in_specs, out_specs=out_specs, check_vma=False
    )
```

```python
import functools
import math

import jax
import jax.numpy as jnp
from jax import lax
from jax.experimental import pallas as pl
from jax.experimental.pallas import tpu as pltpu
from jax.sharding import PartitionSpec as P

DH = 128
BS = 128
CROSS = 3
BATCH = 4
TILE = 768
NEG = -1e30
LOG2_SCALE = math.log2(math.e) / math.sqrt(DH)
MIB = 1024 * 1024


def frame_ids():
    frame = lax.axis_index("frame")
    return frame, 1 - 2 * lax.rem(frame, 2)


def entry(table_ref, query_frame, key_frame):
    frames = table_ref.shape[0]
    inside = (key_frame >= 0) & (key_frame < frames)
    count = table_ref[query_frame, jnp.clip(key_frame, 0, frames - 1)]
    return jnp.where(inside, count, 0)


def attend(problems):
    scores = []
    for query, parts in problems:
        row = []
        for keys, _, valid in parts:
            raw = lax.dot_general(
                query, keys, (((1,), (1,)), ((), ())), preferred_element_type=jnp.float32
            )
            row.append(raw if valid is None else jnp.where(valid, raw, NEG))
        scores.append(row)
    tops = []
    for row in scores:
        best = None
        for raw in row:
            for at in range(0, raw.shape[1], BS):
                piece = raw[:, at : at + BS]
                best = piece if best is None else jnp.maximum(best, piece)
        tops.append(best.max(axis=1, keepdims=True))
    weights = [
        [jnp.exp2((raw - top) * LOG2_SCALE) for raw in row] for row, top in zip(scores, tops)
    ]
    totals = []
    for row in weights:
        total = None
        for weight in row:
            for at in range(0, weight.shape[1], BS):
                piece = weight[:, at : at + BS]
                total = piece if total is None else total + piece
        totals.append(total.sum(axis=1, keepdims=True))
    results = []
    for (_, parts), row, top, total in zip(problems, weights, tops, totals):
        blended = 0.0
        for (_, values, _), weight in zip(parts, row):
            blended = blended + jnp.dot(
                weight.astype(jnp.bfloat16), values, preferred_element_type=jnp.float32
            )
        results.append((blended / total, top * LOG2_SCALE + jnp.log2(total)))
    return results


def attend_heads(group, blocks, problem, out):
    rows = blocks * BS
    heads = range(*group)
    lanes = lax.broadcasted_iota(jnp.int32, (rows, DH), 1)
    stats = jnp.zeros((rows, DH), jnp.float32)
    items = [(place, head, block) for place, head in enumerate(heads) for block in range(blocks)]
    sums = {}
    for at in range(0, len(items), BATCH):
        chunk = items[at : at + BATCH]
        results = attend([problem(head, block) for _, head, block in chunk])
        for (place, head, block), (blended, logsum) in zip(chunk, results):
            out[block * BS : (block + 1) * BS, head_cols(place)] = blended.astype(out.dtype)
            sums[place, block] = logsum
    for place in range(len(heads)):
        column = jnp.concatenate([sums[place, block] for block in range(blocks)], axis=0)
        stats = jnp.where(lanes == place, column, stats)
    return stats


def head_cols(head):
    return slice(head * DH, (head + 1) * DH)


def stat_rows(heads):
    return (4, 16) if heads <= 4 else (8, 32)


def write_stats(out, stats, heads):
    pad, count = stat_rows(heads)
    rows = stats.shape[0]
    packed, rest = 0.0, stats
    for part in range(3):
        piece = rest.astype(jnp.bfloat16).astype(jnp.float32)
        rest = rest - piece
        packed = packed + (pltpu.roll(piece, part * pad, 1) if part else piece)
    out[rows:, :] = jnp.zeros((count, out.shape[1]), out.dtype)
    out[rows:, :rows] = packed.T[:count].astype(out.dtype)


def read_stats(ref, heads):
    pad, count = stat_rows(heads)
    rows = ref.shape[0] - count
    packed = ref[rows:, :rows].astype(jnp.float32)
    padding = jnp.zeros((DH - count, rows), jnp.float32)
    packed = jnp.concatenate([packed, padding], axis=0).T
    return packed + pltpu.roll(packed, DH - pad, 1) + pltpu.roll(packed, DH - 2 * pad, 1)


def pair(ref, col, block):
    rows = ref.shape[0] // 2
    cols = head_cols(col)
    return (
        ref[block * BS : (block + 1) * BS, cols],
        ref[rows + block * BS : rows + (block + 1) * BS, cols],
    )


class Buffers:
    def __init__(self, refs):
        self.refs = refs

    def cross(self, head, block):
        return pair(self.refs["major2"], head, block)

    def far(self, head, block):
        return pair(self.refs["major4"], head, block)

    def away(self, head, block):
        if head < 6:
            return pair(self.refs["major1"], head, block)
        return pair(self.refs["major3"], head - 6, block)

    def near(self, head, block):
        if head < 9:
            return pair(self.refs["minor1"], head - 3, block)
        return pair(self.refs["minor2"], head - 9, block)

    def near_first(self, head):
        return pair(self.refs["nearest"], head - 3, 0)

    def cross_first(self, head):
        return pair(self.refs["nearest"], 9 + head, 0)

    def relay(self, head, block):
        if head < 9:
            return pair(self.refs["minor3"], head - 3, block)
        return pair(self.refs["minor4"], head - 9, block)


def partner_kernel(group, names, table_ref, query, keys, values, sib_keys, sib_values, *rest):
    frame, sign = frame_ids()
    buffers = Buffers(dict(zip(names, rest)))
    out = rest[-1]
    rows = query.shape[0]
    blocks = rows // BS
    partner = frame + sign
    own_count = entry(table_ref, partner, frame)
    near_count = entry(table_ref, partner, frame + 2 * sign)
    away_valid = entry(table_ref, partner, frame - 2 * sign) > 0
    relay_valid = entry(table_ref, partner, frame + 4 * sign) > 0
    cross_valid = entry(table_ref, partner, frame - sign) > 0

    def problem(head, block):
        mine = slice(block * BS, (block + 1) * BS)
        cols = head_cols(head)
        last = block + 1 == blocks
        parts = [(keys[mine, cols], values[mine, cols], None)]
        if last:
            parts.append((sib_keys[:BS, cols], sib_values[:BS, cols], own_count > 1))
        else:
            after = slice((block + 1) * BS, (block + 2) * BS)
            parts.append((keys[after, cols], values[after, cols], own_count > 1))
        parts.append((*buffers.away(head, block), away_valid))
        if head < CROSS:
            parts.append((*buffers.cross(head, block), cross_valid))
        else:
            parts.append((*buffers.near(head, block), near_count > 0))
            after = buffers.near_first(head) if last else buffers.near(head, block + 1)
            parts.append((*after, near_count > 1))
            parts.append((*buffers.relay(head, block), relay_valid))
        return query[mine, cols], parts

    stats = attend_heads(group, blocks, problem, out)
    write_stats(out, stats, group[1] - group[0])


def own_kernel(group, names, table_ref, query, keys, values, sib_keys, sib_values, *rest):
    frame, sign = frame_ids()
    buffers = Buffers(dict(zip(names, rest)))
    out, out_stats = rest[-2:]
    rows = query.shape[0]
    blocks = rows // BS
    near_valid = entry(table_ref, frame, frame + 2 * sign) > 0
    away_valid = entry(table_ref, frame, frame - 2 * sign) > 0
    cross_count = entry(table_ref, frame, frame - sign)
    far_valid = entry(table_ref, frame, frame - 3 * sign) > 0

    def problem(head, block):
        mine = slice(block * BS, (block + 1) * BS)
        cols = head_cols(head)
        parts = [
            (keys[:, cols], values[:, cols], None),
            (sib_keys[:, cols], sib_values[:, cols], None),
            (*buffers.away(head, block), away_valid),
        ]
        if head < CROSS:
            last = block + 1 == blocks
            parts.append((*buffers.cross(head, block), cross_count > 0))
            after = buffers.cross_first(head) if last else buffers.cross(head, block + 1)
            parts.append((*after, cross_count > 1))
            parts.append((*buffers.far(head, block), far_valid))
        else:
            parts.append((*buffers.near(head, block), near_valid))
        return query[mine, cols], parts

    out_stats[...] = attend_heads(group, blocks, problem, out)


def project_kernel(span, own_groups, part_groups, has_base, *refs):
    refs = list(refs)
    weight, sib_weight = refs.pop(0), refs.pop(0)
    owns = [(group, refs.pop(0), refs.pop(0)) for group in own_groups]
    parts = [(group, refs.pop(0)) for group in part_groups]
    base = refs.pop(0) if has_base else None
    out, attended = refs
    rows = out.shape[0]
    lanes = lax.broadcasted_iota(jnp.int32, (rows, DH), 1)
    own_at, part_at = {}, {}
    own_sum = part_sum = jnp.zeros((rows, DH), jnp.float32)
    for (first, last), own, stats in owns:
        shifted = pltpu.roll(stats[...], first, 1) if first else stats[...]
        own_sum = jnp.where((lanes >= first) & (lanes < last), shifted, own_sum)
        own_at.update({head: (own, head - first) for head in range(first, last)})
    for (first, last), part in parts:
        stats = read_stats(part, last - first)
        shifted = pltpu.roll(stats, first, 1) if first else stats
        part_sum = jnp.where((lanes >= first) & (lanes < last), shifted, part_sum)
        part_at.update({head: (part, head - first) for head in range(first, last)})
    top = jnp.maximum(own_sum, part_sum)
    own_weight = jnp.exp2(own_sum - top)
    part_weight = jnp.exp2(part_sum - top)
    inverse = 1.0 / (own_weight + part_weight)
    own_weight = own_weight * inverse
    part_weight = part_weight * inverse
    for head in range(*span):
        own, own_place = own_at[head]
        part, part_place = part_at[head]
        mixed = own_weight[:, head : head + 1] * own[:, head_cols(own_place)] + part_weight[
            :, head : head + 1
        ] * part[:rows, head_cols(part_place)].astype(jnp.float32)
        attended[:, head_cols(head - span[0])] = mixed.astype(attended.dtype)

    depth = weight.shape[0]
    start, stop = span[0] * DH, span[1] * DH

    def multiply(halves):
        for at in range(0, out.shape[1], TILE):
            product = base[:, at : at + TILE] if has_base else 0.0
            for index, half in enumerate(halves):
                low, high = max(start, index * depth), min(stop, (index + 1) * depth)
                if low < high:
                    product = product + jnp.dot(
                        attended[:, low - start : high - start],
                        half[low - index * depth : high - index * depth, at : at + TILE],
                        preferred_element_type=jnp.float32,
                    )
            out[:, at : at + TILE] = product.astype(out.dtype)

    core = lax.axis_index("head")

    @pl.when(core == 0)
    def _():
        multiply((weight, sib_weight))

    @pl.when(core != 0)
    def _():
        multiply((sib_weight, weight))


def whole(shape):
    return pl.BlockSpec(shape, lambda i: (0,) * len(shape))


def run(body, name, table, operands, out_shapes, flops, after=()):
    return pl.pallas_call(
        body,
        grid=(1,),
        in_specs=[pl.BlockSpec(memory_space=pltpu.SMEM)]
        + [whole(x.shape) for x in operands]
        + [pl.BlockSpec(memory_space=pl.ANY)] * len(after),
        out_specs=[whole(s.shape) for s in out_shapes],
        out_shape=out_shapes,
        compiler_params=pltpu.CompilerParams(vmem_limit_bytes=8 * MIB),
        cost_estimate=pl.CostEstimate(
            flops=flops, bytes_accessed=MIB, transcendentals=flops // 512
        ),
        name=name,
    )(table, *operands, *after)


def tie_kernel(*refs):
    del refs


def tie(before, *payloads):
    before = tuple(before)
    anywhere = pl.BlockSpec(memory_space=pl.ANY)
    return pl.pallas_call(
        tie_kernel,
        in_specs=[anywhere] * (len(before) + len(payloads)),
        out_specs=[anywhere] * len(payloads),
        out_shape=[jax.ShapeDtypeStruct(p.shape, p.dtype) for p in payloads],
        input_output_aliases={len(before) + i: i for i in range(len(payloads))},
        compiler_params=pltpu.CompilerParams(vmem_limit_bytes=MIB),
        name="tie",
    )(*before, *payloads)


def project(span, owns, parts, weights, base, dtype):
    rows, columns = owns[0][1][0].shape[0], weights[0].shape[1]
    depth = (span[1] - span[0]) * DH
    operands = [*weights]
    for _, own in owns:
        operands += own
    operands += [part for _, part in parts]
    if base is not None:
        operands.append(base)
    return pl.pallas_call(
        functools.partial(
            project_kernel,
            span,
            tuple(group for group, _ in owns),
            tuple(group for group, _ in parts),
            base is not None,
        ),
        grid=(1,),
        in_specs=[whole(x.shape) for x in operands],
        out_specs=whole((rows, columns)),
        out_shape=jax.ShapeDtypeStruct((rows, columns), dtype),
        scratch_shapes=[pltpu.VMEM((rows, depth), jnp.bfloat16)],
        compiler_params=pltpu.CompilerParams(vmem_limit_bytes=8 * MIB),
        cost_estimate=pl.CostEstimate(
            flops=2 * rows * depth * columns, bytes_accessed=4 * MIB, transcendentals=0
        ),
        name="merge_and_project",
    )(*operands)


def per_device(queries, key_tokens, value_tokens, radial_table, out_weight):
    frames = lax.axis_size("frame")
    cores = lax.axis_size("head")
    rows = queries.shape[0]

    def moves(target):
        return [(f, target(f)) for f in range(frames) if 0 <= target(f) < frames]

    partner_moves = moves(lambda f: f ^ 1)
    near_moves = moves(lambda f: f - 2 if f % 2 == 0 else f + 2)
    away_moves = moves(lambda f: f + 2 if f % 2 == 0 else f - 2)
    cross_moves = moves(lambda f: f - 1 if f % 2 == 0 else f + 1)
    core_moves = [(c, cores - 1 - c) for c in range(cores)]

    def pack(first, last):
        cols = slice(first * DH, last * DH)
        return jnp.concatenate([key_tokens[:, cols], value_tokens[:, cols]], axis=0)

    def firsts(*packed):
        return jnp.concatenate(
            [jnp.concatenate([p[at : at + BS] for p in packed], axis=1) for at in (0, rows)],
            axis=0,
        )

    major1 = lax.ppermute(pack(0, 6), "frame", away_moves)
    minor1 = lax.ppermute(pack(3, 9), "frame", near_moves)
    own_weight = [out_weight]
    sib_weight = [lax.ppermute(out_weight, "head", core_moves)]
    cross = lax.ppermute(pack(0, 3), "frame", partner_moves)
    cross, to_minor2 = tie(sib_weight, cross, pack(9, 12))
    minor2 = lax.ppermute(to_minor2, "frame", near_moves)
    partner_query = lax.ppermute(queries, "frame", partner_moves)
    major2 = lax.ppermute(cross, "frame", away_moves)
    minor3 = lax.ppermute(minor1, "frame", near_moves)
    (to_major3,) = tie((major1,), pack(6, 12))
    major3 = lax.ppermute(to_major3, "frame", away_moves)
    major4 = lax.ppermute(major2, "frame", away_moves)
    minor4 = lax.ppermute(minor2, "frame", near_moves)
    to_sib_keys, to_sib_values = tie((major2, partner_query, minor2), key_tokens, value_tokens)
    sib_keys = lax.ppermute(to_sib_keys, "head", core_moves)
    sib_values = lax.ppermute(to_sib_values, "head", core_moves)
    nearest = lax.ppermute(firsts(minor1, minor2, major2), "head", core_moves)
    refs = {
        "major1": major1,
        "major2": major2,
        "major3": major3,
        "major4": major4,
        "minor1": minor1,
        "minor2": minor2,
        "minor3": minor3,
        "minor4": minor4,
        "nearest": nearest,
    }
    local = (key_tokens, value_tokens, sib_keys, sib_values)

    def partner_part(group, names, after=()):
        heads = group[1] - group[0]
        shape = jax.ShapeDtypeStruct((rows + stat_rows(heads)[1], heads * DH), jnp.bfloat16)
        (part,) = run(
            functools.partial(partner_kernel, group, names),
            "partner_part",
            radial_table,
            (partner_query, *local, *(refs[n] for n in names)),
            [shape],
            heads * rows * 6 * BS * DH * 4,
            after,
        )
        return part

    def own_part(group, names, after=()):
        heads = group[1] - group[0]
        return run(
            functools.partial(own_kernel, group, names),
            "own_part",
            radial_table,
            (queries, *local, *(refs[n] for n in names)),
            [
                jax.ShapeDtypeStruct((rows, heads * DH), jnp.float32),
                jax.ShapeDtypeStruct((rows, DH), jnp.float32),
            ],
            heads * rows * 6 * BS * DH * 4,
            after,
        )

    part_low = partner_part((0, 3), ("major1", "major2"))
    own_early = own_part((3, 6), ("major1", "minor1"))
    part_middle = partner_part(
        (3, 6), ("major1", "minor1", "minor3", "nearest"), (part_low, own_early[1], major3)
    )
    part_late = partner_part((6, 9), ("major3", "minor1", "minor3", "nearest"), (part_middle,))
    part_low = lax.ppermute(part_low, "frame", partner_moves)
    part_middle = lax.ppermute(part_middle, "frame", partner_moves)
    part_late = lax.ppermute(part_late, "frame", partner_moves)
    own_late = own_part((6, 12), ("major3", "minor1", "minor2"))
    part_high = partner_part(
        (9, 12),
        ("major3", "minor2", "minor4", "nearest"),
        (own_late[1], major4, part_low, *sib_weight),
    )
    part_high = lax.ppermute(part_high, "frame", partner_moves)
    own_low = own_part((0, 3), ("major1", "major2", "major4", "nearest"))
    weights = (*own_weight, *sib_weight)
    owns = (((0, 3), own_low), ((3, 6), own_early), ((6, 12), own_late))
    base = project(
        (0, 9),
        owns,
        (((0, 3), part_low), ((3, 6), part_middle), ((6, 9), part_late)),
        weights,
        None,
        jnp.float32,
    )
    return project(
        (9, 12), (((6, 12), own_late),), (((9, 12), part_high),), weights, base, jnp.bfloat16
    )


def solution(mesh):
    in_specs = (
        P(("clip", "frame", "head"), None),
        P(("clip", "frame", "head"), None),
        P(("clip", "frame", "head"), None),
        P(),
        P("head", None),
    )
    out_specs = P(("clip", "frame", "head"), None)
    return jax.shard_map(
        per_device, mesh=mesh, in_specs=in_specs, out_specs=out_specs, check_vma=False
    )
```

```python
import functools
import math

import jax
import jax.numpy as jnp
from jax import lax
from jax.experimental import pallas as pl
from jax.experimental.pallas import tpu as pltpu
from jax.sharding import PartitionSpec as P

DH = 128
BS = 128
CROSS = 3
BATCH = 6
TILE = 768
NEG = -1e30
LOG2_SCALE = math.log2(math.e) / math.sqrt(DH)
MIB = 1024 * 1024


def frame_ids():
    frame = lax.axis_index("frame")
    return frame, 1 - 2 * lax.rem(frame, 2)


def entry(table_ref, query_frame, key_frame):
    frames = table_ref.shape[0]
    inside = (key_frame >= 0) & (key_frame < frames)
    count = table_ref[query_frame, jnp.clip(key_frame, 0, frames - 1)]
    return jnp.where(inside, count, 0)


def attend(problems):
    scores = []
    for query, parts in problems:
        row = []
        for keys, _, valid in parts:
            raw = lax.dot_general(
                query, keys, (((1,), (1,)), ((), ())), preferred_element_type=jnp.float32
            )
            row.append(raw if valid is None else jnp.where(valid, raw, NEG))
        scores.append(row)
    tops = []
    for row in scores:
        best = None
        for raw in row:
            for at in range(0, raw.shape[1], BS):
                piece = raw[:, at : at + BS]
                best = piece if best is None else jnp.maximum(best, piece)
        tops.append(best.max(axis=1, keepdims=True))
    weights = [
        [jnp.exp2((raw - top) * LOG2_SCALE) for raw in row] for row, top in zip(scores, tops)
    ]
    totals = []
    for row in weights:
        total = None
        for weight in row:
            for at in range(0, weight.shape[1], BS):
                piece = weight[:, at : at + BS]
                total = piece if total is None else total + piece
        totals.append(total.sum(axis=1, keepdims=True))
    results = []
    for (_, parts), row, top, total in zip(problems, weights, tops, totals):
        blended = 0.0
        for (_, values, _), weight in zip(parts, row):
            blended = blended + jnp.dot(
                weight.astype(jnp.bfloat16), values, preferred_element_type=jnp.float32
            )
        results.append((blended / total, top * LOG2_SCALE + jnp.log2(total)))
    return results


def attend_heads(group, blocks, problem, out):
    rows = blocks * BS
    heads = range(*group)
    lanes = lax.broadcasted_iota(jnp.int32, (rows, DH), 1)
    stats = jnp.zeros((rows, DH), jnp.float32)
    items = [(place, head, block) for place, head in enumerate(heads) for block in range(blocks)]
    sums = {}
    for at in range(0, len(items), BATCH):
        chunk = items[at : at + BATCH]
        results = attend([problem(head, block) for _, head, block in chunk])
        for (place, head, block), (blended, logsum) in zip(chunk, results):
            out[block * BS : (block + 1) * BS, head_cols(place)] = blended.astype(out.dtype)
            sums[place, block] = logsum
    for place in range(len(heads)):
        column = jnp.concatenate([sums[place, block] for block in range(blocks)], axis=0)
        stats = jnp.where(lanes == place, column, stats)
    return stats


def head_cols(head):
    return slice(head * DH, (head + 1) * DH)


def stat_rows(heads):
    return (4, 16) if heads <= 4 else (8, 32)


def write_stats(out, stats, heads):
    pad, count = stat_rows(heads)
    rows = stats.shape[0]
    packed, rest = 0.0, stats
    for part in range(3):
        piece = rest.astype(jnp.bfloat16).astype(jnp.float32)
        rest = rest - piece
        packed = packed + (pltpu.roll(piece, part * pad, 1) if part else piece)
    out[rows:, :] = jnp.zeros((count, out.shape[1]), out.dtype)
    out[rows:, :rows] = packed.T[:count].astype(out.dtype)


def read_stats(ref, heads):
    pad, count = stat_rows(heads)
    rows = ref.shape[0] - count
    packed = ref[rows:, :rows].astype(jnp.float32)
    padding = jnp.zeros((DH - count, rows), jnp.float32)
    packed = jnp.concatenate([packed, padding], axis=0).T
    return packed + pltpu.roll(packed, DH - pad, 1) + pltpu.roll(packed, DH - 2 * pad, 1)


def pair(ref, col, block):
    rows = ref.shape[0] // 2
    cols = head_cols(col)
    return (
        ref[block * BS : (block + 1) * BS, cols],
        ref[rows + block * BS : rows + (block + 1) * BS, cols],
    )


class Buffers:
    def __init__(self, refs):
        self.refs = refs

    def cross(self, head, block):
        return pair(self.refs["major2"], head, block)

    def far(self, head, block):
        return pair(self.refs["major4"], head, block)

    def away(self, head, block):
        if head < 6:
            return pair(self.refs["major1"], head, block)
        return pair(self.refs["major3"], head - 6, block)

    def near(self, head, block):
        if head < 9:
            return pair(self.refs["minor1"], head - 3, block)
        return pair(self.refs["minor2"], head - 9, block)

    def near_first(self, head):
        return pair(self.refs["nearest"], head - 3, 0)

    def cross_first(self, head):
        return pair(self.refs["nearest"], 9 + head, 0)

    def relay(self, head, block):
        if head < 9:
            return pair(self.refs["minor3"], head - 3, block)
        return pair(self.refs["minor4"], head - 9, block)


def partner_kernel(group, names, table_ref, query, keys, values, sib_keys, sib_values, *rest):
    frame, sign = frame_ids()
    buffers = Buffers(dict(zip(names, rest)))
    out = rest[-1]
    rows = query.shape[0]
    blocks = rows // BS
    partner = frame + sign
    own_count = entry(table_ref, partner, frame)
    near_count = entry(table_ref, partner, frame + 2 * sign)
    away_valid = entry(table_ref, partner, frame - 2 * sign) > 0
    relay_valid = entry(table_ref, partner, frame + 4 * sign) > 0
    cross_valid = entry(table_ref, partner, frame - sign) > 0

    def problem(head, block):
        mine = slice(block * BS, (block + 1) * BS)
        cols = head_cols(head)
        last = block + 1 == blocks
        parts = [(keys[mine, cols], values[mine, cols], None)]
        if last:
            parts.append((sib_keys[:BS, cols], sib_values[:BS, cols], own_count > 1))
        else:
            after = slice((block + 1) * BS, (block + 2) * BS)
            parts.append((keys[after, cols], values[after, cols], own_count > 1))
        parts.append((*buffers.away(head, block), away_valid))
        if head < CROSS:
            parts.append((*buffers.cross(head, block), cross_valid))
        else:
            parts.append((*buffers.near(head, block), near_count > 0))
            after = buffers.near_first(head) if last else buffers.near(head, block + 1)
            parts.append((*after, near_count > 1))
            parts.append((*buffers.relay(head, block), relay_valid))
        return query[mine, cols], parts

    stats = attend_heads(group, blocks, problem, out)
    write_stats(out, stats, group[1] - group[0])


def own_kernel(group, names, table_ref, query, keys, values, sib_keys, sib_values, *rest):
    frame, sign = frame_ids()
    buffers = Buffers(dict(zip(names, rest)))
    out, out_stats = rest[-2:]
    rows = query.shape[0]
    blocks = rows // BS
    near_valid = entry(table_ref, frame, frame + 2 * sign) > 0
    away_valid = entry(table_ref, frame, frame - 2 * sign) > 0
    cross_count = entry(table_ref, frame, frame - sign)
    far_valid = entry(table_ref, frame, frame - 3 * sign) > 0

    def problem(head, block):
        mine = slice(block * BS, (block + 1) * BS)
        cols = head_cols(head)
        parts = [
            (keys[:, cols], values[:, cols], None),
            (sib_keys[:, cols], sib_values[:, cols], None),
            (*buffers.away(head, block), away_valid),
        ]
        if head < CROSS:
            last = block + 1 == blocks
            parts.append((*buffers.cross(head, block), cross_count > 0))
            after = buffers.cross_first(head) if last else buffers.cross(head, block + 1)
            parts.append((*after, cross_count > 1))
            parts.append((*buffers.far(head, block), far_valid))
        else:
            parts.append((*buffers.near(head, block), near_valid))
        return query[mine, cols], parts

    out_stats[...] = attend_heads(group, blocks, problem, out)


def project_kernel(span, own_groups, part_groups, has_base, *refs):
    refs = list(refs)
    weight, sib_weight = refs.pop(0), refs.pop(0)
    owns = [(group, refs.pop(0), refs.pop(0)) for group in own_groups]
    parts = [(group, refs.pop(0)) for group in part_groups]
    base = refs.pop(0) if has_base else None
    out, attended = refs
    rows = out.shape[0]
    lanes = lax.broadcasted_iota(jnp.int32, (rows, DH), 1)
    own_at, part_at = {}, {}
    own_sum = part_sum = jnp.zeros((rows, DH), jnp.float32)
    for (first, last), own, stats in owns:
        shifted = pltpu.roll(stats[...], first, 1) if first else stats[...]
        own_sum = jnp.where((lanes >= first) & (lanes < last), shifted, own_sum)
        own_at.update({head: (own, head - first) for head in range(first, last)})
    for (first, last), part in parts:
        stats = read_stats(part, last - first)
        shifted = pltpu.roll(stats, first, 1) if first else stats
        part_sum = jnp.where((lanes >= first) & (lanes < last), shifted, part_sum)
        part_at.update({head: (part, head - first) for head in range(first, last)})
    top = jnp.maximum(own_sum, part_sum)
    own_weight = jnp.exp2(own_sum - top)
    part_weight = jnp.exp2(part_sum - top)
    inverse = 1.0 / (own_weight + part_weight)
    own_weight = own_weight * inverse
    part_weight = part_weight * inverse
    for head in range(*span):
        own, own_place = own_at[head]
        part, part_place = part_at[head]
        mixed = own_weight[:, head : head + 1] * own[:, head_cols(own_place)] + part_weight[
            :, head : head + 1
        ] * part[:rows, head_cols(part_place)].astype(jnp.float32)
        attended[:, head_cols(head - span[0])] = mixed.astype(attended.dtype)

    depth = weight.shape[0]
    start, stop = span[0] * DH, span[1] * DH

    def multiply(halves):
        for at in range(0, out.shape[1], TILE):
            product = base[:, at : at + TILE] if has_base else 0.0
            for index, half in enumerate(halves):
                low, high = max(start, index * depth), min(stop, (index + 1) * depth)
                if low < high:
                    product = product + jnp.dot(
                        attended[:, low - start : high - start],
                        half[low - index * depth : high - index * depth, at : at + TILE],
                        preferred_element_type=jnp.float32,
                    )
            out[:, at : at + TILE] = product.astype(out.dtype)

    core = lax.axis_index("head")

    @pl.when(core == 0)
    def _():
        multiply((weight, sib_weight))

    @pl.when(core != 0)
    def _():
        multiply((sib_weight, weight))


def whole(shape):
    return pl.BlockSpec(shape, lambda i: (0,) * len(shape))


def run(body, name, table, operands, out_shapes, flops, after=()):
    return pl.pallas_call(
        body,
        grid=(1,),
        in_specs=[pl.BlockSpec(memory_space=pltpu.SMEM)]
        + [whole(x.shape) for x in operands]
        + [pl.BlockSpec(memory_space=pl.ANY)] * len(after),
        out_specs=[whole(s.shape) for s in out_shapes],
        out_shape=out_shapes,
        compiler_params=pltpu.CompilerParams(vmem_limit_bytes=8 * MIB),
        cost_estimate=pl.CostEstimate(
            flops=flops, bytes_accessed=MIB, transcendentals=flops // 512
        ),
        name=name,
    )(table, *operands, *after)


def tie_kernel(*refs):
    del refs


def tie(before, *payloads):
    before = tuple(before)
    anywhere = pl.BlockSpec(memory_space=pl.ANY)
    return pl.pallas_call(
        tie_kernel,
        in_specs=[anywhere] * (len(before) + len(payloads)),
        out_specs=[anywhere] * len(payloads),
        out_shape=[jax.ShapeDtypeStruct(p.shape, p.dtype) for p in payloads],
        input_output_aliases={len(before) + i: i for i in range(len(payloads))},
        compiler_params=pltpu.CompilerParams(vmem_limit_bytes=MIB),
        name="tie",
    )(*before, *payloads)


def project(span, owns, parts, weights, base, dtype):
    rows, columns = owns[0][1][0].shape[0], weights[0].shape[1]
    depth = (span[1] - span[0]) * DH
    operands = [*weights]
    for _, own in owns:
        operands += own
    operands += [part for _, part in parts]
    if base is not None:
        operands.append(base)
    return pl.pallas_call(
        functools.partial(
            project_kernel,
            span,
            tuple(group for group, _ in owns),
            tuple(group for group, _ in parts),
            base is not None,
        ),
        grid=(1,),
        in_specs=[whole(x.shape) for x in operands],
        out_specs=whole((rows, columns)),
        out_shape=jax.ShapeDtypeStruct((rows, columns), dtype),
        scratch_shapes=[pltpu.VMEM((rows, depth), jnp.bfloat16)],
        compiler_params=pltpu.CompilerParams(vmem_limit_bytes=8 * MIB),
        cost_estimate=pl.CostEstimate(
            flops=2 * rows * depth * columns, bytes_accessed=4 * MIB, transcendentals=0
        ),
        name="merge_and_project",
    )(*operands)


def per_device(queries, key_tokens, value_tokens, radial_table, out_weight):
    frames = lax.axis_size("frame")
    cores = lax.axis_size("head")
    rows = queries.shape[0]

    def moves(target):
        return [(f, target(f)) for f in range(frames) if 0 <= target(f) < frames]

    partner_moves = moves(lambda f: f ^ 1)
    near_moves = moves(lambda f: f - 2 if f % 2 == 0 else f + 2)
    away_moves = moves(lambda f: f + 2 if f % 2 == 0 else f - 2)
    cross_moves = moves(lambda f: f - 1 if f % 2 == 0 else f + 1)
    core_moves = [(c, cores - 1 - c) for c in range(cores)]

    def pack(first, last):
        cols = slice(first * DH, last * DH)
        return jnp.concatenate([key_tokens[:, cols], value_tokens[:, cols]], axis=0)

    def firsts(*packed):
        return jnp.concatenate(
            [jnp.concatenate([p[at : at + BS] for p in packed], axis=1) for at in (0, rows)],
            axis=0,
        )

    major1 = lax.ppermute(pack(0, 6), "frame", away_moves)
    minor1 = lax.ppermute(pack(3, 9), "frame", near_moves)
    own_weight = [out_weight]
    sib_weight = [lax.ppermute(out_weight, "head", core_moves)]
    cross = lax.ppermute(pack(0, 3), "frame", partner_moves)
    cross, to_minor2 = tie(sib_weight, cross, pack(9, 12))
    minor2 = lax.ppermute(to_minor2, "frame", near_moves)
    partner_query = lax.ppermute(queries, "frame", partner_moves)
    major2 = lax.ppermute(cross, "frame", away_moves)
    minor3 = lax.ppermute(minor1, "frame", near_moves)
    (to_major3,) = tie((major1,), pack(6, 12))
    major3 = lax.ppermute(to_major3, "frame", away_moves)
    major4 = lax.ppermute(major2, "frame", away_moves)
    minor4 = lax.ppermute(minor2, "frame", near_moves)
    to_sib_keys, to_sib_values = tie((major2, partner_query, minor2), key_tokens, value_tokens)
    sib_keys = lax.ppermute(to_sib_keys, "head", core_moves)
    sib_values = lax.ppermute(to_sib_values, "head", core_moves)
    nearest = lax.ppermute(firsts(minor1, minor2, major2), "head", core_moves)
    refs = {
        "major1": major1,
        "major2": major2,
        "major3": major3,
        "major4": major4,
        "minor1": minor1,
        "minor2": minor2,
        "minor3": minor3,
        "minor4": minor4,
        "nearest": nearest,
    }
    local = (key_tokens, value_tokens, sib_keys, sib_values)

    def partner_part(group, names, after=()):
        heads = group[1] - group[0]
        shape = jax.ShapeDtypeStruct((rows + stat_rows(heads)[1], heads * DH), jnp.bfloat16)
        (part,) = run(
            functools.partial(partner_kernel, group, names),
            "partner_part",
            radial_table,
            (partner_query, *local, *(refs[n] for n in names)),
            [shape],
            heads * rows * 6 * BS * DH * 4,
            after,
        )
        return part

    def own_part(group, names, after=()):
        heads = group[1] - group[0]
        return run(
            functools.partial(own_kernel, group, names),
            "own_part",
            radial_table,
            (queries, *local, *(refs[n] for n in names)),
            [
                jax.ShapeDtypeStruct((rows, heads * DH), jnp.float32),
                jax.ShapeDtypeStruct((rows, DH), jnp.float32),
            ],
            heads * rows * 6 * BS * DH * 4,
            after,
        )

    own_early = own_part((3, 6), ("major1", "minor1"))
    part_low = partner_part((0, 3), ("major1", "major2"), (own_early[1],))
    part_middle = partner_part(
        (3, 6), ("major1", "minor1", "minor3", "nearest"), (part_low, major3)
    )
    part_late = partner_part((6, 9), ("major3", "minor1", "minor3", "nearest"), (part_middle,))
    part_low = lax.ppermute(part_low, "frame", partner_moves)
    part_middle = lax.ppermute(part_middle, "frame", partner_moves)
    part_late = lax.ppermute(part_late, "frame", partner_moves)
    own_late = own_part((6, 12), ("major3", "minor1", "minor2"))
    part_high = partner_part(
        (9, 12),
        ("major3", "minor2", "minor4", "nearest"),
        (own_late[1], major4, part_low, *sib_weight),
    )
    part_high = lax.ppermute(part_high, "frame", partner_moves)
    own_low = own_part((0, 3), ("major1", "major2", "major4", "nearest"))
    weights = (*own_weight, *sib_weight)
    owns = (((0, 3), own_low), ((3, 6), own_early), ((6, 12), own_late))
    base = project(
        (0, 9),
        owns,
        (((0, 3), part_low), ((3, 6), part_middle), ((6, 9), part_late)),
        weights,
        None,
        jnp.float32,
    )
    return project(
        (9, 12), (((6, 12), own_late),), (((9, 12), part_high),), weights, base, jnp.bfloat16
    )


def solution(mesh):
    in_specs = (
        P(("clip", "frame", "head"), None),
        P(("clip", "frame", "head"), None),
        P(("clip", "frame", "head"), None),
        P(),
        P("head", None),
    )
    out_specs = P(("clip", "frame", "head"), None)
    return jax.shard_map(
        per_device, mesh=mesh, in_specs=in_specs, out_specs=out_specs, check_vma=False
    )
```

```python
import functools
import math

import jax
import jax.numpy as jnp
from jax import lax
from jax.experimental import pallas as pl
from jax.experimental.pallas import tpu as pltpu
from jax.sharding import PartitionSpec as P

DH = 128
BS = 128
CROSS = 3
BATCH = 6
TILE = 768
NEG = -1e30
LOG2_SCALE = math.log2(math.e) / math.sqrt(DH)
MIB = 1024 * 1024


def frame_ids():
    frame = lax.axis_index("frame")
    return frame, 1 - 2 * lax.rem(frame, 2)


def entry(table_ref, query_frame, key_frame):
    frames = table_ref.shape[0]
    inside = (key_frame >= 0) & (key_frame < frames)
    count = table_ref[query_frame, jnp.clip(key_frame, 0, frames - 1)]
    return jnp.where(inside, count, 0)


def attend(problems):
    scores = []
    for query, parts in problems:
        row = []
        for keys, _, valid in parts:
            raw = lax.dot_general(
                query, keys, (((1,), (1,)), ((), ())), preferred_element_type=jnp.float32
            )
            row.append(raw if valid is None else jnp.where(valid, raw, NEG))
        scores.append(row)
    tops = []
    for row in scores:
        best = None
        for raw in row:
            for at in range(0, raw.shape[1], BS):
                piece = raw[:, at : at + BS]
                best = piece if best is None else jnp.maximum(best, piece)
        tops.append(best.max(axis=1, keepdims=True))
    weights = [
        [jnp.exp2((raw - top) * LOG2_SCALE) for raw in row] for row, top in zip(scores, tops)
    ]
    totals = []
    for row in weights:
        total = None
        for weight in row:
            for at in range(0, weight.shape[1], BS):
                piece = weight[:, at : at + BS]
                total = piece if total is None else total + piece
        totals.append(total.sum(axis=1, keepdims=True))
    results = []
    for (_, parts), row, top, total in zip(problems, weights, tops, totals):
        blended = 0.0
        for (_, values, _), weight in zip(parts, row):
            blended = blended + jnp.dot(
                weight.astype(jnp.bfloat16), values, preferred_element_type=jnp.float32
            )
        results.append((blended / total, top * LOG2_SCALE + jnp.log2(total)))
    return results


def attend_heads(group, blocks, problem, out):
    rows = blocks * BS
    heads = range(*group)
    lanes = lax.broadcasted_iota(jnp.int32, (rows, DH), 1)
    stats = jnp.zeros((rows, DH), jnp.float32)
    items = [(place, head, block) for place, head in enumerate(heads) for block in range(blocks)]
    sums = {}
    for at in range(0, len(items), BATCH):
        chunk = items[at : at + BATCH]
        results = attend([problem(head, block) for _, head, block in chunk])
        for (place, head, block), (blended, logsum) in zip(chunk, results):
            out[block * BS : (block + 1) * BS, head_cols(place)] = blended.astype(out.dtype)
            sums[place, block] = logsum
    for place in range(len(heads)):
        column = jnp.concatenate([sums[place, block] for block in range(blocks)], axis=0)
        stats = jnp.where(lanes == place, column, stats)
    return stats


def head_cols(head):
    return slice(head * DH, (head + 1) * DH)


def stat_rows(heads):
    return (4, 16) if heads <= 4 else (8, 32)


def write_stats(out, stats, heads):
    pad, count = stat_rows(heads)
    rows = stats.shape[0]
    packed, rest = 0.0, stats
    for part in range(3):
        piece = rest.astype(jnp.bfloat16).astype(jnp.float32)
        rest = rest - piece
        packed = packed + (pltpu.roll(piece, part * pad, 1) if part else piece)
    out[rows:, :] = jnp.zeros((count, out.shape[1]), out.dtype)
    out[rows:, :rows] = packed.T[:count].astype(out.dtype)


def read_stats(ref, heads):
    pad, count = stat_rows(heads)
    rows = ref.shape[0] - count
    packed = ref[rows:, :rows].astype(jnp.float32)
    padding = jnp.zeros((DH - count, rows), jnp.float32)
    packed = jnp.concatenate([packed, padding], axis=0).T
    return packed + pltpu.roll(packed, DH - pad, 1) + pltpu.roll(packed, DH - 2 * pad, 1)


def pair(ref, col, block):
    rows = ref.shape[0] // 2
    cols = head_cols(col)
    return (
        ref[block * BS : (block + 1) * BS, cols],
        ref[rows + block * BS : rows + (block + 1) * BS, cols],
    )


class Buffers:
    def __init__(self, refs):
        self.refs = refs

    def cross(self, head, block):
        return pair(self.refs["major2"], head, block)

    def far(self, head, block):
        return pair(self.refs["major4"], head, block)

    def away(self, head, block):
        if head < 6:
            return pair(self.refs["major1"], head, block)
        return pair(self.refs["major3"], head - 6, block)

    def near(self, head, block):
        if head < 9:
            return pair(self.refs["minor1"], head - 3, block)
        return pair(self.refs["minor2"], head - 9, block)

    def near_first(self, head):
        return pair(self.refs["nearest"], head - 3, 0)

    def cross_first(self, head):
        return pair(self.refs["nearest"], 9 + head, 0)

    def relay(self, head, block):
        if head < 9:
            return pair(self.refs["minor3"], head - 3, block)
        return pair(self.refs["minor4"], head - 9, block)


def partner_kernel(group, names, table_ref, query, keys, values, sib_keys, sib_values, *rest):
    frame, sign = frame_ids()
    buffers = Buffers(dict(zip(names, rest)))
    out = rest[-1]
    rows = query.shape[0]
    blocks = rows // BS
    partner = frame + sign
    own_count = entry(table_ref, partner, frame)
    near_count = entry(table_ref, partner, frame + 2 * sign)
    away_valid = entry(table_ref, partner, frame - 2 * sign) > 0
    relay_valid = entry(table_ref, partner, frame + 4 * sign) > 0
    cross_valid = entry(table_ref, partner, frame - sign) > 0

    def problem(head, block):
        mine = slice(block * BS, (block + 1) * BS)
        cols = head_cols(head)
        last = block + 1 == blocks
        parts = [(keys[mine, cols], values[mine, cols], None)]
        if last:
            parts.append((sib_keys[:BS, cols], sib_values[:BS, cols], own_count > 1))
        else:
            after = slice((block + 1) * BS, (block + 2) * BS)
            parts.append((keys[after, cols], values[after, cols], own_count > 1))
        parts.append((*buffers.away(head, block), away_valid))
        if head < CROSS:
            parts.append((*buffers.cross(head, block), cross_valid))
        else:
            parts.append((*buffers.near(head, block), near_count > 0))
            after = buffers.near_first(head) if last else buffers.near(head, block + 1)
            parts.append((*after, near_count > 1))
            parts.append((*buffers.relay(head, block), relay_valid))
        return query[mine, cols], parts

    stats = attend_heads(group, blocks, problem, out)
    write_stats(out, stats, group[1] - group[0])


def own_kernel(group, names, table_ref, query, keys, values, sib_keys, sib_values, *rest):
    frame, sign = frame_ids()
    buffers = Buffers(dict(zip(names, rest)))
    out, out_stats = rest[-2:]
    rows = query.shape[0]
    blocks = rows // BS
    near_valid = entry(table_ref, frame, frame + 2 * sign) > 0
    away_valid = entry(table_ref, frame, frame - 2 * sign) > 0
    cross_count = entry(table_ref, frame, frame - sign)
    far_valid = entry(table_ref, frame, frame - 3 * sign) > 0

    def problem(head, block):
        mine = slice(block * BS, (block + 1) * BS)
        cols = head_cols(head)
        parts = [
            (keys[:, cols], values[:, cols], None),
            (sib_keys[:, cols], sib_values[:, cols], None),
            (*buffers.away(head, block), away_valid),
        ]
        if head < CROSS:
            last = block + 1 == blocks
            parts.append((*buffers.cross(head, block), cross_count > 0))
            after = buffers.cross_first(head) if last else buffers.cross(head, block + 1)
            parts.append((*after, cross_count > 1))
            parts.append((*buffers.far(head, block), far_valid))
        else:
            parts.append((*buffers.near(head, block), near_valid))
        return query[mine, cols], parts

    out_stats[...] = attend_heads(group, blocks, problem, out)


def project_kernel(span, own_groups, part_groups, has_base, *refs):
    refs = list(refs)
    weight, sib_weight = refs.pop(0), refs.pop(0)
    owns = [(group, refs.pop(0), refs.pop(0)) for group in own_groups]
    parts = [(group, refs.pop(0)) for group in part_groups]
    base = refs.pop(0) if has_base else None
    out, attended = refs
    rows = out.shape[0]
    lanes = lax.broadcasted_iota(jnp.int32, (rows, DH), 1)
    own_at, part_at = {}, {}
    own_sum = part_sum = jnp.zeros((rows, DH), jnp.float32)
    for (first, last), own, stats in owns:
        shifted = pltpu.roll(stats[...], first, 1) if first else stats[...]
        own_sum = jnp.where((lanes >= first) & (lanes < last), shifted, own_sum)
        own_at.update({head: (own, head - first) for head in range(first, last)})
    for (first, last), part in parts:
        stats = read_stats(part, last - first)
        shifted = pltpu.roll(stats, first, 1) if first else stats
        part_sum = jnp.where((lanes >= first) & (lanes < last), shifted, part_sum)
        part_at.update({head: (part, head - first) for head in range(first, last)})
    top = jnp.maximum(own_sum, part_sum)
    own_weight = jnp.exp2(own_sum - top)
    part_weight = jnp.exp2(part_sum - top)
    inverse = 1.0 / (own_weight + part_weight)
    own_weight = own_weight * inverse
    part_weight = part_weight * inverse
    for head in range(*span):
        own, own_place = own_at[head]
        part, part_place = part_at[head]
        mixed = own_weight[:, head : head + 1] * own[:, head_cols(own_place)] + part_weight[
            :, head : head + 1
        ] * part[:rows, head_cols(part_place)].astype(jnp.float32)
        attended[:, head_cols(head - span[0])] = mixed.astype(attended.dtype)

    depth = weight.shape[0]
    start, stop = span[0] * DH, span[1] * DH

    def multiply(halves):
        for at in range(0, out.shape[1], TILE):
            product = base[:, at : at + TILE] if has_base else 0.0
            for index, half in enumerate(halves):
                low, high = max(start, index * depth), min(stop, (index + 1) * depth)
                if low < high:
                    product = product + jnp.dot(
                        attended[:, low - start : high - start],
                        half[low - index * depth : high - index * depth, at : at + TILE],
                        preferred_element_type=jnp.float32,
                    )
            out[:, at : at + TILE] = product.astype(out.dtype)

    core = lax.axis_index("head")

    @pl.when(core == 0)
    def _():
        multiply((weight, sib_weight))

    @pl.when(core != 0)
    def _():
        multiply((sib_weight, weight))


def whole(shape):
    return pl.BlockSpec(shape, lambda i: (0,) * len(shape))


def run(body, name, table, operands, out_shapes, flops, after=()):
    return pl.pallas_call(
        body,
        grid=(1,),
        in_specs=[pl.BlockSpec(memory_space=pltpu.SMEM)]
        + [whole(x.shape) for x in operands]
        + [pl.BlockSpec(memory_space=pl.ANY)] * len(after),
        out_specs=[whole(s.shape) for s in out_shapes],
        out_shape=out_shapes,
        compiler_params=pltpu.CompilerParams(vmem_limit_bytes=8 * MIB),
        cost_estimate=pl.CostEstimate(
            flops=flops, bytes_accessed=MIB, transcendentals=flops // 512
        ),
        name=name,
    )(table, *operands, *after)


def tie_kernel(*refs):
    del refs


def tie(before, *payloads):
    before = tuple(before)
    anywhere = pl.BlockSpec(memory_space=pl.ANY)
    return pl.pallas_call(
        tie_kernel,
        in_specs=[anywhere] * (len(before) + len(payloads)),
        out_specs=[anywhere] * len(payloads),
        out_shape=[jax.ShapeDtypeStruct(p.shape, p.dtype) for p in payloads],
        input_output_aliases={len(before) + i: i for i in range(len(payloads))},
        compiler_params=pltpu.CompilerParams(vmem_limit_bytes=MIB),
        name="tie",
    )(*before, *payloads)


def project(span, owns, parts, weights, base, dtype):
    rows, columns = owns[0][1][0].shape[0], weights[0].shape[1]
    depth = (span[1] - span[0]) * DH
    operands = [*weights]
    for _, own in owns:
        operands += own
    operands += [part for _, part in parts]
    if base is not None:
        operands.append(base)
    return pl.pallas_call(
        functools.partial(
            project_kernel,
            span,
            tuple(group for group, _ in owns),
            tuple(group for group, _ in parts),
            base is not None,
        ),
        grid=(1,),
        in_specs=[whole(x.shape) for x in operands],
        out_specs=whole((rows, columns)),
        out_shape=jax.ShapeDtypeStruct((rows, columns), dtype),
        scratch_shapes=[pltpu.VMEM((rows, depth), jnp.bfloat16)],
        compiler_params=pltpu.CompilerParams(vmem_limit_bytes=8 * MIB),
        cost_estimate=pl.CostEstimate(
            flops=2 * rows * depth * columns, bytes_accessed=4 * MIB, transcendentals=0
        ),
        name="merge_and_project",
    )(*operands)


def per_device(queries, key_tokens, value_tokens, radial_table, out_weight):
    frames = lax.axis_size("frame")
    cores = lax.axis_size("head")
    rows = queries.shape[0]

    def moves(target):
        return [(f, target(f)) for f in range(frames) if 0 <= target(f) < frames]

    partner_moves = moves(lambda f: f ^ 1)
    near_moves = moves(lambda f: f - 2 if f % 2 == 0 else f + 2)
    away_moves = moves(lambda f: f + 2 if f % 2 == 0 else f - 2)
    cross_moves = moves(lambda f: f - 1 if f % 2 == 0 else f + 1)
    core_moves = [(c, cores - 1 - c) for c in range(cores)]

    def pack(first, last):
        cols = slice(first * DH, last * DH)
        return jnp.concatenate([key_tokens[:, cols], value_tokens[:, cols]], axis=0)

    def firsts(*packed):
        return jnp.concatenate(
            [jnp.concatenate([p[at : at + BS] for p in packed], axis=1) for at in (0, rows)],
            axis=0,
        )

    major1 = lax.ppermute(pack(0, 6), "frame", away_moves)
    minor1 = lax.ppermute(pack(3, 9), "frame", near_moves)
    own_weight = [out_weight]
    sib_weight = [lax.ppermute(out_weight, "head", core_moves)]
    cross = lax.ppermute(pack(0, 3), "frame", partner_moves)
    cross, to_minor2 = tie(sib_weight, cross, pack(9, 12))
    minor2 = lax.ppermute(to_minor2, "frame", near_moves)
    partner_query = lax.ppermute(queries, "frame", partner_moves)
    major2 = lax.ppermute(cross, "frame", away_moves)
    minor3 = lax.ppermute(minor1, "frame", near_moves)
    (to_major3,) = tie((major1,), pack(6, 12))
    major3 = lax.ppermute(to_major3, "frame", away_moves)
    major4 = lax.ppermute(major2, "frame", away_moves)
    minor4 = lax.ppermute(minor2, "frame", near_moves)
    to_sib_keys, to_sib_values = tie((major2, partner_query, minor2), key_tokens, value_tokens)
    sib_keys = lax.ppermute(to_sib_keys, "head", core_moves)
    sib_values = lax.ppermute(to_sib_values, "head", core_moves)
    nearest = lax.ppermute(firsts(minor1, minor2, major2), "head", core_moves)
    refs = {
        "major1": major1,
        "major2": major2,
        "major3": major3,
        "major4": major4,
        "minor1": minor1,
        "minor2": minor2,
        "minor3": minor3,
        "minor4": minor4,
        "nearest": nearest,
    }
    local = (key_tokens, value_tokens, sib_keys, sib_values)

    def partner_part(group, names, after=()):
        heads = group[1] - group[0]
        shape = jax.ShapeDtypeStruct((rows + stat_rows(heads)[1], heads * DH), jnp.bfloat16)
        (part,) = run(
            functools.partial(partner_kernel, group, names),
            "partner_part",
            radial_table,
            (partner_query, *local, *(refs[n] for n in names)),
            [shape],
            heads * rows * 6 * BS * DH * 4,
            after,
        )
        return part

    def own_part(group, names, after=()):
        heads = group[1] - group[0]
        return run(
            functools.partial(own_kernel, group, names),
            "own_part",
            radial_table,
            (queries, *local, *(refs[n] for n in names)),
            [
                jax.ShapeDtypeStruct((rows, heads * DH), jnp.float32),
                jax.ShapeDtypeStruct((rows, DH), jnp.float32),
            ],
            heads * rows * 6 * BS * DH * 4,
            after,
        )

    own_early = own_part((3, 6), ("major1", "minor1"))
    part_low = partner_part((0, 3), ("major1", "major2"), (own_early[1],))
    own_late = own_part((6, 12), ("major3", "minor1", "minor2"), (part_low,))
    part_middle = partner_part(
        (3, 6), ("major1", "minor1", "minor3", "nearest"), (own_late[1],)
    )
    part_late = partner_part((6, 9), ("major3", "minor1", "minor3", "nearest"), (part_middle,))
    part_low = lax.ppermute(part_low, "frame", partner_moves)
    part_middle = lax.ppermute(part_middle, "frame", partner_moves)
    part_late = lax.ppermute(part_late, "frame", partner_moves)
    part_high = partner_part(
        (9, 12),
        ("major3", "minor2", "minor4", "nearest"),
        (own_late[1], major4, part_low, *sib_weight),
    )
    part_high = lax.ppermute(part_high, "frame", partner_moves)
    own_low = own_part((0, 3), ("major1", "major2", "major4", "nearest"))
    weights = (*own_weight, *sib_weight)
    owns = (((0, 3), own_low), ((3, 6), own_early), ((6, 12), own_late))
    base = project(
        (0, 9),
        owns,
        (((0, 3), part_low), ((3, 6), part_middle), ((6, 9), part_late)),
        weights,
        None,
        jnp.float32,
    )
    return project(
        (9, 12), (((6, 12), own_late),), (((9, 12), part_high),), weights, base, jnp.bfloat16
    )


def solution(mesh):
    in_specs = (
        P(("clip", "frame", "head"), None),
        P(("clip", "frame", "head"), None),
        P(("clip", "frame", "head"), None),
        P(),
        P("head", None),
    )
    out_specs = P(("clip", "frame", "head"), None)
    return jax.shard_map(
        per_device, mesh=mesh, in_specs=in_specs, out_specs=out_specs, check_vma=False
    )
```

```python
import functools
import math

import jax
import jax.numpy as jnp
from jax import lax
from jax.experimental import pallas as pl
from jax.experimental.pallas import tpu as pltpu
from jax.sharding import PartitionSpec as P

DH = 128
BS = 128
CROSS = 3
BATCH = 6
TILE = 768
NEG = -1e30
LOG2_SCALE = math.log2(math.e) / math.sqrt(DH)
MIB = 1024 * 1024


def frame_ids():
    frame = lax.axis_index("frame")
    return frame, 1 - 2 * lax.rem(frame, 2)


def entry(table_ref, query_frame, key_frame):
    frames = table_ref.shape[0]
    inside = (key_frame >= 0) & (key_frame < frames)
    count = table_ref[query_frame, jnp.clip(key_frame, 0, frames - 1)]
    return jnp.where(inside, count, 0)


def attend(problems):
    scores = []
    for query, parts in problems:
        row = []
        for keys, _, valid in parts:
            raw = lax.dot_general(
                query, keys, (((1,), (1,)), ((), ())), preferred_element_type=jnp.float32
            )
            row.append(raw if valid is None else jnp.where(valid, raw, NEG))
        scores.append(row)
    tops = []
    for row in scores:
        best = None
        for raw in row:
            for at in range(0, raw.shape[1], BS):
                piece = raw[:, at : at + BS]
                best = piece if best is None else jnp.maximum(best, piece)
        tops.append(best.max(axis=1, keepdims=True))
    weights = [
        [jnp.exp2((raw - top) * LOG2_SCALE) for raw in row] for row, top in zip(scores, tops)
    ]
    totals = []
    for row in weights:
        total = None
        for weight in row:
            for at in range(0, weight.shape[1], BS):
                piece = weight[:, at : at + BS]
                total = piece if total is None else total + piece
        totals.append(total.sum(axis=1, keepdims=True))
    results = []
    for (_, parts), row, top, total in zip(problems, weights, tops, totals):
        blended = 0.0
        for (_, values, _), weight in zip(parts, row):
            blended = blended + jnp.dot(
                weight.astype(jnp.bfloat16), values, preferred_element_type=jnp.float32
            )
        results.append((blended / total, top * LOG2_SCALE + jnp.log2(total)))
    return results


def attend_heads(group, blocks, problem, out):
    rows = blocks * BS
    heads = range(*group)
    lanes = lax.broadcasted_iota(jnp.int32, (rows, DH), 1)
    stats = jnp.zeros((rows, DH), jnp.float32)
    items = [(place, head, block) for place, head in enumerate(heads) for block in range(blocks)]
    sums = {}
    for at in range(0, len(items), BATCH):
        chunk = items[at : at + BATCH]
        results = attend([problem(head, block) for _, head, block in chunk])
        for (place, head, block), (blended, logsum) in zip(chunk, results):
            out[block * BS : (block + 1) * BS, head_cols(place)] = blended.astype(out.dtype)
            sums[place, block] = logsum
    for place in range(len(heads)):
        column = jnp.concatenate([sums[place, block] for block in range(blocks)], axis=0)
        stats = jnp.where(lanes == place, column, stats)
    return stats


def head_cols(head):
    return slice(head * DH, (head + 1) * DH)


def stat_rows(heads):
    return (4, 16) if heads <= 4 else (8, 32)


def write_stats(out, stats, heads):
    pad, count = stat_rows(heads)
    rows = stats.shape[0]
    packed, rest = 0.0, stats
    for part in range(3):
        piece = rest.astype(jnp.bfloat16).astype(jnp.float32)
        rest = rest - piece
        packed = packed + (pltpu.roll(piece, part * pad, 1) if part else piece)
    out[rows:, :] = jnp.zeros((count, out.shape[1]), out.dtype)
    out[rows:, :rows] = packed.T[:count].astype(out.dtype)


def read_stats(ref, heads):
    pad, count = stat_rows(heads)
    rows = ref.shape[0] - count
    packed = ref[rows:, :rows].astype(jnp.float32)
    padding = jnp.zeros((DH - count, rows), jnp.float32)
    packed = jnp.concatenate([packed, padding], axis=0).T
    return packed + pltpu.roll(packed, DH - pad, 1) + pltpu.roll(packed, DH - 2 * pad, 1)


def pair(ref, col, block):
    rows = ref.shape[0] // 2
    cols = head_cols(col)
    return (
        ref[block * BS : (block + 1) * BS, cols],
        ref[rows + block * BS : rows + (block + 1) * BS, cols],
    )


class Buffers:
    def __init__(self, refs):
        self.refs = refs

    def cross(self, head, block):
        return pair(self.refs["major2"], head, block)

    def far(self, head, block):
        return pair(self.refs["major4"], head, block)

    def away(self, head, block):
        if head < 6:
            return pair(self.refs["major1"], head, block)
        return pair(self.refs["major3"], head - 6, block)

    def near(self, head, block):
        if head < 9:
            return pair(self.refs["minor1"], head - 3, block)
        return pair(self.refs["minor2"], head - 9, block)

    def near_first(self, head):
        return pair(self.refs["nearest"], head - 3, 0)

    def cross_first(self, head):
        return pair(self.refs["nearest"], 9 + head, 0)

    def relay(self, head, block):
        if head < 9:
            return pair(self.refs["minor3"], head - 3, block)
        return pair(self.refs["minor4"], head - 9, block)


def partner_kernel(group, names, table_ref, query, keys, values, sib_keys, sib_values, *rest):
    frame, sign = frame_ids()
    buffers = Buffers(dict(zip(names, rest)))
    out = rest[-1]
    rows = query.shape[0]
    blocks = rows // BS
    partner = frame + sign
    own_count = entry(table_ref, partner, frame)
    near_count = entry(table_ref, partner, frame + 2 * sign)
    away_valid = entry(table_ref, partner, frame - 2 * sign) > 0
    relay_valid = entry(table_ref, partner, frame + 4 * sign) > 0
    cross_valid = entry(table_ref, partner, frame - sign) > 0

    def problem(head, block):
        mine = slice(block * BS, (block + 1) * BS)
        cols = head_cols(head)
        last = block + 1 == blocks
        parts = [(keys[mine, cols], values[mine, cols], None)]
        if last:
            parts.append((sib_keys[:BS, cols], sib_values[:BS, cols], own_count > 1))
        else:
            after = slice((block + 1) * BS, (block + 2) * BS)
            parts.append((keys[after, cols], values[after, cols], own_count > 1))
        parts.append((*buffers.away(head, block), away_valid))
        if head < CROSS:
            parts.append((*buffers.cross(head, block), cross_valid))
        else:
            parts.append((*buffers.near(head, block), near_count > 0))
            after = buffers.near_first(head) if last else buffers.near(head, block + 1)
            parts.append((*after, near_count > 1))
            parts.append((*buffers.relay(head, block), relay_valid))
        return query[mine, cols], parts

    stats = attend_heads(group, blocks, problem, out)
    write_stats(out, stats, group[1] - group[0])


def own_kernel(group, names, table_ref, query, keys, values, sib_keys, sib_values, *rest):
    frame, sign = frame_ids()
    buffers = Buffers(dict(zip(names, rest)))
    out, out_stats = rest[-2:]
    rows = query.shape[0]
    blocks = rows // BS
    near_valid = entry(table_ref, frame, frame + 2 * sign) > 0
    away_valid = entry(table_ref, frame, frame - 2 * sign) > 0
    cross_count = entry(table_ref, frame, frame - sign)
    far_valid = entry(table_ref, frame, frame - 3 * sign) > 0

    def problem(head, block):
        mine = slice(block * BS, (block + 1) * BS)
        cols = head_cols(head)
        parts = [
            (keys[:, cols], values[:, cols], None),
            (sib_keys[:, cols], sib_values[:, cols], None),
            (*buffers.away(head, block), away_valid),
        ]
        if head < CROSS:
            last = block + 1 == blocks
            parts.append((*buffers.cross(head, block), cross_count > 0))
            after = buffers.cross_first(head) if last else buffers.cross(head, block + 1)
            parts.append((*after, cross_count > 1))
            parts.append((*buffers.far(head, block), far_valid))
        else:
            parts.append((*buffers.near(head, block), near_valid))
        return query[mine, cols], parts

    out_stats[...] = attend_heads(group, blocks, problem, out)


def project_kernel(span, own_groups, part_groups, has_base, *refs):
    refs = list(refs)
    weight, sib_weight = refs.pop(0), refs.pop(0)
    owns = [(group, refs.pop(0), refs.pop(0)) for group in own_groups]
    parts = [(group, refs.pop(0)) for group in part_groups]
    base = refs.pop(0) if has_base else None
    out, attended = refs
    rows = out.shape[0]
    lanes = lax.broadcasted_iota(jnp.int32, (rows, DH), 1)
    own_at, part_at = {}, {}
    own_sum = part_sum = jnp.zeros((rows, DH), jnp.float32)
    for (first, last), own, stats in owns:
        shifted = pltpu.roll(stats[...], first, 1) if first else stats[...]
        own_sum = jnp.where((lanes >= first) & (lanes < last), shifted, own_sum)
        own_at.update({head: (own, head - first) for head in range(first, last)})
    for (first, last), part in parts:
        stats = read_stats(part, last - first)
        shifted = pltpu.roll(stats, first, 1) if first else stats
        part_sum = jnp.where((lanes >= first) & (lanes < last), shifted, part_sum)
        part_at.update({head: (part, head - first) for head in range(first, last)})
    top = jnp.maximum(own_sum, part_sum)
    own_weight = jnp.exp2(own_sum - top)
    part_weight = jnp.exp2(part_sum - top)
    inverse = 1.0 / (own_weight + part_weight)
    own_weight = own_weight * inverse
    part_weight = part_weight * inverse
    for head in range(*span):
        own, own_place = own_at[head]
        part, part_place = part_at[head]
        mixed = own_weight[:, head : head + 1] * own[:, head_cols(own_place)] + part_weight[
            :, head : head + 1
        ] * part[:rows, head_cols(part_place)].astype(jnp.float32)
        attended[:, head_cols(head - span[0])] = mixed.astype(attended.dtype)

    depth = weight.shape[0]
    start, stop = span[0] * DH, span[1] * DH

    def multiply(halves):
        for at in range(0, out.shape[1], TILE):
            product = base[:, at : at + TILE] if has_base else 0.0
            for index, half in enumerate(halves):
                low, high = max(start, index * depth), min(stop, (index + 1) * depth)
                if low < high:
                    product = product + jnp.dot(
                        attended[:, low - start : high - start],
                        half[low - index * depth : high - index * depth, at : at + TILE],
                        preferred_element_type=jnp.float32,
                    )
            out[:, at : at + TILE] = product.astype(out.dtype)

    core = lax.axis_index("head")

    @pl.when(core == 0)
    def _():
        multiply((weight, sib_weight))

    @pl.when(core != 0)
    def _():
        multiply((sib_weight, weight))


def whole(shape):
    return pl.BlockSpec(shape, lambda i: (0,) * len(shape))


def run(body, name, table, operands, out_shapes, flops, after=()):
    return pl.pallas_call(
        body,
        grid=(1,),
        in_specs=[pl.BlockSpec(memory_space=pltpu.SMEM)]
        + [whole(x.shape) for x in operands]
        + [pl.BlockSpec(memory_space=pl.ANY)] * len(after),
        out_specs=[whole(s.shape) for s in out_shapes],
        out_shape=out_shapes,
        compiler_params=pltpu.CompilerParams(vmem_limit_bytes=8 * MIB),
        cost_estimate=pl.CostEstimate(
            flops=flops, bytes_accessed=MIB, transcendentals=flops // 512
        ),
        name=name,
    )(table, *operands, *after)


def tie_kernel(*refs):
    del refs


def tie(before, *payloads):
    before = tuple(before)
    anywhere = pl.BlockSpec(memory_space=pl.ANY)
    return pl.pallas_call(
        tie_kernel,
        in_specs=[anywhere] * (len(before) + len(payloads)),
        out_specs=[anywhere] * len(payloads),
        out_shape=[jax.ShapeDtypeStruct(p.shape, p.dtype) for p in payloads],
        input_output_aliases={len(before) + i: i for i in range(len(payloads))},
        compiler_params=pltpu.CompilerParams(vmem_limit_bytes=MIB),
        name="tie",
    )(*before, *payloads)


def project(span, owns, parts, weights, base, dtype):
    rows, columns = owns[0][1][0].shape[0], weights[0].shape[1]
    depth = (span[1] - span[0]) * DH
    operands = [*weights]
    for _, own in owns:
        operands += own
    operands += [part for _, part in parts]
    if base is not None:
        operands.append(base)
    return pl.pallas_call(
        functools.partial(
            project_kernel,
            span,
            tuple(group for group, _ in owns),
            tuple(group for group, _ in parts),
            base is not None,
        ),
        grid=(1,),
        in_specs=[whole(x.shape) for x in operands],
        out_specs=whole((rows, columns)),
        out_shape=jax.ShapeDtypeStruct((rows, columns), dtype),
        scratch_shapes=[pltpu.VMEM((rows, depth), jnp.bfloat16)],
        compiler_params=pltpu.CompilerParams(vmem_limit_bytes=8 * MIB),
        cost_estimate=pl.CostEstimate(
            flops=2 * rows * depth * columns, bytes_accessed=4 * MIB, transcendentals=0
        ),
        name="merge_and_project",
    )(*operands)


def per_device(queries, key_tokens, value_tokens, radial_table, out_weight):
    frames = lax.axis_size("frame")
    cores = lax.axis_size("head")
    rows = queries.shape[0]

    def moves(target):
        return [(f, target(f)) for f in range(frames) if 0 <= target(f) < frames]

    partner_moves = moves(lambda f: f ^ 1)
    near_moves = moves(lambda f: f - 2 if f % 2 == 0 else f + 2)
    away_moves = moves(lambda f: f + 2 if f % 2 == 0 else f - 2)
    cross_moves = moves(lambda f: f - 1 if f % 2 == 0 else f + 1)
    core_moves = [(c, cores - 1 - c) for c in range(cores)]

    def pack(first, last):
        cols = slice(first * DH, last * DH)
        return jnp.concatenate([key_tokens[:, cols], value_tokens[:, cols]], axis=0)

    def firsts(*packed):
        return jnp.concatenate(
            [jnp.concatenate([p[at : at + BS] for p in packed], axis=1) for at in (0, rows)],
            axis=0,
        )

    major1 = lax.ppermute(pack(0, 6), "frame", away_moves)
    minor1 = lax.ppermute(pack(3, 9), "frame", near_moves)
    own_weight = [out_weight]
    sib_weight = [lax.ppermute(out_weight, "head", core_moves)]
    cross = lax.ppermute(pack(0, 3), "frame", partner_moves)
    cross, to_minor2 = tie(sib_weight, cross, pack(9, 12))
    minor2 = lax.ppermute(to_minor2, "frame", near_moves)
    partner_query = lax.ppermute(queries, "frame", partner_moves)
    major2 = lax.ppermute(cross, "frame", away_moves)
    minor3 = lax.ppermute(minor1, "frame", near_moves)
    (to_major3,) = tie((major1,), pack(6, 12))
    major3 = lax.ppermute(to_major3, "frame", away_moves)
    major4 = lax.ppermute(major2, "frame", away_moves)
    minor4 = lax.ppermute(minor2, "frame", near_moves)
    to_sib_keys, to_sib_values = tie((major2, partner_query, minor2, major1), key_tokens, value_tokens)
    sib_keys = lax.ppermute(to_sib_keys, "head", core_moves)
    sib_values = lax.ppermute(to_sib_values, "head", core_moves)
    nearest = lax.ppermute(firsts(minor1, minor2, major2), "head", core_moves)
    refs = {
        "major1": major1,
        "major2": major2,
        "major3": major3,
        "major4": major4,
        "minor1": minor1,
        "minor2": minor2,
        "minor3": minor3,
        "minor4": minor4,
        "nearest": nearest,
    }
    local = (key_tokens, value_tokens, sib_keys, sib_values)

    def partner_part(group, names, after=()):
        heads = group[1] - group[0]
        shape = jax.ShapeDtypeStruct((rows + stat_rows(heads)[1], heads * DH), jnp.bfloat16)
        (part,) = run(
            functools.partial(partner_kernel, group, names),
            "partner_part",
            radial_table,
            (partner_query, *local, *(refs[n] for n in names)),
            [shape],
            heads * rows * 6 * BS * DH * 4,
            after,
        )
        return part

    def own_part(group, names, after=()):
        heads = group[1] - group[0]
        return run(
            functools.partial(own_kernel, group, names),
            "own_part",
            radial_table,
            (queries, *local, *(refs[n] for n in names)),
            [
                jax.ShapeDtypeStruct((rows, heads * DH), jnp.float32),
                jax.ShapeDtypeStruct((rows, DH), jnp.float32),
            ],
            heads * rows * 6 * BS * DH * 4,
            after,
        )

    own_early = own_part((3, 6), ("major1", "minor1"))
    part_low = partner_part((0, 3), ("major1", "major2"), (own_early[1],))
    part_middle = partner_part(
        (3, 6), ("major1", "minor1", "minor3", "nearest"), (part_low,)
    )
    part_late = partner_part((6, 9), ("major3", "minor1", "minor3", "nearest"), (part_middle,))
    part_low = lax.ppermute(part_low, "frame", partner_moves)
    part_middle = lax.ppermute(part_middle, "frame", partner_moves)
    own_late = own_part((6, 12), ("major3", "minor1", "minor2"), (part_late,))
    part_late = lax.ppermute(part_late, "frame", partner_moves)
    part_high = partner_part(
        (9, 12),
        ("major3", "minor2", "minor4", "nearest"),
        (own_late[1], major4, part_low, *sib_weight),
    )
    part_high = lax.ppermute(part_high, "frame", partner_moves)
    own_low = own_part((0, 3), ("major1", "major2", "major4", "nearest"))
    weights = (*own_weight, *sib_weight)
    owns = (((0, 3), own_low), ((3, 6), own_early), ((6, 12), own_late))
    base = project(
        (0, 9),
        owns,
        (((0, 3), part_low), ((3, 6), part_middle), ((6, 9), part_late)),
        weights,
        None,
        jnp.float32,
    )
    return project(
        (9, 12), (((6, 12), own_late),), (((9, 12), part_high),), weights, base, jnp.bfloat16
    )


def solution(mesh):
    in_specs = (
        P(("clip", "frame", "head"), None),
        P(("clip", "frame", "head"), None),
        P(("clip", "frame", "head"), None),
        P(),
        P("head", None),
    )
    out_specs = P(("clip", "frame", "head"), None)
    return jax.shard_map(
        per_device, mesh=mesh, in_specs=in_specs, out_specs=out_specs, check_vma=False
    )
```

```python
import functools
import math

import jax
import jax.numpy as jnp
from jax import lax
from jax.experimental import pallas as pl
from jax.experimental.pallas import tpu as pltpu
from jax.sharding import PartitionSpec as P

DH = 128
BS = 128
CROSS = 3
BATCH = 6
TILE = 768
NEG = -1e30
LOG2_SCALE = math.log2(math.e) / math.sqrt(DH)
MIB = 1024 * 1024


def frame_ids():
    frame = lax.axis_index("frame")
    return frame, 1 - 2 * lax.rem(frame, 2)


def entry(table_ref, query_frame, key_frame):
    frames = table_ref.shape[0]
    inside = (key_frame >= 0) & (key_frame < frames)
    count = table_ref[query_frame, jnp.clip(key_frame, 0, frames - 1)]
    return jnp.where(inside, count, 0)


def attend(problems):
    scores = []
    for query, parts in problems:
        row = []
        for keys, _, valid in parts:
            raw = lax.dot_general(
                query, keys, (((1,), (1,)), ((), ())), preferred_element_type=jnp.float32
            )
            row.append(raw if valid is None else jnp.where(valid, raw, NEG))
        scores.append(row)
    tops = []
    for row in scores:
        best = None
        for raw in row:
            for at in range(0, raw.shape[1], BS):
                piece = raw[:, at : at + BS]
                best = piece if best is None else jnp.maximum(best, piece)
        tops.append(best.max(axis=1, keepdims=True))
    weights = [
        [jnp.exp2((raw - top) * LOG2_SCALE) for raw in row] for row, top in zip(scores, tops)
    ]
    totals = []
    for row in weights:
        total = None
        for weight in row:
            for at in range(0, weight.shape[1], BS):
                piece = weight[:, at : at + BS]
                total = piece if total is None else total + piece
        totals.append(total.sum(axis=1, keepdims=True))
    results = []
    for (_, parts), row, top, total in zip(problems, weights, tops, totals):
        blended = 0.0
        for (_, values, _), weight in zip(parts, row):
            blended = blended + jnp.dot(
                weight.astype(jnp.bfloat16), values, preferred_element_type=jnp.float32
            )
        results.append((blended / total, top * LOG2_SCALE + jnp.log2(total)))
    return results


def attend_heads(group, blocks, problem, out):
    rows = blocks * BS
    heads = range(*group)
    lanes = lax.broadcasted_iota(jnp.int32, (rows, DH), 1)
    stats = jnp.zeros((rows, DH), jnp.float32)
    items = [(place, head, block) for place, head in enumerate(heads) for block in range(blocks)]
    sums = {}
    for at in range(0, len(items), BATCH):
        chunk = items[at : at + BATCH]
        results = attend([problem(head, block) for _, head, block in chunk])
        for (place, head, block), (blended, logsum) in zip(chunk, results):
            out[block * BS : (block + 1) * BS, head_cols(place)] = blended.astype(out.dtype)
            sums[place, block] = logsum
    for place in range(len(heads)):
        column = jnp.concatenate([sums[place, block] for block in range(blocks)], axis=0)
        stats = jnp.where(lanes == place, column, stats)
    return stats


def head_cols(head):
    return slice(head * DH, (head + 1) * DH)


def stat_rows(heads):
    return (4, 16) if heads <= 4 else (8, 32)


def write_stats(out, stats, heads):
    pad, count = stat_rows(heads)
    rows = stats.shape[0]
    packed, rest = 0.0, stats
    for part in range(3):
        piece = rest.astype(jnp.bfloat16).astype(jnp.float32)
        rest = rest - piece
        packed = packed + (pltpu.roll(piece, part * pad, 1) if part else piece)
    out[rows:, :] = jnp.zeros((count, out.shape[1]), out.dtype)
    out[rows:, :rows] = packed.T[:count].astype(out.dtype)


def read_stats(ref, heads):
    pad, count = stat_rows(heads)
    rows = ref.shape[0] - count
    packed = ref[rows:, :rows].astype(jnp.float32)
    padding = jnp.zeros((DH - count, rows), jnp.float32)
    packed = jnp.concatenate([packed, padding], axis=0).T
    return packed + pltpu.roll(packed, DH - pad, 1) + pltpu.roll(packed, DH - 2 * pad, 1)


def pair(ref, col, block):
    rows = ref.shape[0] // 2
    cols = head_cols(col)
    return (
        ref[block * BS : (block + 1) * BS, cols],
        ref[rows + block * BS : rows + (block + 1) * BS, cols],
    )


class Buffers:
    def __init__(self, refs):
        self.refs = refs

    def cross(self, head, block):
        return pair(self.refs["major2"], head, block)

    def far(self, head, block):
        return pair(self.refs["major4"], head, block)

    def away(self, head, block):
        if head < 6:
            return pair(self.refs["major1"], head, block)
        return pair(self.refs["major3"], head - 6, block)

    def near(self, head, block):
        if head < 9:
            return pair(self.refs["minor1"], head - 3, block)
        return pair(self.refs["minor2"], head - 9, block)

    def near_first(self, head):
        return pair(self.refs["nearest"], head - 3, 0)

    def cross_first(self, head):
        return pair(self.refs["nearest"], 9 + head, 0)

    def relay(self, head, block):
        if head < 9:
            return pair(self.refs["minor3"], head - 3, block)
        return pair(self.refs["minor4"], head - 9, block)


def partner_kernel(group, names, table_ref, query, keys, values, sib_keys, sib_values, *rest):
    frame, sign = frame_ids()
    buffers = Buffers(dict(zip(names, rest)))
    out = rest[-1]
    rows = query.shape[0]
    blocks = rows // BS
    partner = frame + sign
    own_count = entry(table_ref, partner, frame)
    near_count = entry(table_ref, partner, frame + 2 * sign)
    away_valid = entry(table_ref, partner, frame - 2 * sign) > 0
    relay_valid = entry(table_ref, partner, frame + 4 * sign) > 0
    cross_valid = entry(table_ref, partner, frame - sign) > 0

    def problem(head, block):
        mine = slice(block * BS, (block + 1) * BS)
        cols = head_cols(head)
        last = block + 1 == blocks
        parts = [(keys[mine, cols], values[mine, cols], None)]
        if last:
            parts.append((sib_keys[:BS, cols], sib_values[:BS, cols], own_count > 1))
        else:
            after = slice((block + 1) * BS, (block + 2) * BS)
            parts.append((keys[after, cols], values[after, cols], own_count > 1))
        parts.append((*buffers.away(head, block), away_valid))
        if head < CROSS:
            parts.append((*buffers.cross(head, block), cross_valid))
        else:
            parts.append((*buffers.near(head, block), near_count > 0))
            after = buffers.near_first(head) if last else buffers.near(head, block + 1)
            parts.append((*after, near_count > 1))
            parts.append((*buffers.relay(head, block), relay_valid))
        return query[mine, cols], parts

    stats = attend_heads(group, blocks, problem, out)
    write_stats(out, stats, group[1] - group[0])


def own_kernel(group, names, table_ref, query, keys, values, sib_keys, sib_values, *rest):
    frame, sign = frame_ids()
    buffers = Buffers(dict(zip(names, rest)))
    out, out_stats = rest[-2:]
    rows = query.shape[0]
    blocks = rows // BS
    near_valid = entry(table_ref, frame, frame + 2 * sign) > 0
    away_valid = entry(table_ref, frame, frame - 2 * sign) > 0
    cross_count = entry(table_ref, frame, frame - sign)
    far_valid = entry(table_ref, frame, frame - 3 * sign) > 0

    def problem(head, block):
        mine = slice(block * BS, (block + 1) * BS)
        cols = head_cols(head)
        parts = [
            (keys[:, cols], values[:, cols], None),
            (sib_keys[:, cols], sib_values[:, cols], None),
            (*buffers.away(head, block), away_valid),
        ]
        if head < CROSS:
            last = block + 1 == blocks
            parts.append((*buffers.cross(head, block), cross_count > 0))
            after = buffers.cross_first(head) if last else buffers.cross(head, block + 1)
            parts.append((*after, cross_count > 1))
            parts.append((*buffers.far(head, block), far_valid))
        else:
            parts.append((*buffers.near(head, block), near_valid))
        return query[mine, cols], parts

    out_stats[...] = attend_heads(group, blocks, problem, out)


def project_kernel(span, own_groups, part_groups, has_base, *refs):
    refs = list(refs)
    weight, sib_weight = refs.pop(0), refs.pop(0)
    owns = [(group, refs.pop(0), refs.pop(0)) for group in own_groups]
    parts = [(group, refs.pop(0)) for group in part_groups]
    base = refs.pop(0) if has_base else None
    out, attended = refs
    rows = out.shape[0]
    lanes = lax.broadcasted_iota(jnp.int32, (rows, DH), 1)
    own_at, part_at = {}, {}
    own_sum = part_sum = jnp.zeros((rows, DH), jnp.float32)
    for (first, last), own, stats in owns:
        shifted = pltpu.roll(stats[...], first, 1) if first else stats[...]
        own_sum = jnp.where((lanes >= first) & (lanes < last), shifted, own_sum)
        own_at.update({head: (own, head - first) for head in range(first, last)})
    for (first, last), part in parts:
        stats = read_stats(part, last - first)
        shifted = pltpu.roll(stats, first, 1) if first else stats
        part_sum = jnp.where((lanes >= first) & (lanes < last), shifted, part_sum)
        part_at.update({head: (part, head - first) for head in range(first, last)})
    top = jnp.maximum(own_sum, part_sum)
    own_weight = jnp.exp2(own_sum - top)
    part_weight = jnp.exp2(part_sum - top)
    inverse = 1.0 / (own_weight + part_weight)
    own_weight = own_weight * inverse
    part_weight = part_weight * inverse
    for head in range(*span):
        own, own_place = own_at[head]
        part, part_place = part_at[head]
        mixed = own_weight[:, head : head + 1] * own[:, head_cols(own_place)] + part_weight[
            :, head : head + 1
        ] * part[:rows, head_cols(part_place)].astype(jnp.float32)
        attended[:, head_cols(head - span[0])] = mixed.astype(attended.dtype)

    depth = weight.shape[0]
    start, stop = span[0] * DH, span[1] * DH

    def multiply(halves):
        for at in range(0, out.shape[1], TILE):
            product = base[:, at : at + TILE] if has_base else 0.0
            for index, half in enumerate(halves):
                low, high = max(start, index * depth), min(stop, (index + 1) * depth)
                if low < high:
                    product = product + jnp.dot(
                        attended[:, low - start : high - start],
                        half[low - index * depth : high - index * depth, at : at + TILE],
                        preferred_element_type=jnp.float32,
                    )
            out[:, at : at + TILE] = product.astype(out.dtype)

    core = lax.axis_index("head")

    @pl.when(core == 0)
    def _():
        multiply((weight, sib_weight))

    @pl.when(core != 0)
    def _():
        multiply((sib_weight, weight))


def whole(shape):
    return pl.BlockSpec(shape, lambda i: (0,) * len(shape))


def run(body, name, table, operands, out_shapes, flops, after=()):
    return pl.pallas_call(
        body,
        grid=(1,),
        in_specs=[pl.BlockSpec(memory_space=pltpu.SMEM)]
        + [whole(x.shape) for x in operands]
        + [pl.BlockSpec(memory_space=pl.ANY)] * len(after),
        out_specs=[whole(s.shape) for s in out_shapes],
        out_shape=out_shapes,
        compiler_params=pltpu.CompilerParams(vmem_limit_bytes=8 * MIB),
        cost_estimate=pl.CostEstimate(
            flops=flops, bytes_accessed=MIB, transcendentals=flops // 512
        ),
        name=name,
    )(table, *operands, *after)


def tie_kernel(*refs):
    del refs


def tie(before, *payloads):
    before = tuple(before)
    anywhere = pl.BlockSpec(memory_space=pl.ANY)
    return pl.pallas_call(
        tie_kernel,
        in_specs=[anywhere] * (len(before) + len(payloads)),
        out_specs=[anywhere] * len(payloads),
        out_shape=[jax.ShapeDtypeStruct(p.shape, p.dtype) for p in payloads],
        input_output_aliases={len(before) + i: i for i in range(len(payloads))},
        compiler_params=pltpu.CompilerParams(vmem_limit_bytes=MIB),
        name="tie",
    )(*before, *payloads)


def project(span, owns, parts, weights, base, dtype):
    rows, columns = owns[0][1][0].shape[0], weights[0].shape[1]
    depth = (span[1] - span[0]) * DH
    operands = [*weights]
    for _, own in owns:
        operands += own
    operands += [part for _, part in parts]
    if base is not None:
        operands.append(base)
    return pl.pallas_call(
        functools.partial(
            project_kernel,
            span,
            tuple(group for group, _ in owns),
            tuple(group for group, _ in parts),
            base is not None,
        ),
        grid=(1,),
        in_specs=[whole(x.shape) for x in operands],
        out_specs=whole((rows, columns)),
        out_shape=jax.ShapeDtypeStruct((rows, columns), dtype),
        scratch_shapes=[pltpu.VMEM((rows, depth), jnp.bfloat16)],
        compiler_params=pltpu.CompilerParams(vmem_limit_bytes=8 * MIB),
        cost_estimate=pl.CostEstimate(
            flops=2 * rows * depth * columns, bytes_accessed=4 * MIB, transcendentals=0
        ),
        name="merge_and_project",
    )(*operands)


def per_device(queries, key_tokens, value_tokens, radial_table, out_weight):
    frames = lax.axis_size("frame")
    cores = lax.axis_size("head")
    rows = queries.shape[0]

    def moves(target):
        return [(f, target(f)) for f in range(frames) if 0 <= target(f) < frames]

    partner_moves = moves(lambda f: f ^ 1)
    near_moves = moves(lambda f: f - 2 if f % 2 == 0 else f + 2)
    away_moves = moves(lambda f: f + 2 if f % 2 == 0 else f - 2)
    cross_moves = moves(lambda f: f - 1 if f % 2 == 0 else f + 1)
    core_moves = [(c, cores - 1 - c) for c in range(cores)]

    def pack(first, last):
        cols = slice(first * DH, last * DH)
        return jnp.concatenate([key_tokens[:, cols], value_tokens[:, cols]], axis=0)

    def firsts(*packed):
        return jnp.concatenate(
            [jnp.concatenate([p[at : at + BS] for p in packed], axis=1) for at in (0, rows)],
            axis=0,
        )

    major1 = lax.ppermute(pack(0, 6), "frame", away_moves)
    minor1 = lax.ppermute(pack(3, 9), "frame", near_moves)
    own_weight = [out_weight]
    sib_weight = [lax.ppermute(out_weight, "head", core_moves)]
    cross = lax.ppermute(pack(0, 3), "frame", partner_moves)
    cross, to_minor2 = tie(sib_weight, cross, pack(9, 12))
    minor2 = lax.ppermute(to_minor2, "frame", near_moves)
    partner_query = lax.ppermute(queries, "frame", partner_moves)
    major2 = lax.ppermute(cross, "frame", away_moves)
    minor3 = lax.ppermute(minor1, "frame", near_moves)
    (to_major3,) = tie((major1,), pack(6, 12))
    major3 = lax.ppermute(to_major3, "frame", away_moves)
    major4 = lax.ppermute(major2, "frame", away_moves)
    minor4 = lax.ppermute(minor2, "frame", near_moves)
    to_sib_keys, to_sib_values = tie((major2, partner_query, minor2), key_tokens, value_tokens)
    sib_keys = lax.ppermute(to_sib_keys, "head", core_moves)
    sib_values = lax.ppermute(to_sib_values, "head", core_moves)
    nearest = lax.ppermute(firsts(minor1, minor2, major2), "head", core_moves)
    refs = {
        "major1": major1,
        "major2": major2,
        "major3": major3,
        "major4": major4,
        "minor1": minor1,
        "minor2": minor2,
        "minor3": minor3,
        "minor4": minor4,
        "nearest": nearest,
    }
    local = (key_tokens, value_tokens, sib_keys, sib_values)

    def partner_part(group, names, after=()):
        heads = group[1] - group[0]
        shape = jax.ShapeDtypeStruct((rows + stat_rows(heads)[1], heads * DH), jnp.bfloat16)
        (part,) = run(
            functools.partial(partner_kernel, group, names),
            "partner_part",
            radial_table,
            (partner_query, *local, *(refs[n] for n in names)),
            [shape],
            heads * rows * 6 * BS * DH * 4,
            after,
        )
        return part

    def own_part(group, names, after=()):
        heads = group[1] - group[0]
        return run(
            functools.partial(own_kernel, group, names),
            "own_part",
            radial_table,
            (queries, *local, *(refs[n] for n in names)),
            [
                jax.ShapeDtypeStruct((rows, heads * DH), jnp.float32),
                jax.ShapeDtypeStruct((rows, DH), jnp.float32),
            ],
            heads * rows * 6 * BS * DH * 4,
            after,
        )

    part_low = partner_part((0, 3), ("major1", "major2"))
    own_early = own_part((3, 6), ("major1", "minor1"))
    part_middle = partner_part(
        (3, 6), ("major1", "minor1", "minor3", "nearest"), (part_low, own_early[1], major3)
    )
    part_late = partner_part((6, 9), ("major3", "minor1", "minor3", "nearest"), (part_middle,))
    part_low = lax.ppermute(part_low, "frame", partner_moves)
    part_middle = lax.ppermute(part_middle, "frame", partner_moves)
    part_late = lax.ppermute(part_late, "frame", partner_moves)
    own_late = own_part((6, 12), ("major3", "minor1", "minor2"))
    part_high = partner_part(
        (9, 12),
        ("major3", "minor2", "minor4", "nearest"),
        (own_late[1], major4, part_low, *sib_weight),
    )
    part_high = lax.ppermute(part_high, "frame", partner_moves)
    own_low = own_part((0, 3), ("major1", "major2", "major4", "nearest"))
    weights = (*own_weight, *sib_weight)
    owns = (((0, 3), own_low), ((3, 6), own_early), ((6, 12), own_late))
    base = project(
        (0, 9),
        owns,
        (((0, 3), part_low), ((3, 6), part_middle), ((6, 9), part_late)),
        weights,
        None,
        jnp.float32,
    )
    return project(
        (9, 12), (((6, 12), own_late),), (((9, 12), part_high),), weights, base, jnp.bfloat16
    )


def solution(mesh):
    in_specs = (
        P(("clip", "frame", "head"), None),
        P(("clip", "frame", "head"), None),
        P(("clip", "frame", "head"), None),
        P(),
        P("head", None),
    )
    out_specs = P(("clip", "frame", "head"), None)
    return jax.shard_map(
        per_device, mesh=mesh, in_specs=in_specs, out_specs=out_specs, check_vma=False
    )
```

```python
import functools
import math

import jax
import jax.numpy as jnp
from jax import lax
from jax.experimental import pallas as pl
from jax.experimental.pallas import tpu as pltpu
from jax.sharding import PartitionSpec as P

DH = 128
BS = 128
CROSS = 3
BATCH = 6
TILE = 768
NEG = -1e30
LOG2_SCALE = math.log2(math.e) / math.sqrt(DH)
MIB = 1024 * 1024


def frame_ids():
    frame = lax.axis_index("frame")
    return frame, 1 - 2 * lax.rem(frame, 2)


def entry(table_ref, query_frame, key_frame):
    frames = table_ref.shape[0]
    inside = (key_frame >= 0) & (key_frame < frames)
    count = table_ref[query_frame, jnp.clip(key_frame, 0, frames - 1)]
    return jnp.where(inside, count, 0)


def attend(problems):
    scores = []
    for query, parts in problems:
        row = []
        for keys, _, valid in parts:
            raw = lax.dot_general(
                query, keys, (((1,), (1,)), ((), ())), preferred_element_type=jnp.float32
            )
            count = keys.shape[0] // BS
            valid = valid if isinstance(valid, tuple) else (valid,) * count
            pieces = [raw[:, index * BS : (index + 1) * BS] for index in range(count)]
            row.append(
                [
                    piece if allowed is None else jnp.where(allowed, piece, NEG)
                    for piece, allowed in zip(pieces, valid)
                ]
            )
        scores.append(row)
    tops = []
    for row in scores:
        best = None
        for piece in sum(row, []):
            best = piece if best is None else jnp.maximum(best, piece)
        tops.append(best.max(axis=1, keepdims=True))
    weights = [
        [[jnp.exp2((piece - top) * LOG2_SCALE) for piece in pieces] for pieces in row]
        for row, top in zip(scores, tops)
    ]
    totals = []
    for row in weights:
        total = None
        for piece in sum(row, []):
            total = piece if total is None else total + piece
        totals.append(total.sum(axis=1, keepdims=True))
    results = []
    for (_, parts), row, top, total in zip(problems, weights, tops, totals):
        blended = 0.0
        for (_, values, _), pieces in zip(parts, row):
            weight = [piece.astype(jnp.bfloat16) for piece in pieces]
            weight = weight[0] if len(weight) == 1 else jnp.concatenate(weight, axis=1)
            blended = blended + jnp.dot(weight, values, preferred_element_type=jnp.float32)
        results.append((blended / total, top * LOG2_SCALE + jnp.log2(total)))
    return results


def attend_heads(group, blocks, problem, out):
    rows = blocks * BS
    heads = range(*group)
    lanes = lax.broadcasted_iota(jnp.int32, (rows, DH), 1)
    stats = jnp.zeros((rows, DH), jnp.float32)
    items = [(place, head, block) for place, head in enumerate(heads) for block in range(blocks)]
    sums = {}
    for at in range(0, len(items), BATCH):
        chunk = items[at : at + BATCH]
        results = attend([problem(head, block) for _, head, block in chunk])
        for (place, head, block), (blended, logsum) in zip(chunk, results):
            out[block * BS : (block + 1) * BS, head_cols(place)] = blended.astype(out.dtype)
            sums[place, block] = logsum
    for place in range(len(heads)):
        column = jnp.concatenate([sums[place, block] for block in range(blocks)], axis=0)
        stats = jnp.where(lanes == place, column, stats)
    return stats


def head_cols(head):
    return slice(head * DH, (head + 1) * DH)


def stat_rows(heads):
    return (4, 16) if heads <= 4 else (8, 32)


def write_stats(out, stats, heads):
    pad, count = stat_rows(heads)
    rows = stats.shape[0]
    packed, rest = 0.0, stats
    for part in range(3):
        piece = rest.astype(jnp.bfloat16).astype(jnp.float32)
        rest = rest - piece
        packed = packed + (pltpu.roll(piece, part * pad, 1) if part else piece)
    out[rows:, :] = jnp.zeros((count, out.shape[1]), out.dtype)
    out[rows:, :rows] = packed.T[:count].astype(out.dtype)


def read_stats(ref, heads):
    pad, count = stat_rows(heads)
    rows = ref.shape[0] - count
    packed = ref[rows:, :rows].astype(jnp.float32)
    padding = jnp.zeros((DH - count, rows), jnp.float32)
    packed = jnp.concatenate([packed, padding], axis=0).T
    return packed + pltpu.roll(packed, DH - pad, 1) + pltpu.roll(packed, DH - 2 * pad, 1)


def pair(ref, col, block, count=1):
    rows = ref.shape[0] // 2
    cols = head_cols(col)
    return (
        ref[block * BS : (block + count) * BS, cols],
        ref[rows + block * BS : rows + (block + count) * BS, cols],
    )


class Buffers:
    def __init__(self, refs):
        self.refs = refs

    def cross(self, head, block, count=1):
        return pair(self.refs["major2"], head, block, count)

    def far(self, head, block):
        return pair(self.refs["major4"], head, block)

    def away(self, head, block):
        if head < 6:
            return pair(self.refs["major1"], head, block)
        return pair(self.refs["major3"], head - 6, block)

    def near(self, head, block, count=1):
        if head < 9:
            return pair(self.refs["minor1"], head - 3, block, count)
        return pair(self.refs["minor2"], head - 9, block, count)

    def near_first(self, head):
        return pair(self.refs["nearest"], head - 3, 0)

    def cross_first(self, head):
        return pair(self.refs["nearest"], 9 + head, 0)

    def relay(self, head, block):
        if head < 9:
            return pair(self.refs["minor3"], head - 3, block)
        return pair(self.refs["minor4"], head - 9, block)


def partner_kernel(group, names, table_ref, query, keys, values, sib_keys, sib_values, *rest):
    frame, sign = frame_ids()
    buffers = Buffers(dict(zip(names, rest)))
    out = rest[-1]
    rows = query.shape[0]
    blocks = rows // BS
    partner = frame + sign
    own_count = entry(table_ref, partner, frame)
    near_count = entry(table_ref, partner, frame + 2 * sign)
    away_valid = entry(table_ref, partner, frame - 2 * sign) > 0
    relay_valid = entry(table_ref, partner, frame + 4 * sign) > 0
    cross_valid = entry(table_ref, partner, frame - sign) > 0

    def problem(head, block):
        mine = slice(block * BS, (block + 1) * BS)
        cols = head_cols(head)
        last = block + 1 == blocks
        if last:
            parts = [(keys[mine, cols], values[mine, cols], None)]
            parts.append((sib_keys[:BS, cols], sib_values[:BS, cols], own_count > 1))
        else:
            both = slice(block * BS, (block + 2) * BS)
            parts = [(keys[both, cols], values[both, cols], (None, own_count > 1))]
        parts.append((*buffers.away(head, block), away_valid))
        if head < CROSS:
            parts.append((*buffers.cross(head, block), cross_valid))
        else:
            if last:
                parts.append((*buffers.near(head, block), near_count > 0))
                parts.append((*buffers.near_first(head), near_count > 1))
            else:
                allowed = (near_count > 0, near_count > 1)
                parts.append((*buffers.near(head, block, 2), allowed))
            parts.append((*buffers.relay(head, block), relay_valid))
        return query[mine, cols], parts

    stats = attend_heads(group, blocks, problem, out)
    write_stats(out, stats, group[1] - group[0])


def own_kernel(group, names, table_ref, query, keys, values, sib_keys, sib_values, *rest):
    frame, sign = frame_ids()
    buffers = Buffers(dict(zip(names, rest)))
    out, out_stats = rest[-2:]
    rows = query.shape[0]
    blocks = rows // BS
    near_valid = entry(table_ref, frame, frame + 2 * sign) > 0
    away_valid = entry(table_ref, frame, frame - 2 * sign) > 0
    cross_count = entry(table_ref, frame, frame - sign)
    far_valid = entry(table_ref, frame, frame - 3 * sign) > 0

    def problem(head, block):
        mine = slice(block * BS, (block + 1) * BS)
        cols = head_cols(head)
        parts = [
            (keys[:, cols], values[:, cols], None),
            (sib_keys[:, cols], sib_values[:, cols], None),
            (*buffers.away(head, block), away_valid),
        ]
        if head < CROSS:
            last = block + 1 == blocks
            if last:
                parts.append((*buffers.cross(head, block), cross_count > 0))
                parts.append((*buffers.cross_first(head), cross_count > 1))
            else:
                allowed = (cross_count > 0, cross_count > 1)
                parts.append((*buffers.cross(head, block, 2), allowed))
            parts.append((*buffers.far(head, block), far_valid))
        else:
            parts.append((*buffers.near(head, block), near_valid))
        return query[mine, cols], parts

    out_stats[...] = attend_heads(group, blocks, problem, out)


def project_kernel(span, own_groups, part_groups, has_base, *refs):
    refs = list(refs)
    weight, sib_weight = refs.pop(0), refs.pop(0)
    owns = [(group, refs.pop(0), refs.pop(0)) for group in own_groups]
    parts = [(group, refs.pop(0)) for group in part_groups]
    base = refs.pop(0) if has_base else None
    if has_base:
        target, attended, out, sems = refs
    else:
        out, attended = refs
    rows = out.shape[0]
    lanes = lax.broadcasted_iota(jnp.int32, (rows, DH), 1)
    own_at, part_at = {}, {}
    own_sum = part_sum = jnp.zeros((rows, DH), jnp.float32)
    for (first, last), own, stats in owns:
        shifted = pltpu.roll(stats[...], first, 1) if first else stats[...]
        own_sum = jnp.where((lanes >= first) & (lanes < last), shifted, own_sum)
        own_at.update({head: (own, head - first) for head in range(first, last)})
    for (first, last), part in parts:
        stats = read_stats(part, last - first)
        shifted = pltpu.roll(stats, first, 1) if first else stats
        part_sum = jnp.where((lanes >= first) & (lanes < last), shifted, part_sum)
        part_at.update({head: (part, head - first) for head in range(first, last)})
    top = jnp.maximum(own_sum, part_sum)
    own_weight = jnp.exp2(own_sum - top)
    part_weight = jnp.exp2(part_sum - top)
    inverse = 1.0 / (own_weight + part_weight)
    own_weight = own_weight * inverse
    part_weight = part_weight * inverse
    for head in range(*span):
        own, own_place = own_at[head]
        part, part_place = part_at[head]
        mixed = own_weight[:, head : head + 1] * own[:, head_cols(own_place)] + part_weight[
            :, head : head + 1
        ] * part[:rows, head_cols(part_place)].astype(jnp.float32)
        attended[:, head_cols(head - span[0])] = mixed.astype(attended.dtype)

    depth = weight.shape[0]
    start, stop = span[0] * DH, span[1] * DH

    def multiply(halves):
        for at in range(0, out.shape[1], TILE):
            product = base[:, at : at + TILE] if has_base else 0.0
            for index, half in enumerate(halves):
                low, high = max(start, index * depth), min(stop, (index + 1) * depth)
                if low < high:
                    product = product + jnp.dot(
                        attended[:, low - start : high - start],
                        half[low - index * depth : high - index * depth, at : at + TILE],
                        preferred_element_type=jnp.float32,
                    )
            out[:, at : at + TILE] = product.astype(out.dtype)
            if has_base:
                copy_out(at).start()

    def copy_out(at):
        cols = slice(at, at + TILE)
        return pltpu.make_async_copy(out.at[:, cols], target.at[:, cols], sems.at[at // TILE])

    core = lax.axis_index("head")

    @pl.when(core == 0)
    def _():
        multiply((weight, sib_weight))

    @pl.when(core != 0)
    def _():
        multiply((sib_weight, weight))

    if has_base:
        for at in range(0, out.shape[1], TILE):
            copy_out(at).wait()


def whole(shape):
    return pl.BlockSpec(shape, lambda i: (0,) * len(shape))


def run(body, name, table, operands, out_shapes, flops, after=()):
    return pl.pallas_call(
        body,
        grid=(1,),
        in_specs=[pl.BlockSpec(memory_space=pltpu.SMEM)]
        + [whole(x.shape) for x in operands]
        + [pl.BlockSpec(memory_space=pl.ANY)] * len(after),
        out_specs=[whole(s.shape) for s in out_shapes],
        out_shape=out_shapes,
        compiler_params=pltpu.CompilerParams(vmem_limit_bytes=8 * MIB),
        cost_estimate=pl.CostEstimate(
            flops=flops, bytes_accessed=MIB, transcendentals=flops // 512
        ),
        name=name,
    )(table, *operands, *after)


def tie_kernel(*refs):
    del refs


def tie(before, *payloads):
    before = tuple(before)
    anywhere = pl.BlockSpec(memory_space=pl.ANY)
    return pl.pallas_call(
        tie_kernel,
        in_specs=[anywhere] * (len(before) + len(payloads)),
        out_specs=[anywhere] * len(payloads),
        out_shape=[jax.ShapeDtypeStruct(p.shape, p.dtype) for p in payloads],
        input_output_aliases={len(before) + i: i for i in range(len(payloads))},
        compiler_params=pltpu.CompilerParams(vmem_limit_bytes=MIB),
        name="tie",
    )(*before, *payloads)


def project(span, owns, parts, weights, base, dtype):
    rows, columns = owns[0][1][0].shape[0], weights[0].shape[1]
    depth = (span[1] - span[0]) * DH
    operands = [*weights]
    for _, own in owns:
        operands += own
    operands += [part for _, part in parts]
    streams = []
    if base is not None:
        operands.append(base)
        streams = [
            pltpu.VMEM((rows, columns), dtype),
            pltpu.SemaphoreType.DMA((columns // TILE,)),
        ]
    return pl.pallas_call(
        functools.partial(
            project_kernel,
            span,
            tuple(group for group, _ in owns),
            tuple(group for group, _ in parts),
            base is not None,
        ),
        grid=(1,),
        in_specs=[whole(x.shape) for x in operands],
        out_specs=whole((rows, columns)) if base is None else pl.BlockSpec(memory_space=pl.ANY),
        out_shape=jax.ShapeDtypeStruct((rows, columns), dtype),
        scratch_shapes=[pltpu.VMEM((rows, depth), jnp.bfloat16), *streams],
        compiler_params=pltpu.CompilerParams(vmem_limit_bytes=8 * MIB),
        cost_estimate=pl.CostEstimate(
            flops=2 * rows * depth * columns, bytes_accessed=4 * MIB, transcendentals=0
        ),
        name="merge_and_project",
    )(*operands)


def per_device(queries, key_tokens, value_tokens, radial_table, out_weight):
    frames = lax.axis_size("frame")
    cores = lax.axis_size("head")
    rows = queries.shape[0]

    def moves(target):
        return [(f, target(f)) for f in range(frames) if 0 <= target(f) < frames]

    partner_moves = moves(lambda f: f ^ 1)
    near_moves = moves(lambda f: f - 2 if f % 2 == 0 else f + 2)
    away_moves = moves(lambda f: f + 2 if f % 2 == 0 else f - 2)
    cross_moves = moves(lambda f: f - 1 if f % 2 == 0 else f + 1)
    core_moves = [(c, cores - 1 - c) for c in range(cores)]

    def pack(first, last):
        cols = slice(first * DH, last * DH)
        return jnp.concatenate([key_tokens[:, cols], value_tokens[:, cols]], axis=0)

    def firsts(*packed):
        return jnp.concatenate(
            [jnp.concatenate([p[at : at + BS] for p in packed], axis=1) for at in (0, rows)],
            axis=0,
        )

    major1 = lax.ppermute(pack(0, 6), "frame", away_moves)
    minor1 = lax.ppermute(pack(3, 9), "frame", near_moves)
    own_weight = [out_weight]
    sib_weight = [lax.ppermute(out_weight, "head", core_moves)]
    cross = lax.ppermute(pack(0, 3), "frame", partner_moves)
    cross, to_minor2 = tie(sib_weight, cross, pack(9, 12))
    minor2 = lax.ppermute(to_minor2, "frame", near_moves)
    partner_query = lax.ppermute(queries, "frame", partner_moves)
    major2 = lax.ppermute(cross, "frame", away_moves)
    minor3 = lax.ppermute(minor1, "frame", near_moves)
    (to_major3,) = tie((major1,), pack(6, 12))
    major3 = lax.ppermute(to_major3, "frame", away_moves)
    major4 = lax.ppermute(major2, "frame", away_moves)
    minor4 = lax.ppermute(minor2, "frame", near_moves)
    to_sib_keys, to_sib_values = tie((major2, partner_query, minor2), key_tokens, value_tokens)
    sib_keys = lax.ppermute(to_sib_keys, "head", core_moves)
    sib_values = lax.ppermute(to_sib_values, "head", core_moves)
    nearest = lax.ppermute(firsts(minor1, minor2, major2), "head", core_moves)
    refs = {
        "major1": major1,
        "major2": major2,
        "major3": major3,
        "major4": major4,
        "minor1": minor1,
        "minor2": minor2,
        "minor3": minor3,
        "minor4": minor4,
        "nearest": nearest,
    }
    local = (key_tokens, value_tokens, sib_keys, sib_values)

    def partner_part(group, names, after=()):
        heads = group[1] - group[0]
        shape = jax.ShapeDtypeStruct((rows + stat_rows(heads)[1], heads * DH), jnp.bfloat16)
        (part,) = run(
            functools.partial(partner_kernel, group, names),
            "partner_part",
            radial_table,
            (partner_query, *local, *(refs[n] for n in names)),
            [shape],
            heads * rows * 6 * BS * DH * 4,
            after,
        )
        return part

    def own_part(group, names, after=()):
        heads = group[1] - group[0]
        return run(
            functools.partial(own_kernel, group, names),
            "own_part",
            radial_table,
            (queries, *local, *(refs[n] for n in names)),
            [
                jax.ShapeDtypeStruct((rows, heads * DH), jnp.float32),
                jax.ShapeDtypeStruct((rows, DH), jnp.float32),
            ],
            heads * rows * 6 * BS * DH * 4,
            after,
        )

    part_low = partner_part((0, 3), ("major1", "major2"))
    own_early = own_part((3, 6), ("major1", "minor1"))
    part_middle = partner_part(
        (3, 6), ("major1", "minor1", "minor3", "nearest"), (part_low, own_early[1], major3)
    )
    part_late = partner_part((6, 9), ("major3", "minor1", "minor3", "nearest"), (part_middle,))
    part_low = lax.ppermute(part_low, "frame", partner_moves)
    part_middle = lax.ppermute(part_middle, "frame", partner_moves)
    part_late = lax.ppermute(part_late, "frame", partner_moves)
    own_late = own_part((6, 12), ("major3", "minor1", "minor2"))
    part_high = partner_part(
        (9, 12),
        ("major3", "minor2", "minor4", "nearest"),
        (own_late[1], major4, part_low, *sib_weight),
    )
    part_high = lax.ppermute(part_high, "frame", partner_moves)
    own_low = own_part((0, 3), ("major1", "major2", "major4", "nearest"))
    weights = (*own_weight, *sib_weight)
    owns = (((0, 3), own_low), ((3, 6), own_early), ((6, 12), own_late))
    base = project(
        (0, 9),
        owns,
        (((0, 3), part_low), ((3, 6), part_middle), ((6, 9), part_late)),
        weights,
        None,
        jnp.float32,
    )
    return project(
        (9, 12), (((6, 12), own_late),), (((9, 12), part_high),), weights, base, jnp.bfloat16
    )


def solution(mesh):
    in_specs = (
        P(("clip", "frame", "head"), None),
        P(("clip", "frame", "head"), None),
        P(("clip", "frame", "head"), None),
        P(),
        P("head", None),
    )
    out_specs = P(("clip", "frame", "head"), None)
    return jax.shard_map(
        per_device, mesh=mesh, in_specs=in_specs, out_specs=out_specs, check_vma=False
    )
```

```python
import functools
import math

import jax
import jax.numpy as jnp
from jax import lax
from jax.experimental import pallas as pl
from jax.experimental.pallas import tpu as pltpu
from jax.sharding import PartitionSpec as P

DH = 128
BS = 128
CROSS = 3
BATCH = 6
TILE = 768
NEG = -1e30
LOG2_SCALE = math.log2(math.e) / math.sqrt(DH)
MIB = 1024 * 1024


def frame_ids():
    frame = lax.axis_index("frame")
    return frame, 1 - 2 * lax.rem(frame, 2)


def entry(table_ref, query_frame, key_frame):
    frames = table_ref.shape[0]
    inside = (key_frame >= 0) & (key_frame < frames)
    count = table_ref[query_frame, jnp.clip(key_frame, 0, frames - 1)]
    return jnp.where(inside, count, 0)


def attend(problems):
    scores = []
    for query, parts in problems:
        row = []
        for keys, _, valid in parts:
            raw = lax.dot_general(
                query, keys, (((1,), (1,)), ((), ())), preferred_element_type=jnp.float32
            )
            count = keys.shape[0] // BS
            valid = valid if isinstance(valid, tuple) else (valid,) * count
            pieces = [raw[:, index * BS : (index + 1) * BS] for index in range(count)]
            row.append(
                [
                    piece if allowed is None else jnp.where(allowed, piece, NEG)
                    for piece, allowed in zip(pieces, valid)
                ]
            )
        scores.append(row)
    tops = []
    for row in scores:
        best = None
        for piece in sum(row, []):
            best = piece if best is None else jnp.maximum(best, piece)
        tops.append(best.max(axis=1, keepdims=True))
    weights = [
        [[jnp.exp2((piece - top) * LOG2_SCALE) for piece in pieces] for pieces in row]
        for row, top in zip(scores, tops)
    ]
    totals = []
    for row in weights:
        total = None
        for piece in sum(row, []):
            total = piece if total is None else total + piece
        totals.append(total.sum(axis=1, keepdims=True))
    results = []
    for (_, parts), row, top, total in zip(problems, weights, tops, totals):
        blended = 0.0
        for (_, values, _), pieces in zip(parts, row):
            weight = [piece.astype(jnp.bfloat16) for piece in pieces]
            weight = weight[0] if len(weight) == 1 else jnp.concatenate(weight, axis=1)
            blended = blended + jnp.dot(weight, values, preferred_element_type=jnp.float32)
        results.append((blended / total, top * LOG2_SCALE + jnp.log2(total)))
    return results


def attend_heads(group, blocks, problem, out):
    rows = blocks * BS
    heads = range(*group)
    lanes = lax.broadcasted_iota(jnp.int32, (rows, DH), 1)
    stats = jnp.zeros((rows, DH), jnp.float32)
    items = [(place, head, block) for place, head in enumerate(heads) for block in range(blocks)]
    sums = {}
    for at in range(0, len(items), BATCH):
        chunk = items[at : at + BATCH]
        results = attend([problem(head, block) for _, head, block in chunk])
        for (place, head, block), (blended, logsum) in zip(chunk, results):
            out[block * BS : (block + 1) * BS, head_cols(place)] = blended.astype(out.dtype)
            sums[place, block] = logsum
    for place in range(len(heads)):
        column = jnp.concatenate([sums[place, block] for block in range(blocks)], axis=0)
        stats = jnp.where(lanes == place, column, stats)
    return stats


def head_cols(head):
    return slice(head * DH, (head + 1) * DH)


def stat_rows(heads):
    return (4, 16) if heads <= 4 else (8, 32)


def write_stats(out, stats, heads):
    pad, count = stat_rows(heads)
    rows = stats.shape[0]
    packed, rest = 0.0, stats
    for part in range(3):
        piece = rest.astype(jnp.bfloat16).astype(jnp.float32)
        rest = rest - piece
        packed = packed + (pltpu.roll(piece, part * pad, 1) if part else piece)
    out[rows:, :] = jnp.zeros((count, out.shape[1]), out.dtype)
    out[rows:, :rows] = packed.T[:count].astype(out.dtype)


def read_stats(ref, heads):
    pad, count = stat_rows(heads)
    rows = ref.shape[0] - count
    packed = ref[rows:, :rows].astype(jnp.float32)
    padding = jnp.zeros((DH - count, rows), jnp.float32)
    packed = jnp.concatenate([packed, padding], axis=0).T
    return packed + pltpu.roll(packed, DH - pad, 1) + pltpu.roll(packed, DH - 2 * pad, 1)


def pair(ref, col, block, count=1):
    rows = ref.shape[0] // 2
    cols = head_cols(col)
    return (
        ref[block * BS : (block + count) * BS, cols],
        ref[rows + block * BS : rows + (block + count) * BS, cols],
    )


class Buffers:
    def __init__(self, refs):
        self.refs = refs

    def cross(self, head, block, count=1):
        return pair(self.refs["major2"], head, block, count)

    def far(self, head, block):
        return pair(self.refs["major4"], head, block)

    def away(self, head, block):
        if head < 6:
            return pair(self.refs["major1"], head, block)
        return pair(self.refs["major3"], head - 6, block)

    def near(self, head, block, count=1):
        if head < 9:
            return pair(self.refs["minor1"], head - 3, block, count)
        return pair(self.refs["minor2"], head - 9, block, count)

    def near_first(self, head):
        return pair(self.refs["nearest"], head - 3, 0)

    def cross_first(self, head):
        return pair(self.refs["nearest"], 9 + head, 0)

    def relay(self, head, block):
        if head < 9:
            return pair(self.refs["minor3"], head - 3, block)
        return pair(self.refs["minor4"], head - 9, block)


def partner_kernel(group, names, table_ref, query, keys, values, sib_keys, sib_values, *rest):
    frame, sign = frame_ids()
    buffers = Buffers(dict(zip(names, rest)))
    out = rest[-1]
    rows = query.shape[0]
    blocks = rows // BS
    partner = frame + sign
    own_count = entry(table_ref, partner, frame)
    near_count = entry(table_ref, partner, frame + 2 * sign)
    away_valid = entry(table_ref, partner, frame - 2 * sign) > 0
    relay_valid = entry(table_ref, partner, frame + 4 * sign) > 0
    cross_valid = entry(table_ref, partner, frame - sign) > 0

    def problem(head, block):
        mine = slice(block * BS, (block + 1) * BS)
        cols = head_cols(head)
        last = block + 1 == blocks
        if last:
            parts = [(keys[mine, cols], values[mine, cols], None)]
            parts.append((sib_keys[:BS, cols], sib_values[:BS, cols], own_count > 1))
        else:
            both = slice(block * BS, (block + 2) * BS)
            parts = [(keys[both, cols], values[both, cols], (None, own_count > 1))]
        parts.append((*buffers.away(head, block), away_valid))
        if head < CROSS:
            parts.append((*buffers.cross(head, block), cross_valid))
        else:
            if last:
                parts.append((*buffers.near(head, block), near_count > 0))
                parts.append((*buffers.near_first(head), near_count > 1))
            else:
                allowed = (near_count > 0, near_count > 1)
                parts.append((*buffers.near(head, block, 2), allowed))
            parts.append((*buffers.relay(head, block), relay_valid))
        return query[mine, cols], parts

    stats = attend_heads(group, blocks, problem, out)
    write_stats(out, stats, group[1] - group[0])


def own_kernel(group, names, table_ref, query, keys, values, sib_keys, sib_values, *rest):
    frame, sign = frame_ids()
    buffers = Buffers(dict(zip(names, rest)))
    out, out_stats = rest[-2:]
    rows = query.shape[0]
    blocks = rows // BS
    near_valid = entry(table_ref, frame, frame + 2 * sign) > 0
    away_valid = entry(table_ref, frame, frame - 2 * sign) > 0
    cross_count = entry(table_ref, frame, frame - sign)
    far_valid = entry(table_ref, frame, frame - 3 * sign) > 0

    def problem(head, block):
        mine = slice(block * BS, (block + 1) * BS)
        cols = head_cols(head)
        parts = [
            (keys[:, cols], values[:, cols], None),
            (sib_keys[:, cols], sib_values[:, cols], None),
            (*buffers.away(head, block), away_valid),
        ]
        if head < CROSS:
            last = block + 1 == blocks
            if last:
                parts.append((*buffers.cross(head, block), cross_count > 0))
                parts.append((*buffers.cross_first(head), cross_count > 1))
            else:
                allowed = (cross_count > 0, cross_count > 1)
                parts.append((*buffers.cross(head, block, 2), allowed))
            parts.append((*buffers.far(head, block), far_valid))
        else:
            parts.append((*buffers.near(head, block), near_valid))
        return query[mine, cols], parts

    out_stats[...] = attend_heads(group, blocks, problem, out)


def project_kernel(span, own_groups, part_groups, has_base, *refs):
    refs = list(refs)
    weight, sib_weight = refs.pop(0), refs.pop(0)
    owns = [(group, refs.pop(0), refs.pop(0)) for group in own_groups]
    parts = [(group, refs.pop(0)) for group in part_groups]
    base = refs.pop(0) if has_base else None
    if has_base:
        target, attended, out, sems = refs
    else:
        out, attended = refs
    rows = out.shape[0]
    lanes = lax.broadcasted_iota(jnp.int32, (rows, DH), 1)
    own_at, part_at = {}, {}
    own_sum = part_sum = jnp.zeros((rows, DH), jnp.float32)
    for (first, last), own, stats in owns:
        shifted = pltpu.roll(stats[...], first, 1) if first else stats[...]
        own_sum = jnp.where((lanes >= first) & (lanes < last), shifted, own_sum)
        own_at.update({head: (own, head - first) for head in range(first, last)})
    for (first, last), part in parts:
        stats = read_stats(part, last - first)
        shifted = pltpu.roll(stats, first, 1) if first else stats
        part_sum = jnp.where((lanes >= first) & (lanes < last), shifted, part_sum)
        part_at.update({head: (part, head - first) for head in range(first, last)})
    top = jnp.maximum(own_sum, part_sum)
    own_weight = jnp.exp2(own_sum - top)
    part_weight = jnp.exp2(part_sum - top)
    inverse = 1.0 / (own_weight + part_weight)
    own_weight = own_weight * inverse
    part_weight = part_weight * inverse
    for head in range(*span):
        own, own_place = own_at[head]
        part, part_place = part_at[head]
        mixed = own_weight[:, head : head + 1] * own[:, head_cols(own_place)] + part_weight[
            :, head : head + 1
        ] * part[:rows, head_cols(part_place)].astype(jnp.float32)
        attended[:, head_cols(head - span[0])] = mixed.astype(attended.dtype)

    depth = weight.shape[0]
    start, stop = span[0] * DH, span[1] * DH

    def multiply(halves):
        for at in range(0, out.shape[1], TILE):
            product = base[:, at : at + TILE] if has_base else 0.0
            for index, half in enumerate(halves):
                low, high = max(start, index * depth), min(stop, (index + 1) * depth)
                if low < high:
                    product = product + jnp.dot(
                        attended[:, low - start : high - start],
                        half[low - index * depth : high - index * depth, at : at + TILE],
                        preferred_element_type=jnp.float32,
                    )
            out[:, at : at + TILE] = product.astype(out.dtype)
            if has_base:
                copy_out(at).start()

    def copy_out(at):
        cols = slice(at, at + TILE)
        return pltpu.make_async_copy(out.at[:, cols], target.at[:, cols], sems.at[at // TILE])

    core = lax.axis_index("head")

    @pl.when(core == 0)
    def _():
        multiply((weight, sib_weight))

    @pl.when(core != 0)
    def _():
        multiply((sib_weight, weight))

    if has_base:
        for at in range(0, out.shape[1], TILE):
            copy_out(at).wait()


def whole(shape):
    return pl.BlockSpec(shape, lambda i: (0,) * len(shape))


def run(body, name, table, operands, out_shapes, flops, after=()):
    return pl.pallas_call(
        body,
        grid=(1,),
        in_specs=[pl.BlockSpec(memory_space=pltpu.SMEM)]
        + [whole(x.shape) for x in operands]
        + [pl.BlockSpec(memory_space=pl.ANY)] * len(after),
        out_specs=[whole(s.shape) for s in out_shapes],
        out_shape=out_shapes,
        compiler_params=pltpu.CompilerParams(vmem_limit_bytes=8 * MIB),
        cost_estimate=pl.CostEstimate(
            flops=flops, bytes_accessed=MIB, transcendentals=flops // 512
        ),
        name=name,
    )(table, *operands, *after)


def tie_kernel(*refs):
    del refs


def tie(before, *payloads):
    before = tuple(before)
    anywhere = pl.BlockSpec(memory_space=pl.ANY)
    return pl.pallas_call(
        tie_kernel,
        in_specs=[anywhere] * (len(before) + len(payloads)),
        out_specs=[anywhere] * len(payloads),
        out_shape=[jax.ShapeDtypeStruct(p.shape, p.dtype) for p in payloads],
        input_output_aliases={len(before) + i: i for i in range(len(payloads))},
        compiler_params=pltpu.CompilerParams(vmem_limit_bytes=MIB),
        name="tie",
    )(*before, *payloads)


def project(span, owns, parts, weights, base, dtype):
    rows, columns = owns[0][1][0].shape[0], weights[0].shape[1]
    depth = (span[1] - span[0]) * DH
    operands = [*weights]
    for _, own in owns:
        operands += own
    operands += [part for _, part in parts]
    streams = []
    if base is not None:
        operands.append(base)
        streams = [
            pltpu.VMEM((rows, columns), dtype),
            pltpu.SemaphoreType.DMA((columns // TILE,)),
        ]
    return pl.pallas_call(
        functools.partial(
            project_kernel,
            span,
            tuple(group for group, _ in owns),
            tuple(group for group, _ in parts),
            base is not None,
        ),
        grid=(1,),
        in_specs=[whole(x.shape) for x in operands],
        out_specs=whole((rows, columns)) if base is None else pl.BlockSpec(memory_space=pl.ANY),
        out_shape=jax.ShapeDtypeStruct((rows, columns), dtype),
        scratch_shapes=[pltpu.VMEM((rows, depth), jnp.bfloat16), *streams],
        compiler_params=pltpu.CompilerParams(vmem_limit_bytes=8 * MIB),
        cost_estimate=pl.CostEstimate(
            flops=2 * rows * depth * columns, bytes_accessed=4 * MIB, transcendentals=0
        ),
        name="merge_and_project",
    )(*operands)


def per_device(queries, key_tokens, value_tokens, radial_table, out_weight):
    frames = lax.axis_size("frame")
    cores = lax.axis_size("head")
    rows = queries.shape[0]

    def moves(target):
        return [(f, target(f)) for f in range(frames) if 0 <= target(f) < frames]

    partner_moves = moves(lambda f: f ^ 1)
    near_moves = moves(lambda f: f - 2 if f % 2 == 0 else f + 2)
    away_moves = moves(lambda f: f + 2 if f % 2 == 0 else f - 2)
    cross_moves = moves(lambda f: f - 1 if f % 2 == 0 else f + 1)
    core_moves = [(c, cores - 1 - c) for c in range(cores)]

    def pack(first, last):
        cols = slice(first * DH, last * DH)
        return jnp.concatenate([key_tokens[:, cols], value_tokens[:, cols]], axis=0)

    def firsts(*packed):
        return jnp.concatenate(
            [jnp.concatenate([p[at : at + BS] for p in packed], axis=1) for at in (0, rows)],
            axis=0,
        )

    major1 = lax.ppermute(pack(0, 6), "frame", away_moves)
    minor1 = lax.ppermute(pack(3, 9), "frame", near_moves)
    own_weight = [out_weight]
    sib_weight = [lax.ppermute(out_weight, "head", core_moves)]
    cross = lax.ppermute(pack(0, 3), "frame", partner_moves)
    cross, to_minor2 = tie(sib_weight, cross, pack(9, 12))
    minor2 = lax.ppermute(to_minor2, "frame", near_moves)
    partner_query = lax.ppermute(queries, "frame", partner_moves)
    major2 = lax.ppermute(cross, "frame", away_moves)
    minor3 = lax.ppermute(minor1, "frame", near_moves)
    (to_major3,) = tie((major1,), pack(6, 12))
    major3 = lax.ppermute(to_major3, "frame", away_moves)
    major4 = lax.ppermute(major2, "frame", away_moves)
    minor4 = lax.ppermute(minor2, "frame", near_moves)
    to_sib_keys, to_sib_values = tie((major2, partner_query, minor2), key_tokens, value_tokens)
    sib_keys = lax.ppermute(to_sib_keys, "head", core_moves)
    sib_values = lax.ppermute(to_sib_values, "head", core_moves)
    nearest = lax.ppermute(firsts(minor1, minor2, major2), "head", core_moves)
    refs = {
        "major1": major1,
        "major2": major2,
        "major3": major3,
        "major4": major4,
        "minor1": minor1,
        "minor2": minor2,
        "minor3": minor3,
        "minor4": minor4,
        "nearest": nearest,
    }
    local = (key_tokens, value_tokens, sib_keys, sib_values)

    def partner_part(group, names, after=()):
        heads = group[1] - group[0]
        shape = jax.ShapeDtypeStruct((rows + stat_rows(heads)[1], heads * DH), jnp.bfloat16)
        (part,) = run(
            functools.partial(partner_kernel, group, names),
            "partner_part",
            radial_table,
            (partner_query, *local, *(refs[n] for n in names)),
            [shape],
            heads * rows * 6 * BS * DH * 4,
            after,
        )
        return part

    def own_part(group, names, after=()):
        heads = group[1] - group[0]
        return run(
            functools.partial(own_kernel, group, names),
            "own_part",
            radial_table,
            (queries, *local, *(refs[n] for n in names)),
            [
                jax.ShapeDtypeStruct((rows, heads * DH), jnp.float32),
                jax.ShapeDtypeStruct((rows, DH), jnp.float32),
            ],
            heads * rows * 6 * BS * DH * 4,
            after,
        )

    own_early = own_part((3, 6), ("major1", "minor1"))
    part_low = partner_part((0, 3), ("major1", "major2"), (own_early[1],))
    own_middle = own_part((6, 9), ("major3", "minor1"), (part_low,))
    part_middle = partner_part(
        (3, 6), ("major1", "minor1", "minor3", "nearest"), (own_middle[1],)
    )
    part_late = partner_part((6, 9), ("major3", "minor1", "minor3", "nearest"), (part_middle,))
    part_low = lax.ppermute(part_low, "frame", partner_moves)
    part_middle = lax.ppermute(part_middle, "frame", partner_moves)
    own_late = own_part((9, 12), ("major3", "minor2"), (part_late,))
    part_late = lax.ppermute(part_late, "frame", partner_moves)
    part_high = partner_part(
        (9, 12),
        ("major3", "minor2", "minor4", "nearest"),
        (own_late[1], major4, part_low, *sib_weight),
    )
    part_high = lax.ppermute(part_high, "frame", partner_moves)
    own_low = own_part((0, 3), ("major1", "major2", "major4", "nearest"))
    weights = (*own_weight, *sib_weight)
    owns = (((0, 3), own_low), ((3, 6), own_early), ((6, 9), own_middle))
    base = project(
        (0, 9),
        owns,
        (((0, 3), part_low), ((3, 6), part_middle), ((6, 9), part_late)),
        weights,
        None,
        jnp.float32,
    )
    return project(
        (9, 12), (((9, 12), own_late),), (((9, 12), part_high),), weights, base, jnp.bfloat16
    )


def solution(mesh):
    in_specs = (
        P(("clip", "frame", "head"), None),
        P(("clip", "frame", "head"), None),
        P(("clip", "frame", "head"), None),
        P(),
        P("head", None),
    )
    out_specs = P(("clip", "frame", "head"), None)
    return jax.shard_map(
        per_device, mesh=mesh, in_specs=in_specs, out_specs=out_specs, check_vma=False
    )
```
